32 devices in a mesh: expert: 4 (over y, core), shard: 8 (over z, x).
Axes of the slice: x: 2, y: 2, z: 4, core: 2. Of those that a mesh axis runs over, the one named last changes fastest.
Arguments:
- inputs: bfloat16 [2, 2048, 2048], P(None, ('expert', 'shard')), may hold values from -6 to 6
- segment_ids: int32 [2, 2048], P(None, 'expert'), may hold values from 0 to 3, as said below
- routes: int32 [2, 2048, 8], P(None, ('expert', 'shard')), may hold values from 0 to 15, all different within a row; in each aligned block of 64 rows (0 to 63, 64 to 127, ..., all dimensions but the last counted through in order) at most 64 rows name the same one
- cotangent: bfloat16 [2, 2048, 2048], P(None, ('expert', 'shard')), may hold values from -6 to 6
- query_weight: bfloat16 [2048, 2048], P('shard'), may hold values from -0.125 to 0.125
- key_weight: bfloat16 [2048, 2048], P('shard'), may hold values from -0.125 to 0.125
- value_weight: bfloat16 [2048, 2048], P('shard'), may hold values from -0.125 to 0.125
- output_weight: bfloat16 [2048, 2048], P('shard'), may hold values from -1.5 to 1.5
- router_weight: bfloat16 [2048, 16], P('shard'), may hold values from -0.0625 to 0.0625
- attention_gain: bfloat16 [2048], P('shard'), may hold values from 0.5 to 1.5
- expert_gain: bfloat16 [2048], P('shard'), may hold values from 0.5 to 1.5
- query_gain: bfloat16 [128], P('shard'), may hold values from 0.099609375 to 1.8984375
- key_gain: bfloat16 [128], P('shard'), may hold values from 0.099609375 to 1.8984375
- gate_weight: bfloat16 [32, 2048, 512], P(('expert', 'shard')), may hold values from -0.125 to 0.125
- up_weight: bfloat16 [32, 2048, 512], P(('expert', 'shard')), may hold values from -0.125 to 0.125
- down_weight: bfloat16 [32, 512, 2048], P(('expert', 'shard')), may hold values from -1 to 1
Outputs:
- layer_out: bfloat16 [2, 2048, 2048], P(None, ('expert', 'shard'))
- input_grad: bfloat16 [2, 2048, 2048], P(None, ('expert', 'shard'))
- query_grad: float32 [2048, 2048], P('shard')
- key_grad: float32 [2048, 2048], P('shard')
- value_grad: float32 [2048, 2048], P('shard')
- output_grad: float32 [2048, 2048], P('shard')
- router_grad: float32 [2048, 16], P('shard')
- gain_attention: float32 [2048], P('shard')
- gain_expert: float32 [2048], P('shard')
- gain_query: float32 [128], P('shard')
- gain_key: float32 [128], P('shard')
- gate_grad: float32 [32, 2048, 512], P(('expert', 'shard'))
- up_grad: float32 [32, 2048, 512], P(('expert', 'shard'))
- down_grad: float32 [32, 512, 2048], P(('expert', 'shard'))
The draws below stay inside these ranges and needn't reach their ends.
Inputs may be any that keep to these rules, and one draw needn't show every extreme that they name: `segment_ids`: within each sequence of 512 tokens (tokens s * 512 to (s + 1) * 512 - 1 of a micro-batch) the ids start at 0 and rise by 0 or 1 from one token to the next; in every micro-batch one sequence is a single document and every other sequence holds exactly four documents. `routes`: A token names 8 different experts; in each micro-batch at most 64 of the 64 tokens of one device name the same expert.
All inputs are finite; a program needn't handle non-finite values.
Results may differ from the reference program's by a relative error of at most 0.025.
Values may be sent and summed in bfloat16 or wider, within the bound.
A program may use at most 208 MiB of HBM per device.

```python
import math
import jax
import jax.numpy as jnp
import numpy as np
from jax import lax

D = 2048
HEADS = 16
HDIM = 128
FF = 1024
TOPK = 8
MICRO = 2
MB_TOK = 64
EXPERTS = 16
HALF = 512
LEN = 512
TOKENS_MB = 2048
CAP = 64
N_EXPERT = 4
N_SHARD = 8


def draw_segment_ids(key, part):
    key = jax.random.fold_in(key, 7)
    key_marks, key_chosen = jax.random.split(key)
    seq_count = TOKENS_MB // LEN
    position = jnp.arange(LEN, dtype=jnp.int32)[None, None, :]
    scores = jax.random.randint(key_marks, (MICRO, seq_count, LEN), 0, LEN) * LEN + position
    scores = jnp.where(position == 0, LEN * LEN, scores)
    order = jnp.argsort(scores, axis=-1)
    rank = jnp.argsort(order, axis=-1)
    chosen = jax.random.randint(key_chosen, (MICRO, 1, 1), 0, seq_count)
    sequence = jnp.arange(seq_count, dtype=jnp.int32)[None, :, None]
    boundary = (rank < 3) & (sequence != chosen)
    return jnp.cumsum(boundary.astype(jnp.int32), axis=-1).reshape(MICRO, TOKENS_MB)


def levels(key, shape, shards, smallest, top_value):
    gain = 1.0
    for axis_at, blocks in shards:
        steps = jax.random.uniform(jax.random.fold_in(jax.random.fold_in(key, 6), axis_at), (blocks,), jnp.float32, smallest / len(shards), top_value / len(shards))
        gain = gain * jnp.repeat(jnp.exp(steps), shape[axis_at] // blocks).reshape((-1,) + (1,) * (len(shape) - 1 - axis_at))
    return gain


def shared_out(rng, own, number, rows, number_of, top, most, slope):
    ranking = jax.random.permutation(rng, number_of)
    heavy_load, ordinary = portions_of(number_of, rows * top, most, slope, True), portions_of(number_of, rows * top, most, slope, False)
    places = jnp.arange(number_of)

    def named(lengths, turn):
        used = int((lengths > 0).sum())
        fixed = max(1, used // 4)
        passed = fixed + (places - fixed + turn * (used - fixed)) % max(1, number_of - fixed)
        return jnp.zeros((number_of,), jnp.int32).at[ranking[jnp.where(places < fixed, places, passed)]].set(jnp.asarray(lengths, jnp.int32))

    lengths = jnp.where(number % 4 == 0, named(heavy_load, number // 4), named(ordinary, number - number // 4 - 1))
    mixed = jax.random.permutation(jax.random.fold_in(own, 3), number_of)
    donor, receiver = mixed[0:number_of // 2 * 2:2], mixed[1:number_of // 2 * 2:2]
    margin = jnp.minimum(lengths[donor] - 1, most - lengths[receiver]) // 2
    margin = jnp.where((donor == ranking[0]) | (receiver == ranking[0]) | (lengths[receiver] == 0), 0, jnp.maximum(margin, 0))
    passed = jax.random.randint(jax.random.fold_in(own, 4), (number_of // 2,), 0, 1 << 20) % (margin + 1)
    lengths = lengths.at[donor].add(-passed).at[receiver].add(passed)
    members = jnp.searchsorted(jnp.cumsum(lengths), jnp.arange(rows * top), side="right").astype(jnp.int32)
    grid = members.reshape(top, rows).T
    grid = grid[jax.random.permutation(jax.random.fold_in(own, 1), rows)]
    turn = jax.random.randint(jax.random.fold_in(own, 2), (rows, 1), 0, top)
    return jnp.take_along_axis(grid, (jnp.arange(top)[None, :] + turn) % top, axis=1)


def portions_of(amount, total, most, lean, full):
    loads = [(1 << 20) // math.isqrt(standing ** lean) + 1 for standing in range(1, amount + 1)]
    largest = most if full else min(most, max(-(-total // amount), total * loads[0] // sum(loads)))
    least = 1 if total - largest >= amount - 1 else 0
    given, surplus = [largest] + [least] * (amount - 1), total - largest - least * (amount - 1)
    while surplus > 0:
        movable = [i for i in range(1, amount) if given[i] < largest] or [i for i in range(1, amount) if given[i] < most]
        pool, budget = sum([loads[i] for i in movable]), surplus
        for i in movable:
            extra = min(most - given[i], max(1, budget * loads[i] // pool), surplus)
            given[i] = given[i] + extra
            surplus = surplus - extra
    return np.array(given)


def centred(rng, shape, width, most, pieces=(), held_as=jnp.bfloat16):
    level = levels(rng, shape, pieces, -0.22, 0.18) if pieces else 1.0
    array = jax.random.normal(rng, shape, jnp.float32) * width * level
    return jnp.minimum(jnp.maximum(array, -most), most).astype(held_as)


def setup_inputs(seed: int = 0) -> dict:
    streams_of = jax.random.split(jax.random.key(seed), 17)
    inputs = centred(streams_of[0], (MICRO, TOKENS_MB, D), 1.0, 6.0, ((1, 32),))
    segment_ids = draw_segment_ids(jax.random.fold_in(streams_of[16], 71), 0)
    routes_keys = jax.random.split(jax.random.fold_in(streams_of[2], 1), MICRO * TOKENS_MB // MB_TOK)
    routes_turns = jax.random.permutation(jax.random.fold_in(streams_of[2], 3), MICRO * TOKENS_MB // MB_TOK)
    routes = jax.vmap(lambda own, number: shared_out(jax.random.fold_in(streams_of[2], 2), own, number, MB_TOK, EXPERTS, TOPK, CAP, 1))(routes_keys, routes_turns).reshape((MICRO, TOKENS_MB, TOPK))
    cotangent = centred(streams_of[3], (MICRO, TOKENS_MB, D), 1.0, 6.0, ((1, 32),))
    query_weight = centred(streams_of[4], (D, D), D ** -0.5, 0.125, ((0, 8),))
    key_weight = centred(streams_of[5], (D, D), D ** -0.5, 0.125, ((0, 8),))
    value_weight = centred(streams_of[6], (D, D), D ** -0.5, 0.125, ((0, 8),))
    output_weight = centred(streams_of[7], (D, D), (max(1, 4 * D // LEN)) ** -0.5, 1.5, ((0, 8),))
    router_weight = centred(streams_of[8], (D, EXPERTS), (4 * D) ** -0.5, 0.0625, ((0, 8),))
    attention_gain = jnp.clip(1.0 + 0.1 * jax.random.normal(streams_of[9], (D,), jnp.float32), 0.5, 1.5).astype(jnp.bfloat16)
    expert_gain = jnp.clip(1.0 + 0.1 * jax.random.normal(streams_of[10], (D,), jnp.float32), 0.5, 1.5).astype(jnp.bfloat16)
    query_gain = jnp.clip(1.0 + 0.18 * jax.random.normal(streams_of[11], (HDIM,), jnp.float32), 0.099609375, 1.8984375).astype(jnp.bfloat16)
    key_gain = jnp.clip(1.0 + 0.18 * jax.random.normal(streams_of[12], (HDIM,), jnp.float32), 0.099609375, 1.8984375).astype(jnp.bfloat16)
    gate_weight = centred(streams_of[13], (2 * EXPERTS, D, HALF), D ** -0.5, 0.125, ((0, 32),))
    up_weight = centred(streams_of[14], (2 * EXPERTS, D, HALF), D ** -0.5, 0.125, ((0, 32),))
    down_weight = centred(streams_of[15], (2 * EXPERTS, HALF, D), (max(1, FF // 32)) ** -0.5, 1.0, ((0, 32),))
    return {"inputs": inputs, "segment_ids": segment_ids, "routes": routes, "cotangent": cotangent, "query_weight": query_weight, "key_weight": key_weight, "value_weight": value_weight, "output_weight": output_weight, "router_weight": router_weight, "attention_gain": attention_gain, "expert_gain": expert_gain, "query_gain": query_gain, "key_gain": key_gain, "gate_weight": gate_weight, "up_weight": up_weight, "down_weight": down_weight}


EPSILON = 1e-05
ROPE_BASE = 10000.0
MASK_FILL = -1e+30

@jax.custom_vjp
def low(v):
    return lax.optimization_barrier(v.astype(jnp.bfloat16)).astype(jnp.float32)

@jax.custom_vjp
def low_back(v):
    return v

def low_keep(v):
    return (low(v), None)

def low_pass(kept, grad):
    return (grad,)

def back_keep(v):
    return (v, None)

def back_low(kept, grad):
    return (low(grad),)
low.defvjp(low_keep, low_pass)
low_back.defvjp(back_keep, back_low)

def product(left, right):
    return jnp.dot(left, right, precision=lax.Precision.HIGHEST, preferred_element_type=jnp.float32)

def rms_scale(values):
    return lax.rsqrt(lax.optimization_barrier(jnp.mean(values * values, axis=-1, keepdims=True)) + EPSILON)

def rotary(places, head_width):
    half_width = head_width // 2
    steps_float = jnp.arange(half_width, dtype=jnp.int32).astype(jnp.float32)
    freqs = jnp.power(ROPE_BASE, -2.0 * steps_float / head_width)
    theta = places[:, None] * freqs[None, :]
    return (jnp.cos(theta)[:, None, :], jnp.sin(theta)[:, None, :])

def rotate(values, cosine_table, sine_table):
    half_width = values.shape[-1] // 2
    front = values[..., :half_width]
    behind = values[..., half_width:]
    return jnp.concatenate([front * cosine_table - behind * sine_table, behind * cosine_table + front * sine_table], axis=-1)

def softmax_rows(scores):
    row_peak = lax.optimization_barrier(jnp.max(scores, axis=-1, keepdims=True))
    exponent = jnp.exp(scores - row_peak)
    return exponent / lax.optimization_barrier(jnp.sum(exponent, axis=-1, keepdims=True))

def slot_tables(expert_ids, experts, capacity):
    onehot = (expert_ids[:, None] == jnp.arange(experts, dtype=jnp.int32)[None, :]).astype(jnp.int32)
    rank_in = jnp.cumsum(onehot, axis=0) - 1
    place_in = lax.optimization_barrier(jnp.sum(rank_in * onehot, axis=1))
    target = expert_ids * capacity + place_in
    pairs = expert_ids.shape[0]
    source = jnp.full((experts * capacity,), pairs, jnp.int32).at[target].set(jnp.arange(pairs, dtype=jnp.int32))
    return (onehot, target, source)

def forward(hidden, query_weight, key_weight, value_weight, output_weight, router_weight, attention_gain, expert_gain, query_gain, key_gain, gate_weight, up_weight, down_weight, seg_row, route_rows):
    tokens = hidden.shape[0]
    mixer_input = low(hidden * rms_scale(hidden) * attention_gain)
    query_proj = low_back(product(mixer_input, query_weight)).reshape(tokens, HEADS, HDIM)
    key_proj = low_back(product(mixer_input, key_weight)).reshape(tokens, HEADS, HDIM)
    value_proj = low(low_back(product(mixer_input, value_weight))).reshape(tokens, HEADS, HDIM)
    places = (jnp.arange(tokens, dtype=jnp.int32) % LEN).astype(jnp.float32)
    cosine_table, sine_table = rotary(places, HDIM)
    query_rot = low(rotate(query_proj * rms_scale(query_proj) * query_gain, cosine_table, sine_table))
    key_rot = low(rotate(key_proj * rms_scale(key_proj) * key_gain, cosine_table, sine_table))
    sequences = tokens // LEN
    score_scale = 1.0 / math.sqrt(HDIM)

    def by_head(values):
        return values.reshape(sequences, LEN, HEADS, HDIM).transpose(0, 2, 1, 3).reshape(sequences * HEADS, LEN, HDIM)
    seg_heads = jnp.repeat(seg_row.reshape(sequences, LEN), HEADS, axis=0)

    def attend(block_item):
        query_block, key_block, value_block, seg_block = block_item
        scores = low_back(product(query_block, key_block.T) * score_scale)
        scores = jnp.where(seg_block[:, None] == seg_block[None, :], scores, MASK_FILL)
        return product(low(softmax_rows(scores)), value_block)
    attended = lax.map(jax.checkpoint(attend), (by_head(query_rot), by_head(key_rot), by_head(value_proj), seg_heads))
    attended = attended.reshape(sequences, HEADS, LEN, HDIM).transpose(0, 2, 1, 3).reshape(tokens, D)
    attended = low(low_back(attended))
    middle = hidden + low_back(product(attended, output_weight))
    expert_input = low(middle * rms_scale(middle) * expert_gain)
    logits = product(expert_input, router_weight)
    gate_share = softmax_rows(jnp.take_along_axis(logits, route_rows, axis=1))
    devices = N_EXPERT * N_SHARD
    per_device = route_rows.reshape(devices, MB_TOK * TOPK)
    tables = jax.vmap(lambda expert_ids: slot_tables(expert_ids, EXPERTS, CAP))(per_device)
    target = tables[1]
    source = tables[2]
    device_base = jnp.arange(devices, dtype=jnp.int32)[:, None]
    token_index = jnp.where(source < MB_TOK * TOPK, device_base * MB_TOK + source // TOPK, tokens)
    token_index = token_index.reshape(devices, EXPERTS, CAP).transpose(1, 0, 2).reshape(EXPERTS, devices * CAP)
    padded = jnp.concatenate([expert_input, jnp.zeros((1, D), jnp.float32)], axis=0)

    def expert_rows(block_item):
        indices, gate_pair, up_pair, down_pair = block_item
        base_rows = padded[indices]
        combined = jnp.zeros((indices.shape[0], D), jnp.float32)
        for half_index in range(2):
            rows_half = low_back(base_rows)
            gate_pre = low_back(product(rows_half, gate_pair[half_index]))
            up_pre = low_back(product(rows_half, up_pair[half_index]))
            activated = low(gate_pre * jax.nn.sigmoid(gate_pre) * up_pre)
            combined = combined + low(low_back(product(activated, down_pair[half_index])))
        return combined
    stacked = lax.map(jax.checkpoint(expert_rows), (token_index, gate_weight.reshape(EXPERTS, 2, D, HALF), up_weight.reshape(EXPERTS, 2, D, HALF), down_weight.reshape(EXPERTS, 2, HALF, D)))
    flat_index = (target // CAP * devices + device_base) * CAP + target % CAP
    picked = stacked.reshape(EXPERTS * devices * CAP, D)[flat_index.reshape(-1)].reshape(tokens, TOPK, D)
    return middle + lax.optimization_barrier(jnp.sum(gate_share[:, :, None] * picked, axis=1))

def reference(inputs, segment_ids, routes, cotangent, query_weight, key_weight, value_weight, output_weight, router_weight, attention_gain, expert_gain, query_gain, key_gain, gate_weight, up_weight, down_weight):
    weights = [matrix.astype(jnp.float32) for matrix in (query_weight, key_weight, value_weight, output_weight, router_weight, attention_gain, expert_gain, query_gain, key_gain, gate_weight, up_weight, down_weight)]
    layer_rows = []
    input_rows = []
    totals = None
    for micro_step in range(MICRO):
        hidden = inputs[micro_step].astype(jnp.float32)
        seg_row = segment_ids[micro_step]
        route_rows = routes[micro_step]

        def layer(hidden_in, *params):
            return forward(hidden_in, *params, seg_row, route_rows)
        result, pullback = jax.vjp(layer, hidden, *weights)
        grads = pullback(cotangent[micro_step].astype(jnp.float32))
        layer_rows.append(result.astype(jnp.bfloat16))
        input_rows.append(grads[0].astype(jnp.bfloat16))
        totals = list(grads[1:]) if totals is None else [left + right for left, right in zip(totals, grads[1:])]
    return (jnp.stack(layer_rows), jnp.stack(input_rows), totals[0], totals[1], totals[2], totals[3], totals[4], totals[5], totals[6], totals[7], totals[8], totals[9], totals[10], totals[11])
```

```python
import functools
import math

import jax
import jax.numpy as jnp
from jax import lax
from jax.experimental import pallas as pl
from jax.experimental.pallas import tpu as pltpu
from jax.sharding import PartitionSpec as P

HDIM = 128
EPSILON = 1e-05
ROPE_BASE = 10000.0
MASK_FILL = -1e30
PRECISE = lax.Precision.HIGHEST
MESH = pl.DeviceIdType.MESH
F32 = jnp.float32
BF16 = jnp.bfloat16
NN = (((1,), (0,)), ((), ()))
NT = (((1,), (1,)), ((), ()))
TN = (((0,), (0,)), ((), ()))
VMEM_LIMIT = 60 << 20


def dot(left, right, dims):
    return lax.dot_general(left, right, dims, preferred_element_type=F32)


def rms_scale(values):
    return lax.rsqrt(jnp.mean(values * values, axis=-1, keepdims=True) + EPSILON)


def norm_back(normed_grad, normed, inv_scale):
    return inv_scale * (
        normed_grad - normed * jnp.mean(normed_grad * normed, axis=-1, keepdims=True)
    )


def rotary(places, head_width):
    half_width = head_width // 2
    steps_float = jnp.arange(half_width, dtype=jnp.int32).astype(F32)
    freqs = jnp.power(ROPE_BASE, -2.0 * steps_float / head_width)
    theta = places[:, None] * freqs[None, :]
    return (jnp.cos(theta)[:, None, :], jnp.sin(theta)[:, None, :])


def rotate(values, cosine_table, sine_table):
    half_width = values.shape[-1] // 2
    front = values[..., :half_width]
    behind = values[..., half_width:]
    return jnp.concatenate(
        [front * cosine_table - behind * sine_table, behind * cosine_table + front * sine_table],
        axis=-1,
    )


def softmax_rows(scores):
    row_peak = jnp.max(scores, axis=-1, keepdims=True)
    exponent = jnp.exp(scores - row_peak)
    return exponent / jnp.sum(exponent, axis=-1, keepdims=True)


def group_place(wide):
    shard_place = lax.axis_index("shard")
    return lax.axis_index("expert"), shard_place // wide, lax.rem(shard_place, wide)


def greet(group, row, column, deep, wide):
    barrier = pltpu.get_barrier_semaphore()
    for step in range(1, deep):
        pl.semaphore_signal(
            barrier,
            inc=1,
            device_id=(group, lax.rem(row + step, deep) * wide + column),
            device_id_type=MESH,
        )
    for step in range(1, wide):
        pl.semaphore_signal(
            barrier,
            inc=1,
            device_id=(group, row * wide + lax.rem(column + step, wide)),
            device_id_type=MESH,
        )
    pl.semaphore_wait(barrier, deep + wide - 2)


def gather_kernel(deep, wide, own, whole, row_send, row_recv, col_send, col_recv, local):
    group, row, column = group_place(wide)
    me = row * wide + column
    greet(group, row, column, deep, wide)
    pieces = own.shape[0]
    here = pltpu.make_async_copy(own, whole.at[:, me], local)
    here.start()
    sends = []

    def along_row(piece, turn, block, place):
        for step in range(1, wide):
            copy = pltpu.make_async_remote_copy(
                src_ref=block,
                dst_ref=whole.at[piece, place],
                send_sem=col_send.at[piece, turn, step - 1],
                recv_sem=col_recv.at[piece, turn, step - 1],
                device_id=(group, row * wide + lax.rem(column + step, wide)),
                device_id_type=MESH,
            )
            copy.start()
            sends.append(copy)

    def along_column(piece, step, place):
        return pltpu.make_async_remote_copy(
            src_ref=own.at[piece],
            dst_ref=whole.at[piece, place],
            send_sem=row_send.at[piece, step - 1],
            recv_sem=row_recv.at[piece, step - 1],
            device_id=(group, lax.rem(row + step, deep) * wide + column),
            device_id_type=MESH,
        )

    for piece in range(pieces):
        for step in range(1, deep):
            copy = along_column(piece, step, me)
            copy.start()
            sends.append(copy)
        along_row(piece, 0, own.at[piece], me)
    for piece in range(pieces):
        for step in range(1, deep):
            place = lax.rem(row - step + deep, deep) * wide + column
            along_column(piece, step, place).wait_recv()
            along_row(piece, step, whole.at[piece, place], place)
    for piece in range(pieces):
        for turn in range(deep):
            for step in range(1, wide):
                place = (
                    lax.rem(row - turn + deep, deep) * wide
                    + lax.rem(column - step + wide, wide)
                )
                pltpu.make_async_remote_copy(
                    src_ref=own.at[piece],
                    dst_ref=whole.at[piece, place],
                    send_sem=col_send.at[piece, turn, step - 1],
                    recv_sem=col_recv.at[piece, turn, step - 1],
                    device_id=(group, row * wide + lax.rem(column + step, wide)),
                    device_id_type=MESH,
                ).wait_recv()
    for copy in sends:
        copy.wait_send()
    here.wait()


def group_gather(own, deep, wide, collective_id):
    pieces, rows, width = own.shape
    return pl.pallas_call(
        functools.partial(gather_kernel, deep, wide),
        out_shape=jax.ShapeDtypeStruct((pieces, deep * wide, rows, width), own.dtype),
        in_specs=[pl.BlockSpec(memory_space=pl.ANY)],
        out_specs=pl.BlockSpec(memory_space=pl.ANY),
        scratch_shapes=[
            pltpu.SemaphoreType.DMA((pieces, deep - 1)),
            pltpu.SemaphoreType.DMA((pieces, deep - 1)),
            pltpu.SemaphoreType.DMA((pieces, deep, max(1, wide - 1))),
            pltpu.SemaphoreType.DMA((pieces, deep, max(1, wide - 1))),
            pltpu.SemaphoreType.DMA,
        ],
        compiler_params=pltpu.CompilerParams(
            collective_id=collective_id, has_side_effects=True, vmem_limit_bytes=VMEM_LIMIT
        ),
    )(own)


def scatter_kernel(
    deep, wide, parts, total, landed, merged, summed, col_send, col_recv, row_send, row_recv
):
    group, row, column = group_place(wide)
    greet(group, row, column, deep, wide)
    pieces = parts.shape[0]
    sends = []

    def target_row(turn):
        return lax.rem(row + turn + 1, deep)

    def along_row(piece, turn, step):
        return pltpu.make_async_remote_copy(
            src_ref=parts.at[piece, target_row(turn) * wide + lax.rem(column + step, wide)],
            dst_ref=landed.at[piece, turn, step - 1],
            send_sem=col_send.at[piece, turn, step - 1],
            recv_sem=col_recv.at[piece, turn, step - 1],
            device_id=(group, row * wide + lax.rem(column + step, wide)),
            device_id_type=MESH,
        )

    def along_column(piece, turn):
        return pltpu.make_async_remote_copy(
            src_ref=merged.at[piece, turn],
            dst_ref=summed.at[piece, turn],
            send_sem=row_send.at[piece, turn],
            recv_sem=row_recv.at[piece, turn],
            device_id=(group, target_row(turn) * wide + column),
            device_id_type=MESH,
        )

    for piece in range(pieces):
        for turn in range(deep):
            for step in range(1, wide):
                copy = along_row(piece, turn, step)
                copy.start()
                sends.append(copy)
    for piece in range(pieces):
        for turn in range(deep):
            value = parts[piece, target_row(turn) * wide + column].astype(F32)
            for step in range(1, wide):
                along_row(piece, turn, step).wait_recv()
                value = value + landed[piece, turn, step - 1].astype(F32)
            if turn < deep - 1:
                merged[piece, turn] = value.astype(BF16)
                copy = along_column(piece, turn)
                copy.start()
                sends.append(copy)
            else:
                total[piece] = value
    for piece in range(pieces):
        value = total[piece]
        for turn in range(deep - 1):
            along_column(piece, turn).wait_recv()
            value = value + summed[piece, turn].astype(F32)
        total[piece] = value
    for copy in sends:
        copy.wait_send()


def group_scatter(parts, deep, wide, collective_id):
    pieces, _, rows, width = parts.shape
    return pl.pallas_call(
        functools.partial(scatter_kernel, deep, wide),
        out_shape=jax.ShapeDtypeStruct((pieces, rows, width), F32),
        in_specs=[pl.BlockSpec(memory_space=pltpu.VMEM)],
        out_specs=pl.BlockSpec(memory_space=pltpu.VMEM),
        scratch_shapes=[
            pltpu.VMEM((pieces, deep, max(1, wide - 1), rows, width), BF16),
            pltpu.VMEM((pieces, deep - 1, rows, width), BF16),
            pltpu.VMEM((pieces, deep - 1, rows, width), BF16),
            pltpu.SemaphoreType.DMA((pieces, deep, max(1, wide - 1))),
            pltpu.SemaphoreType.DMA((pieces, deep, max(1, wide - 1))),
            pltpu.SemaphoreType.DMA((pieces, deep - 1)),
            pltpu.SemaphoreType.DMA((pieces, deep - 1)),
        ],
        compiler_params=pltpu.CompilerParams(
            collective_id=collective_id, has_side_effects=True, vmem_limit_bytes=VMEM_LIMIT
        ),
    )(parts)


def units_kernel(
    span,
    rows_ref,
    upstream_ref,
    share_ref,
    gate_ref,
    up_ref,
    down_ref,
    hidden_ref,
    gate_pre_ref,
    up_pre_ref,
    dot_ref,
):
    half = pl.program_id(0)
    half_width = gate_ref.shape[2]
    lanes = lax.broadcasted_iota(jnp.int32, share_ref.shape, 1)
    share = jnp.sum(jnp.where(lanes == half, share_ref[...], 0.0), axis=1, keepdims=True)

    def body(step, carry):
        units = pl.ds(pl.multiple_of(step * span, span), span)
        gate_pre = dot(rows_ref[...], gate_ref[0, :, units], NN)
        up_pre = dot(rows_ref[...], up_ref[0, :, units], NN)
        units_grad = dot(upstream_ref[...], down_ref[0, units, :], NT)
        sigmoid_gate = 1.0 / (1.0 + jnp.exp(-gate_pre))
        swish_gate = gate_pre * sigmoid_gate
        activated = swish_gate * up_pre
        dots = jnp.sum(activated * units_grad, axis=1, keepdims=True)
        dot_ref[...] += jnp.where(lanes == half, dots, 0.0)
        hidden_ref[0, :, units] = (activated * share).astype(BF16)
        weighted = units_grad * share
        gate_pre_ref[0, :, units] = (
            weighted * up_pre * (sigmoid_gate * (1.0 + gate_pre * (1.0 - sigmoid_gate)))
        ).astype(BF16)
        up_pre_ref[0, :, units] = (weighted * swish_gate).astype(BF16)
        return carry

    @pl.when(half == 0)
    def _():
        dot_ref[...] = jnp.zeros_like(dot_ref)

    lax.fori_loop(0, half_width // span, body, 0)


def expert_units(rows, upstream, share, gate_all, up_all, down_all):
    tokens, width = rows.shape
    halves, _, units = gate_all.shape

    def each(*shape):
        return pl.BlockSpec((1,) + shape, lambda half: (half,) + (0,) * len(shape))

    whole = pl.BlockSpec(memory_space=pltpu.VMEM)
    return pl.pallas_call(
        functools.partial(units_kernel, 256 if tokens <= 1024 else 128),
        grid=(halves,),
        in_specs=[whole, whole, whole, each(width, units), each(width, units), each(units, width)],
        out_specs=[each(tokens, units), each(tokens, units), each(tokens, units), whole],
        out_shape=[
            jax.ShapeDtypeStruct((halves, tokens, units), BF16),
            jax.ShapeDtypeStruct((halves, tokens, units), BF16),
            jax.ShapeDtypeStruct((halves, tokens, units), BF16),
            jax.ShapeDtypeStruct(share.shape, F32),
        ],
        compiler_params=pltpu.CompilerParams(vmem_limit_bytes=VMEM_LIMIT),
        cost_estimate=pl.CostEstimate(
            flops=6 * tokens * width * units * halves,
            bytes_accessed=6 * width * units * halves,
            transcendentals=0,
        ),
    )(rows, upstream, share, gate_all, up_all, down_all)


def merge_kernel(gate_pre_ref, up_pre_ref, gate_ref, up_ref, grad_ref):
    halves = gate_pre_ref.shape[0]
    grad = dot(gate_pre_ref[0], gate_ref[0], NT) + dot(up_pre_ref[0], up_ref[0], NT)
    for half in range(1, halves):
        grad = grad + dot(gate_pre_ref[half], gate_ref[half], NT)
        grad = grad + dot(up_pre_ref[half], up_ref[half], NT)
    grad_ref[...] = grad.astype(BF16)


def expert_merge(gate_pre, up_pre, gate_all, up_all):
    halves, tokens, units = gate_pre.shape
    width = gate_all.shape[1]
    span = 256
    batch = min(tokens, 1024)
    slab = pl.BlockSpec(
        (halves, batch, units), lambda turn, step: (0, turn, 0), pipeline_mode=pl.Buffered(1)
    )
    tile = pl.BlockSpec((halves, span, units), lambda turn, step: (0, step, 0))
    return pl.pallas_call(
        merge_kernel,
        grid=(tokens // batch, width // span),
        in_specs=[slab, slab, tile, tile],
        out_specs=pl.BlockSpec((batch, span), lambda turn, step: (turn, step)),
        out_shape=jax.ShapeDtypeStruct((tokens, width), BF16),
        compiler_params=pltpu.CompilerParams(vmem_limit_bytes=VMEM_LIMIT),
        cost_estimate=pl.CostEstimate(
            flops=4 * tokens * width * units * halves,
            bytes_accessed=4 * width * units * halves,
            transcendentals=0,
        ),
    )(gate_pre, up_pre, gate_all, up_all)


def output_kernel(hidden_ref, down_ref, out_ref):
    halves = hidden_ref.shape[0]
    out = dot(hidden_ref[0], down_ref[0], NN)
    for half in range(1, halves):
        out = out + dot(hidden_ref[half], down_ref[half], NN)
    out_ref[...] = out.astype(BF16)


def expert_output(hidden, down_all):
    halves, tokens, units = hidden.shape
    width = down_all.shape[2]
    span = 256
    batch = min(tokens, 1024)
    slab = pl.BlockSpec(
        (halves, batch, units), lambda turn, step: (0, turn, 0), pipeline_mode=pl.Buffered(1)
    )
    return pl.pallas_call(
        output_kernel,
        grid=(tokens // batch, width // span),
        in_specs=[slab, pl.BlockSpec((halves, units, span), lambda turn, step: (0, 0, step))],
        out_specs=pl.BlockSpec((batch, span), lambda turn, step: (turn, step)),
        out_shape=jax.ShapeDtypeStruct((tokens, width), BF16),
        compiler_params=pltpu.CompilerParams(vmem_limit_bytes=VMEM_LIMIT),
        cost_estimate=pl.CostEstimate(
            flops=2 * tokens * width * units * halves,
            bytes_accessed=2 * width * units * halves,
            transcendentals=0,
        ),
    )(hidden, down_all)


def weights_kernel(
    span,
    rows_ref,
    upstream_ref,
    hidden_ref,
    gate_pre_ref,
    up_pre_ref,
    gate_grad_ref,
    up_grad_ref,
    down_grad_ref,
):
    def body(step, carry):
        units = pl.ds(pl.multiple_of(step * span, span), span)
        gate_grad_ref[0, :, units] = dot(rows_ref[...], gate_pre_ref[0, :, units], TN).astype(BF16)
        up_grad_ref[0, :, units] = dot(rows_ref[...], up_pre_ref[0, :, units], TN).astype(BF16)
        down_grad_ref[0, units, :] = dot(
            hidden_ref[0, :, units], upstream_ref[...], TN
        ).astype(BF16)
        return carry

    lax.fori_loop(0, gate_grad_ref.shape[2] // span, body, 0)


def expert_weights(rows, upstream, hidden, gate_pre, up_pre):
    tokens, width = rows.shape
    halves, _, units = hidden.shape

    def each(*shape):
        return pl.BlockSpec((1,) + shape, lambda half: (half,) + (0,) * len(shape))

    whole = pl.BlockSpec(memory_space=pltpu.VMEM)
    slab = each(tokens, units)
    return pl.pallas_call(
        functools.partial(weights_kernel, 256),
        grid=(halves,),
        in_specs=[whole, whole, slab, slab, slab],
        out_specs=[each(width, units), each(width, units), each(units, width)],
        out_shape=[
            jax.ShapeDtypeStruct((halves, width, units), BF16),
            jax.ShapeDtypeStruct((halves, width, units), BF16),
            jax.ShapeDtypeStruct((halves, units, width), BF16),
        ],
        compiler_params=pltpu.CompilerParams(vmem_limit_bytes=VMEM_LIMIT),
        cost_estimate=pl.CostEstimate(
            flops=6 * tokens * width * units * halves,
            bytes_accessed=6 * width * units * halves,
            transcendentals=0,
        ),
    )(rows, upstream, hidden, gate_pre, up_pre)


def per_device(
    groups,
    shards,
    wide,
    inputs,
    segment_ids,
    routes,
    cotangent,
    query_weight,
    key_weight,
    value_weight,
    output_weight,
    router_weight,
    attention_gain,
    expert_gain,
    query_gain,
    key_gain,
    gate_weight,
    up_weight,
    down_weight,
):
    micros, rows, width = inputs.shape
    deep = shards // wide
    span = shards * rows
    tokens = micros * span
    experts = router_weight.shape[1]
    column_width = width // shards
    heads = column_width // HDIM
    score_scale = 1.0 / math.sqrt(HDIM)
    shard_place = lax.axis_index("shard")

    gate_all = lax.all_gather(gate_weight, "expert", axis=0, tiled=True)
    up_all = lax.all_gather(up_weight, "expert", axis=0, tiled=True)
    down_all = lax.all_gather(down_weight, "expert", axis=0, tiled=True)

    small_own = jnp.concatenate(
        [router_weight.reshape(-1), attention_gain, expert_gain, query_gain, key_gain]
    )
    small = lax.all_gather(small_own, "shard", axis=0)
    cuts = [column_width * experts, column_width, column_width, HDIM // shards, HDIM // shards]
    starts = [sum(cuts[:place]) for place in range(len(cuts))]
    router_full, attn_gain, expert_gain_full, query_gain_full, key_gain_full = (
        small[:, start : start + length].reshape(-1)
        for start, length in zip(starts, cuts, strict=True)
    )
    router_full = router_full.reshape(width, experts)
    attn_gain = attn_gain.astype(F32)
    expert_gain_full = expert_gain_full.astype(F32)
    query_gain_full = query_gain_full.astype(F32)
    key_gain_full = key_gain_full.astype(F32)
    routes_all = lax.all_gather(routes, "shard", axis=1, tiled=True).reshape(tokens, -1)

    projections = jnp.stack(
        [
            weight.reshape(column_width, shards, column_width)
            for weight in (query_weight, key_weight, value_weight)
        ],
        axis=2,
    )
    projections = lax.all_to_all(
        projections, "shard", split_axis=1, concat_axis=0, tiled=True
    ).reshape(width, 3 * column_width)

    hidden_all = group_gather(inputs, deep, wide, 0).reshape(tokens, width)
    upstream_all = group_gather(cotangent, deep, wide, 1).reshape(tokens, width)

    wide_all = hidden_all.astype(F32)
    mixer_all = (wide_all * rms_scale(wide_all) * attn_gain).astype(BF16)
    projected = jnp.dot(mixer_all, projections, preferred_element_type=F32).reshape(
        micros, span, 3, heads, HDIM
    )
    cosine_table, sine_table = rotary(jnp.arange(span, dtype=jnp.int32).astype(F32), HDIM)
    query_proj, key_proj = projected[:, :, 0], projected[:, :, 1]
    value_low = projected[:, :, 2].astype(BF16)
    query_norm_scale = rms_scale(query_proj)
    query_unit = query_proj * query_norm_scale
    query_rot = rotate(query_unit * query_gain_full, cosine_table, sine_table).astype(BF16)
    key_norm_scale = rms_scale(key_proj)
    key_unit = key_proj * key_norm_scale
    key_rot = rotate(key_unit * key_gain_full, cosine_table, sine_table).astype(BF16)
    same_doc = segment_ids[:, :, None] == segment_ids[:, None, :]
    scores = (
        jnp.einsum("mqhd,mkhd->mhqk", query_rot, key_rot, preferred_element_type=F32) * score_scale
    )
    scores = jnp.where(same_doc[:, None], scores, MASK_FILL)
    row_peak = jnp.max(scores, axis=-1, keepdims=True)
    exponent = jnp.exp(scores - row_peak)
    probs = exponent / jnp.sum(exponent, axis=-1, keepdims=True)
    probs_low = probs.astype(BF16)
    attended = jnp.einsum("mhqk,mkhd->mqhd", probs_low, value_low, preferred_element_type=F32)
    attended = attended.astype(BF16).reshape(tokens, column_width)
    middle_parts = jnp.dot(attended, output_weight, preferred_element_type=F32).astype(BF16)
    hidden = inputs.astype(F32)
    middle = hidden + group_scatter(
        middle_parts.reshape(micros, shards, rows, width), deep, wide, 2
    )

    scale_second = rms_scale(middle)
    normed_second = middle * scale_second
    expert_input = (normed_second * expert_gain_full).astype(BF16)
    expert_all = group_gather(expert_input, deep, wide, 3).reshape(tokens, width)
    logits = jnp.dot(expert_all, router_full, preferred_element_type=F32)
    choose = (routes_all[:, :, None] == jnp.arange(experts, dtype=jnp.int32)).astype(F32)
    share = softmax_rows(jnp.sum(choose * logits[:, None, :], axis=-1))
    share_wide = jnp.sum(choose * share[:, :, None], axis=1)
    served = (jnp.arange(groups, dtype=jnp.int32) * shards + shard_place) // 2
    serves = (served[:, None] == jnp.arange(experts, dtype=jnp.int32)).astype(F32)
    share_own = jnp.pad(
        jnp.dot(share_wide, serves.T, precision=PRECISE), ((0, 0), (0, 128 - groups))
    )
    activated, gate_pre, up_pre, dots = expert_units(
        expert_all, upstream_all, share_own, gate_all, up_all, down_all
    )
    expert_grad_parts = expert_merge(gate_pre, up_pre, gate_all, up_all)
    out_parts = expert_output(activated, down_all)
    gate_terms, up_terms, down_terms = expert_weights(
        expert_all, upstream_all, activated, gate_pre, up_pre
    )
    gate_grad = lax.psum_scatter(gate_terms, "expert", scatter_dimension=0, tiled=True)
    up_grad = lax.psum_scatter(up_terms, "expert", scatter_dimension=0, tiled=True)
    down_grad = lax.psum_scatter(down_terms, "expert", scatter_dimension=0, tiled=True)
    share_grad_wide = lax.psum(
        jnp.dot(dots[:, :groups], serves, precision=PRECISE), "shard"
    )
    expert_grad = group_scatter(
        expert_grad_parts.reshape(micros, shards, rows, width), deep, wide, 4
    )
    result = middle + group_scatter(out_parts.reshape(micros, shards, rows, width), deep, wide, 5)

    share_grad = jnp.sum(choose * share_grad_wide[:, None, :], axis=-1)
    chosen_grad = share * (share_grad - jnp.sum(share * share_grad, axis=-1, keepdims=True))
    logits_grad = jnp.sum(choose * chosen_grad[:, :, None], axis=1)
    own_logits_grad = lax.dynamic_slice_in_dim(
        logits_grad.reshape(micros, span, experts), shard_place * rows, rows, 1
    )
    expert_grad = expert_grad + jnp.dot(
        own_logits_grad, router_full.astype(F32).T, precision=PRECISE
    )
    expert_gain_term = jnp.sum(expert_grad * normed_second, axis=(0, 1))
    middle_grad = cotangent.astype(F32) + norm_back(
        expert_grad * expert_gain_full, normed_second, scale_second
    )
    router_term = jnp.einsum(
        "mtd,mte->de", expert_input.astype(F32), own_logits_grad, precision=PRECISE
    )
    branch_all = group_gather(middle_grad.astype(BF16), deep, wide, 6).reshape(tokens, width)

    attended_grad = jnp.einsum("te,de->td", branch_all, output_weight, preferred_element_type=F32)
    attended_grad = attended_grad.astype(BF16).reshape(micros, span, heads, HDIM)
    output_term = jnp.einsum("td,te->de", attended, branch_all, preferred_element_type=F32)
    prob_grad = jnp.einsum("mqhd,mkhd->mhqk", attended_grad, value_low, preferred_element_type=F32)
    row_delta = jnp.sum(probs * prob_grad, axis=-1, keepdims=True)
    score_grad = (probs * (prob_grad - row_delta)).astype(BF16)
    query_rot_grad = (
        jnp.einsum("mhqk,mkhd->mqhd", score_grad, key_rot, preferred_element_type=F32) * score_scale
    )
    key_rot_grad = (
        jnp.einsum("mhqk,mqhd->mkhd", score_grad, query_rot, preferred_element_type=F32)
        * score_scale
    )
    value_grad_low = jnp.einsum(
        "mhqk,mqhd->mkhd", probs_low, attended_grad, preferred_element_type=F32
    ).astype(BF16)
    query_unit_grad = rotate(query_rot_grad, cosine_table, -sine_table)
    query_gain_term = jnp.sum(query_unit_grad * query_unit, axis=(0, 1, 2))
    query_proj_grad = norm_back(
        query_unit_grad * query_gain_full, query_unit, query_norm_scale
    ).astype(BF16)
    key_unit_grad = rotate(key_rot_grad, cosine_table, -sine_table)
    key_gain_term = jnp.sum(key_unit_grad * key_unit, axis=(0, 1, 2))
    key_proj_grad = norm_back(key_unit_grad * key_gain_full, key_unit, key_norm_scale).astype(BF16)
    projected_grad = jnp.stack([query_proj_grad, key_proj_grad, value_grad_low], axis=2).reshape(
        tokens, 3 * column_width
    )
    mixer_parts = jnp.einsum(
        "te,de->td", projected_grad, projections, preferred_element_type=F32
    ).astype(BF16)
    mixer_grad = group_scatter(mixer_parts.reshape(micros, shards, rows, width), deep, wide, 7)
    scale_first = rms_scale(hidden)
    normed_first = hidden * scale_first
    attn_gain_term = jnp.sum(mixer_grad * normed_first, axis=(0, 1))
    hidden_grad = middle_grad + norm_back(mixer_grad * attn_gain, normed_first, scale_first)

    projection_terms = jnp.einsum(
        "td,te->de", mixer_all, projected_grad, preferred_element_type=F32
    ).astype(BF16)
    projection_terms = lax.all_to_all(
        projection_terms.reshape(width, 1, 3, column_width),
        "shard",
        split_axis=0,
        concat_axis=1,
        tiled=True,
    )
    projection_terms = jnp.transpose(projection_terms, (2, 0, 1, 3)).reshape(
        3, column_width, width
    )
    projection_grads, output_grad = lax.psum(
        (projection_terms, output_term.astype(BF16)), "expert"
    )
    projection_grads = projection_grads.astype(F32)
    tail = jnp.concatenate(
        [router_term.reshape(-1), attn_gain_term, expert_gain_term, query_gain_term, key_gain_term]
    )
    tail = lax.psum(tail, ("expert", "shard"))

    def tail_part(start, length):
        return lax.dynamic_slice_in_dim(tail[start * shards :], shard_place * length, length)

    tails = [tail_part(start, length) for start, length in zip(starts, cuts, strict=True)]
    return (
        result.astype(BF16),
        hidden_grad.astype(BF16),
        projection_grads[0],
        projection_grads[1],
        projection_grads[2],
        output_grad.astype(F32),
        tails[0].reshape(column_width, experts),
        tails[1],
        tails[2],
        tails[3],
        tails[4],
        gate_grad.astype(F32),
        up_grad.astype(F32),
        down_grad.astype(F32),
    )


def solution(mesh):
    groups, shards = mesh.shape["expert"], mesh.shape["shard"]
    wide = shards // 4 if shards % 4 == 0 else 1
    in_specs = (
        P(None, ("expert", "shard"), None),
        P(None, "expert"),
        P(None, ("expert", "shard"), None),
        P(None, ("expert", "shard"), None),
        P("shard", None),
        P("shard", None),
        P("shard", None),
        P("shard", None),
        P("shard", None),
        P("shard"),
        P("shard"),
        P("shard"),
        P("shard"),
        P(("expert", "shard"), None, None),
        P(("expert", "shard"), None, None),
        P(("expert", "shard"), None, None),
    )
    out_specs = (
        P(None, ("expert", "shard"), None),
        P(None, ("expert", "shard"), None),
        P("shard", None),
        P("shard", None),
        P("shard", None),
        P("shard", None),
        P("shard", None),
        P("shard"),
        P("shard"),
        P("shard"),
        P("shard"),
        P(("expert", "shard"), None, None),
        P(("expert", "shard"), None, None),
        P(("expert", "shard"), None, None),
    )
    return jax.shard_map(
        functools.partial(per_device, groups, shards, wide),
        mesh=mesh,
        in_specs=in_specs,
        out_specs=out_specs,
        check_vma=False,
    )
```

```python
import functools
import math

import jax
import jax.numpy as jnp
from jax import lax
from jax.experimental import pallas as pl
from jax.experimental.pallas import tpu as pltpu
from jax.sharding import PartitionSpec as P

HDIM = 128
EPSILON = 1e-05
ROPE_BASE = 10000.0
MASK_FILL = -1e30
PRECISE = lax.Precision.HIGHEST
MESH = pl.DeviceIdType.MESH
F32 = jnp.float32
BF16 = jnp.bfloat16
NN = (((1,), (0,)), ((), ()))
NT = (((1,), (1,)), ((), ()))
TN = (((0,), (0,)), ((), ()))
VMEM_LIMIT = 60 << 20
LINK_COST = pl.CostEstimate(flops=60 * 10**9, bytes_accessed=8 << 20, transcendentals=0)


def dot(left, right, dims):
    return lax.dot_general(left, right, dims, preferred_element_type=F32)


def rms_scale(values):
    return lax.rsqrt(jnp.mean(values * values, axis=-1, keepdims=True) + EPSILON)


def norm_back(normed_grad, normed, inv_scale):
    return inv_scale * (
        normed_grad - normed * jnp.mean(normed_grad * normed, axis=-1, keepdims=True)
    )


def rotary(span):
    steps = jnp.arange(HDIM // 2, dtype=jnp.int32).astype(F32)
    freqs = jnp.power(ROPE_BASE, -2.0 * steps / HDIM)
    theta = jnp.arange(span, dtype=jnp.int32).astype(F32)[:, None] * freqs[None, :]
    cosine, sine = jnp.cos(theta), jnp.sin(theta)
    return (
        jnp.concatenate([cosine, cosine], axis=1),
        jnp.concatenate([-sine, sine], axis=1),
    )


def softmax_rows(scores):
    row_peak = jnp.max(scores, axis=-1, keepdims=True)
    exponent = jnp.exp(scores - row_peak)
    return exponent / jnp.sum(exponent, axis=-1, keepdims=True)


class Place:
    def __init__(self, groups, deep, wide):
        self.deep, self.wide = deep, wide
        self.shards, self.groups, self.layers = deep * wide, groups, groups // 2
        group, me = lax.axis_index("expert"), lax.axis_index("shard")
        self.group, self.me = group, me
        self.layer, self.core = group // 2, lax.rem(group, 2)
        self.row, self.column = me // wide, lax.rem(me, wide)

    def peer(self, layer_step=0, core_step=0, row_step=0, column_step=0):
        group, me = self.group, self.me
        if layer_step or core_step:
            group = lax.rem(self.layer + layer_step, self.layers) * 2 + (
                1 - self.core if core_step else self.core
            )
        if row_step or column_step:
            me = lax.rem(self.row + row_step, self.deep) * self.wide + lax.rem(
                self.column + column_step, self.wide
            )
        return group, me

    def grid_place(self, row_step, column_step):
        return self.peer(0, 0, row_step, column_step)[1]

    def back(self, layer_step=0, core_step=0, row_step=0, column_step=0):
        return self.peer(
            (self.layers - layer_step) % self.layers,
            core_step,
            (self.deep - row_step) % self.deep,
            (self.wide - column_step) % self.wide,
        )


def send_to(peer, source, target, send_sem, recv_sem):
    return pltpu.make_async_remote_copy(
        src_ref=source,
        dst_ref=target,
        send_sem=send_sem,
        recv_sem=recv_sem,
        device_id=peer,
        device_id_type=MESH,
    )


def dma(*shape):
    return pltpu.SemaphoreType.DMA(tuple(max(1, size) for size in shape))


ANYWHERE = pl.BlockSpec(memory_space=pl.ANY)
RESIDENT = pl.BlockSpec(memory_space=pltpu.VMEM)


def grid_steps(deep, wide):
    steps = {(0, 0, row, 0) for row in range(1, deep)}
    return steps | {(0, 0, 0, column) for column in range(1, wide)}


def shard_steps(deep, wide):
    return {
        (0, 0, row, column) for row in range(deep) for column in range(wide) if row or column
    }


def expert_steps(layers):
    return {(step, 0, 0, 0) for step in range(1, layers)} | {(0, 1, 0, 0)}


def fuse(parts, layout, collective_id, name):
    groups, deep, wide = layout
    operands = [operand for part in parts for operand in part.operands]
    in_specs = [spec for part in parts for spec in part.in_specs]
    out_shape = [out for part in parts for out in part.outs]
    out_specs = [spec for part in parts for spec in part.out_specs]
    scratch = [buffer for part in parts for buffer in part.scratch]
    steps = sorted(set().union(*(part.steps for part in parts)))

    def kernel(*refs):
        place = Place(groups, deep, wide)
        barrier = pltpu.get_barrier_semaphore()
        for step in steps:
            pl.semaphore_signal(
                barrier, inc=1, device_id=place.peer(*step), device_id_type=MESH
            )
        pl.semaphore_wait(barrier, len(steps))
        ins = list(refs[: len(operands)])
        outs = list(refs[len(operands) : len(operands) + len(out_shape)])
        buffers = list(refs[len(operands) + len(out_shape) :])
        running = []
        for part in parts:
            part_ins = [ins.pop(0) for _ in part.operands]
            part_outs = [outs.pop(0) for _ in part.outs]
            part_buffers = [buffers.pop(0) for _ in part.scratch]
            running.append(part.run(place, *part_ins, *part_outs, *part_buffers))
        while running:
            for part in list(running):
                try:
                    next(part)
                except StopIteration:
                    running.remove(part)

    results = pl.pallas_call(
        kernel,
        out_shape=out_shape,
        in_specs=in_specs,
        out_specs=out_specs,
        scratch_shapes=scratch,
        compiler_params=pltpu.CompilerParams(
            collective_id=collective_id, has_side_effects=True, vmem_limit_bytes=VMEM_LIMIT
        ),
        cost_estimate=LINK_COST,
        name=name,
    )(*operands)
    results = list(results)
    return [[results.pop(0) for _ in part.outs] for part in parts]


class Chain:
    def __init__(self, *parts):
        self.parts = parts
        for name in ("operands", "in_specs", "outs", "out_specs", "scratch"):
            setattr(self, name, [item for part in parts for item in getattr(part, name)])
        self.steps = set().union(*(part.steps for part in parts))

    def run(self, place, *refs):
        refs = list(refs)
        taken = [[] for _ in self.parts]
        for name in ("operands", "outs", "scratch"):
            for part, own in zip(self.parts, taken, strict=True):
                own.extend(refs.pop(0) for _ in getattr(part, name))
        for part, own in zip(self.parts, taken, strict=True):
            yield from part.run(place, *own)


class Gather:
    def __init__(self, own, layout):
        _, deep, wide = layout
        pieces, rows, width = own.shape
        self.operands, self.in_specs = [own], [ANYWHERE]
        self.outs = [jax.ShapeDtypeStruct((pieces, deep * wide, rows, width), own.dtype)]
        self.out_specs = [ANYWHERE]
        self.scratch = [
            dma(pieces, deep - 1),
            dma(pieces, deep - 1),
            dma(pieces, deep, wide - 1),
            dma(pieces, deep, wide - 1),
            dma(1),
        ]
        self.steps = grid_steps(deep, wide)

    def run(self, place, own, whole, row_send, row_recv, col_send, col_recv, local):
        pieces, deep, wide = own.shape[0], place.deep, place.wide
        here = pltpu.make_async_copy(own, whole.at[:, place.me], local.at[0])
        here.start()
        sends = []

        def along_column(piece, step):
            return send_to(
                place.peer(0, 0, step, 0),
                own.at[piece],
                whole.at[piece, place.me],
                row_send.at[piece, step - 1],
                row_recv.at[piece, step - 1],
            )

        def along_row(piece, turn, step, block, source):
            return send_to(
                place.peer(0, 0, 0, step),
                block,
                whole.at[piece, source],
                col_send.at[piece, turn, step - 1],
                col_recv.at[piece, turn, step - 1],
            )

        def forward(piece, turn, block, source):
            for step in range(1, wide):
                sends.append(along_row(piece, turn, step, block, source))
                sends[-1].start()

        for piece in range(pieces):
            for step in range(1, deep):
                sends.append(along_column(piece, step))
                sends[-1].start()
            forward(piece, 0, own.at[piece], place.me)
        yield
        for piece in range(pieces):
            for step in range(1, deep):
                source = place.grid_place(deep - step, 0)
                along_column(piece, step).wait_recv()
                forward(piece, step, whole.at[piece, source], source)
                yield
        for piece in range(pieces):
            for turn in range(deep):
                for step in range(1, wide):
                    source = place.grid_place(deep - turn, wide - step)
                    along_row(piece, turn, step, own.at[piece], source).wait_recv()
                yield
        for copy in sends:
            copy.wait_send()
        here.wait()


class Scatter:
    def __init__(self, parts, layout):
        _, deep, wide = layout
        pieces, _, rows, width = parts.shape
        self.operands, self.in_specs = [parts], [RESIDENT]
        self.outs = [jax.ShapeDtypeStruct((pieces, rows, width), F32)]
        self.out_specs = [RESIDENT]
        self.scratch = [
            pltpu.VMEM((pieces, deep, max(1, wide - 1), rows, width), BF16),
            pltpu.VMEM((pieces, deep - 1, rows, width), BF16),
            pltpu.VMEM((pieces, deep - 1, rows, width), BF16),
            dma(pieces, deep, wide - 1),
            dma(pieces, deep, wide - 1),
            dma(pieces, deep - 1),
            dma(pieces, deep - 1),
        ]
        self.steps = grid_steps(deep, wide)

    def run(
        self, place, parts, total, landed, merged, summed, col_send, col_recv, row_send, row_recv
    ):
        pieces, deep, wide = parts.shape[0], place.deep, place.wide
        sends = []

        def along_row(piece, turn, step):
            return send_to(
                place.peer(0, 0, 0, step),
                parts.at[piece, place.grid_place(turn + 1, step)],
                landed.at[piece, turn, step - 1],
                col_send.at[piece, turn, step - 1],
                col_recv.at[piece, turn, step - 1],
            )

        def along_column(piece, turn):
            return send_to(
                place.peer(0, 0, turn + 1, 0),
                merged.at[piece, turn],
                summed.at[piece, turn],
                row_send.at[piece, turn],
                row_recv.at[piece, turn],
            )

        for piece in range(pieces):
            for turn in range(deep):
                for step in range(1, wide):
                    sends.append(along_row(piece, turn, step))
                    sends[-1].start()
        yield
        for piece in range(pieces):
            for turn in range(deep):
                value = parts[piece, place.grid_place((turn + 1) % deep, 0)].astype(F32)
                for step in range(1, wide):
                    along_row(piece, turn, step).wait_recv()
                    value = value + landed[piece, turn, step - 1].astype(F32)
                if turn < deep - 1:
                    merged[piece, turn] = value.astype(BF16)
                    sends.append(along_column(piece, turn))
                    sends[-1].start()
                else:
                    total[piece] = value
                yield
        for piece in range(pieces):
            value = total[piece]
            for turn in range(deep - 1):
                along_column(piece, turn).wait_recv()
                value = value + summed[piece, turn].astype(F32)
            total[piece] = value
            yield
        for copy in sends:
            copy.wait_send()


class ExpertScatter:
    def __init__(self, terms, layout, chunks=2):
        groups = layout[0]
        layers = groups // 2
        _, rows, width = terms.shape
        part = rows // chunks
        self.operands, self.in_specs = [terms], [ANYWHERE]
        self.outs = [jax.ShapeDtypeStruct((rows, width), BF16)]
        self.out_specs = [RESIDENT]
        self.scratch = [
            pltpu.VMEM((chunks, layers, part, width), BF16),
            pltpu.VMEM((chunks, layers, part, width), BF16),
            pltpu.VMEM((chunks, max(1, layers - 1), part, width), BF16),
            dma(chunks, layers),
            dma(chunks, layers),
            dma(chunks, layers),
            dma(chunks, layers - 1),
            dma(chunks, layers - 1),
        ]
        self.steps = expert_steps(layers)

    def run(
        self,
        place,
        terms,
        total,
        mine,
        landed,
        summed,
        local,
        core_send,
        core_recv,
        layer_send,
        layer_recv,
    ):
        chunks, layers, part, _ = mine.shape
        span = min(part, 128)
        sends = []

        def entry(turn, core):
            return lax.rem(place.layer + turn, layers) * 2 + core

        def block(chunk, turn, core):
            return terms.at[entry(turn, core), pl.ds(chunk * part, part)]

        def load(chunk, turn):
            return pltpu.make_async_copy(
                block(chunk, turn, place.core), mine.at[chunk, turn], local.at[chunk, turn]
            )

        def across(chunk, turn):
            return send_to(
                place.peer(0, 1, 0, 0),
                block(chunk, turn, 1 - place.core),
                landed.at[chunk, turn],
                core_send.at[chunk, turn],
                core_recv.at[chunk, turn],
            )

        def along(chunk, turn):
            return send_to(
                place.peer(turn, 0, 0, 0),
                mine.at[chunk, turn],
                summed.at[chunk, turn - 1],
                layer_send.at[chunk, turn - 1],
                layer_recv.at[chunk, turn - 1],
            )

        order = [*range(1, layers), 0]
        for chunk in range(chunks):
            for turn in order:
                load(chunk, turn).start()
                sends.append(across(chunk, turn))
                sends[-1].start()
        yield
        for chunk in range(chunks):
            for turn in order[:-1]:
                load(chunk, turn).wait()
                across(chunk, turn).wait_recv()

                def merge(step, carry, chunk=chunk, turn=turn):
                    rows = pl.ds(pl.multiple_of(step * span, span), span)
                    value = mine[chunk, turn, rows].astype(F32)
                    value = value + landed[chunk, turn, rows].astype(F32)
                    mine[chunk, turn, rows] = value.astype(BF16)
                    return carry

                lax.fori_loop(0, part // span, merge, 0)
                sends.append(along(chunk, turn))
                sends[-1].start()
                yield
        for chunk in range(chunks):
            load(chunk, 0).wait()
            across(chunk, 0).wait_recv()
            for turn in order[:-1]:
                along(chunk, turn).wait_recv()

            def finish(step, carry, chunk=chunk):
                rows = pl.ds(pl.multiple_of(step * span, span), span)
                here = pl.ds(pl.multiple_of(chunk * part + step * span, span), span)
                value = mine[chunk, 0, rows].astype(F32) + landed[chunk, 0, rows].astype(F32)
                for turn in order[:-1]:
                    value = value + summed[chunk, turn - 1, rows].astype(F32)
                total[here] = value.astype(BF16)
                return carry

            lax.fori_loop(0, part // span, finish, 0)
            yield
        for copy in sends:
            copy.wait_send()


class ExpertWeights:
    SPAN = 256

    def __init__(self, rows, upstream, hidden, gate_pre, up_pre, down_all, layout):
        tokens, width = rows.shape
        halves, _, units = hidden.shape
        self.terms = jax.ShapeDtypeStruct((halves, width, units), BF16)
        self.inner = ExpertScatter(self.terms, layout)
        self.operands = [rows, upstream, hidden, gate_pre, up_pre, down_all]
        self.in_specs = [RESIDENT] * 5 + [ANYWHERE]
        self.outs = [
            self.terms,
            self.terms,
            jax.ShapeDtypeStruct((halves, units, width), BF16),
            jax.ShapeDtypeStruct((tokens, width), BF16),
            *self.inner.outs,
        ]
        self.out_specs = [ANYWHERE] * 3 + [RESIDENT] * 2
        self.scratch = [
            pltpu.VMEM((2, width, units), BF16),
            pltpu.VMEM((units, width), BF16),
            pltpu.VMEM((2, halves, units, self.SPAN), BF16),
            dma(2),
            dma(1),
            dma(2),
            *self.inner.scratch,
        ]
        self.steps = self.inner.steps

    def run(
        self,
        place,
        rows,
        upstream,
        hidden,
        gate_pre,
        up_pre,
        down_all,
        gate_terms,
        up_terms,
        down_terms,
        out,
        gate_total,
        stage,
        stage_down,
        tiles,
        stage_sem,
        stage_down_sem,
        tile_sem,
        *inner_scratch,
    ):
        halves, _, units = hidden.shape
        width = rows.shape[1]
        span = self.SPAN
        state = {"slot": 0, "busy": [None, None], "down": None}

        def columns(grads, target):
            for half in range(halves):
                slot = state["slot"]
                if state["busy"][slot] is not None:
                    state["busy"][slot].wait()
                for step in range(units // span):
                    here = pl.ds(step * span, span)
                    stage[slot, :, here] = dot(rows[...], grads[half, :, here], TN).astype(BF16)
                    if step < units // span - 1:
                        yield
                copy = pltpu.make_async_copy(stage.at[slot], target.at[half], stage_sem.at[slot])
                copy.start()
                state["busy"][slot] = copy
                state["slot"] = 1 - slot
                yield

        def drain():
            for slot in (0, 1):
                if state["busy"][slot] is not None:
                    state["busy"][slot].wait()
                    state["busy"][slot] = None

        def downs():
            copy = None
            for half in range(halves):
                if copy is not None:
                    copy.wait()
                for step in range(units // span):
                    here = pl.ds(step * span, span)
                    stage_down[here, :] = dot(hidden[half, :, here], upstream[...], TN).astype(
                        BF16
                    )
                    if step < units // span - 1:
                        yield
                copy = pltpu.make_async_copy(
                    stage_down, down_terms.at[half], stage_down_sem.at[0]
                )
                copy.start()
                yield
            copy.wait()

        def tile(step):
            return pltpu.make_async_copy(
                down_all.at[:, :, pl.ds(step * span, span)],
                tiles.at[step % 2],
                tile_sem.at[step % 2],
            )

        def outputs():
            for step in range(width // span):
                if step + 1 < width // span:
                    tile(step + 1).start()
                tile(step).wait()
                value = dot(hidden[0], tiles[step % 2, 0], NN)
                for half in range(1, halves):
                    value = value + dot(hidden[half], tiles[step % 2, half], NN)
                out[:, pl.ds(step * span, span)] = value.astype(BF16)
                yield

        def rest():
            yield from columns(up_pre, up_terms)
            yield from downs()
            yield from outputs()
            drain()

        tile(0).start()
        for index, _ in enumerate(columns(gate_pre, gate_terms)):
            if index % 4 == 3:
                yield
        drain()
        inner = self.inner.run(place, gate_terms, gate_total, *inner_scratch)
        next(inner)
        others = rest()
        waiting, working = True, True
        while waiting or working:
            for _ in range(4):
                working = working and next(others, "end") != "end"
            if waiting:
                waiting = next(inner, "end") != "end"
            yield


class Columns:
    def __init__(self, weights, small, layout):
        groups, deep, wide = layout
        shards = deep * wide
        depth = weights[0].shape[0]
        self.operands, self.in_specs = [*weights, small], [ANYWHERE] * 4
        self.outs = [
            jax.ShapeDtypeStruct((shards, groups, depth // groups, 3 * depth), BF16),
            jax.ShapeDtypeStruct((shards,) + small.shape, BF16),
        ]
        self.out_specs = [ANYWHERE] * 2
        self.scratch = [
            dma(3, shards - 1),
            dma(3, shards - 1),
            dma(shards - 1),
            dma(shards - 1),
            dma(groups // 2 - 1),
            dma(groups // 2 - 1),
            dma(groups // 2),
            dma(groups // 2),
            dma(4),
        ]
        self.steps = shard_steps(deep, wide) | expert_steps(groups // 2)

    def run(
        self,
        place,
        query_weight,
        key_weight,
        value_weight,
        small,
        projections,
        small_all,
        weight_send,
        weight_recv,
        small_send,
        small_recv,
        layer_send,
        layer_recv,
        core_send,
        core_recv,
        local,
    ):
        weights = (query_weight, key_weight, value_weight)
        layers, group, me = place.layers, place.group, place.me
        part = projections.shape[2]
        depth = query_weight.shape[0]
        steps = sorted(shard_steps(place.deep, place.wide))
        sends = []

        def block(which, target):
            return weights[which].at[
                pl.ds(pl.multiple_of(group * part, part), part),
                pl.ds(pl.multiple_of(target * depth, depth), depth),
            ]

        def slot(which, source):
            return projections.at[source, group, :, pl.ds(which * depth, depth)]

        def weight_copy(which, index):
            return send_to(
                place.peer(*steps[index]),
                block(which, place.peer(*steps[index])[1]),
                slot(which, me),
                weight_send.at[which, index],
                weight_recv.at[which, index],
            )

        def small_copy(index):
            return send_to(
                place.peer(*steps[index]),
                small,
                small_all.at[me],
                small_send.at[index],
                small_recv.at[index],
            )

        def slab_copy(peer, layer, core, send_sem, recv_sem):
            slab = projections.at[:, layer * 2 + core]
            return send_to(peer, slab, slab, send_sem, recv_sem)

        def layer_copy(step, layer):
            return slab_copy(
                place.peer(step, 0, 0, 0),
                layer,
                place.core,
                layer_send.at[step - 1],
                layer_recv.at[step - 1],
            )

        def core_copy(step, layer, core):
            return slab_copy(
                place.peer(0, 1, 0, 0), layer, core, core_send.at[step], core_recv.at[step]
            )

        here = [
            pltpu.make_async_copy(block(which, me), slot(which, me), local.at[which])
            for which in range(3)
        ]
        here.append(pltpu.make_async_copy(small, small_all.at[me], local.at[3]))
        for copy in here:
            copy.start()
        for index in range(len(steps)):
            for which in range(3):
                sends.append(weight_copy(which, index))
                sends[-1].start()
            sends.append(small_copy(index))
            sends[-1].start()
        yield
        for copy in here:
            copy.wait()
        for index in range(len(steps)):
            for which in range(3):
                weight_copy(which, index).wait_recv()
        for step in range(1, layers):
            sends.append(layer_copy(step, place.layer))
            sends[-1].start()
        sends.append(core_copy(0, place.layer, place.core))
        sends[-1].start()
        yield
        for step in range(1, layers):
            layer = lax.rem(place.layer + layers - step, layers)
            layer_copy(step, layer).wait_recv()
            sends.append(core_copy(step, layer, place.core))
            sends[-1].start()
            yield
        for step in range(layers):
            layer = lax.rem(place.layer + layers - step, layers)
            core_copy(step, layer, 1 - place.core).wait_recv()
            yield
        for index in range(len(steps)):
            small_copy(index).wait_recv()
        for copy in sends:
            copy.wait_send()


class Rows:
    def __init__(self, terms, row_terms, tail, layout):
        groups, deep, wide = layout
        layers = groups // 2
        shards, _, part, width = terms.shape
        depth = row_terms.shape[2]
        self.operands = [terms, row_terms, tail]
        self.in_specs = [RESIDENT] * 3
        self.outs = [
            jax.ShapeDtypeStruct((groups, part, depth), BF16),
            jax.ShapeDtypeStruct(tail.shape[1:], F32),
            *[jax.ShapeDtypeStruct((groups, part, depth), BF16)] * 3,
        ]
        self.out_specs = [RESIDENT] * 5
        others = max(1, layers - 1)
        self.scratch = [
            pltpu.VMEM((groups, shards, part, width), BF16),
            pltpu.VMEM((layers, shards, part, width), BF16),
            pltpu.VMEM((others, shards, part, width), BF16),
            pltpu.VMEM((others, shards, part, width), BF16),
            pltpu.VMEM((shards, part, width), BF16),
            pltpu.VMEM((layers, part, depth), BF16),
            pltpu.VMEM((others, part, depth), BF16),
            pltpu.VMEM((others, part, depth), BF16),
            pltpu.VMEM(tail.shape, F32),
            pltpu.VMEM((groups,) + tail.shape[1:], F32),
            dma(2, layers),
            dma(2, layers),
            dma(2, others),
            dma(2, others),
            dma(shards - 1),
            dma(shards - 1),
            dma(2, others),
            dma(2, others),
            dma(2, layers),
            dma(2, layers),
            dma(shards - 1),
            dma(shards - 1),
            dma(groups - 1),
            dma(groups - 1),
        ]
        self.steps = shard_steps(deep, wide) | expert_steps(layers)
        self.steps |= {(layer, core, 0, 0) for layer in range(layers) for core in (0, 1)}
        self.steps -= {(0, 0, 0, 0)}

    def run(
        self,
        place,
        terms,
        row_terms,
        tail,
        whole_rows,
        tail_out,
        query_out,
        key_out,
        value_out,
        whole,
        landed,
        merged,
        summed,
        ready,
        landed_rows,
        merged_rows,
        summed_rows,
        tails,
        tail_sums,
        core_send,
        core_recv,
        layer_send,
        layer_recv,
        swap_send,
        swap_recv,
        out_send,
        out_recv,
        over_send,
        over_recv,
        tail_send,
        tail_recv,
        sum_send,
        sum_recv,
    ):
        layers, group, me, core = place.layers, place.group, place.me, place.core
        shards = place.shards
        steps = sorted(shard_steps(place.deep, place.wide))
        group_steps = [
            (layer, flip, 0, 0) for layer in range(layers) for flip in (0, 1) if layer or flip
        ]
        sends = []

        def start(copy):
            copy.start()
            sends.append(copy)

        def layer_at(turn):
            return lax.rem(place.layer + turn, layers)

        def tail_copy(index):
            peer = place.peer(*steps[index])
            return send_to(
                peer, tail.at[peer[1]], tails.at[me], tail_send.at[index], tail_recv.at[index]
            )

        def sum_copy(index):
            return send_to(
                place.peer(*group_steps[index]),
                tail_sums.at[group],
                tail_sums.at[group],
                sum_send.at[index],
                sum_recv.at[index],
            )

        def across(which, turn):
            entry = layer_at(turn) * 2 + 1 - core
            source = row_terms.at[entry] if which else terms.at[:, entry]
            target = landed_rows.at[turn] if which else landed.at[turn]
            return send_to(
                place.peer(0, 1, 0, 0),
                source,
                target,
                core_send.at[which, turn],
                core_recv.at[which, turn],
            )

        def along(which, turn):
            source = merged_rows.at[turn - 1] if which else merged.at[turn - 1]
            target = summed_rows.at[turn - 1] if which else summed.at[turn - 1]
            return send_to(
                place.peer(turn, 0, 0, 0),
                source,
                target,
                layer_send.at[which, turn - 1],
                layer_recv.at[which, turn - 1],
            )

        def swap(index):
            peer = place.peer(*steps[index])
            return send_to(
                peer,
                ready.at[peer[1]],
                whole.at[group, me],
                swap_send.at[index],
                swap_recv.at[index],
            )

        def out(which, turn, entry):
            slab = whole_rows.at[entry] if which else whole.at[entry]
            return send_to(
                place.peer(turn, 0, 0, 0),
                slab,
                slab,
                out_send.at[which, turn - 1],
                out_recv.at[which, turn - 1],
            )

        def over(which, turn, entry):
            slab = whole_rows.at[entry] if which else whole.at[entry]
            return send_to(
                place.peer(0, 1, 0, 0),
                slab,
                slab,
                over_send.at[which, turn],
                over_recv.at[which, turn],
            )

        order = [*range(1, layers), 0]
        for which in (0, 1):
            for turn in order:
                start(across(which, turn))
        for index in range(len(steps)):
            start(tail_copy(index))
        yield
        for which in (0, 1):
            for turn in order[:-1]:
                across(which, turn).wait_recv()
                entry = layer_at(turn) * 2 + core
                if which:
                    merged_rows[turn - 1] = (
                        row_terms[entry].astype(F32) + landed_rows[turn].astype(F32)
                    ).astype(BF16)
                else:
                    for shard in range(shards):
                        merged[turn - 1, shard] = (
                            terms[shard, entry].astype(F32) + landed[turn, shard].astype(F32)
                        ).astype(BF16)
                start(along(which, turn))
                yield
        for which in (0, 1):
            across(which, 0).wait_recv()
        for index in range(len(steps)):
            tail_copy(index).wait_recv()
        tails[me] = tail[me]
        tail_sum = tails[0]
        for shard in range(1, shards):
            tail_sum = tail_sum + tails[shard]
        tail_sums[group] = tail_sum
        for index in range(len(group_steps)):
            start(sum_copy(index))
        yield
        for turn in order[:-1]:
            along(0, turn).wait_recv()
        for shard in range(shards):
            value = terms[shard, group].astype(F32) + landed[0, shard].astype(F32)
            for turn in order[:-1]:
                value = value + summed[turn - 1, shard].astype(F32)
            ready[shard] = value.astype(BF16)
        for index in range(len(steps)):
            start(swap(index))
        whole[group, me] = ready[me]
        yield
        for turn in order[:-1]:
            along(1, turn).wait_recv()
        value = row_terms[group].astype(F32) + landed_rows[0].astype(F32)
        for turn in order[:-1]:
            value = value + summed_rows[turn - 1].astype(F32)
        whole_rows[group] = value.astype(BF16)
        for turn in order[:-1]:
            start(out(1, turn, group))
        start(over(1, 0, group))
        yield
        for index in range(len(steps)):
            swap(index).wait_recv()
        for turn in order[:-1]:
            start(out(0, turn, group))
        start(over(0, 0, group))
        yield
        for which in (1, 0):
            for turn in order[:-1]:
                entry = layer_at(layers - turn) * 2 + core
                out(which, turn, entry).wait_recv()
                start(over(which, turn, entry))
                yield
        for index in range(len(group_steps)):
            sum_copy(index).wait_recv()
        tail_sum = tail_sums[0]
        for index in range(1, place.groups):
            tail_sum = tail_sum + tail_sums[index]
        tail_out[...] = tail_sum
        depth = terms.shape[3] // 3
        for which in (1, 0):
            for turn in range(layers):
                entry = layer_at(layers - turn) * 2 + 1 - core
                over(which, turn, entry).wait_recv()
                yield
        for entry in range(place.groups):
            for shard in range(shards):
                here = pl.ds(shard * depth, depth)
                value = whole[entry, shard]
                query_out[entry, :, here] = value[:, :depth]
                key_out[entry, :, here] = value[:, depth : 2 * depth]
                value_out[entry, :, here] = value[:, 2 * depth :]
            yield
        for copy in sends:
            copy.wait_send()


def turn(values, cosine, sine):
    return values * cosine + pltpu.roll(values, HDIM // 2, 1) * sine


def head_forward(projected, place, gain, cosine, sine):
    proj = projected[:, place * HDIM : (place + 1) * HDIM]
    scale = rms_scale(proj)
    unit = proj * scale
    return scale, unit, turn(unit * gain, cosine, sine).astype(BF16)


def head_probs(query_rot, key_rot, seg_column, seg_row):
    scores = dot(query_rot, key_rot, NT) * (1.0 / math.sqrt(HDIM))
    scores = jnp.where(seg_column == seg_row, scores, MASK_FILL)
    exponent = jnp.exp(scores - jnp.max(scores, axis=-1, keepdims=True))
    return exponent * (1.0 / jnp.sum(exponent, axis=-1, keepdims=True))


def forward_steps(
    hidden,
    projections,
    output_weight,
    gain,
    head_gains,
    cosine,
    sine,
    seg_column,
    seg_row,
    mixer,
    projected,
    attended,
    parts,
):
    micros, span = seg_column.shape[0], seg_column.shape[1]
    heads = output_weight.shape[0] // HDIM
    tile = min(span, 256)
    for micro in range(micros):
        for start in range(0, span, tile):
            rows = pl.ds(micro * span + start, tile)
            values = hidden[rows, :].astype(F32)
            mixer[rows, :] = (values * rms_scale(values) * gain[...]).astype(BF16)
        rows = pl.ds(micro * span, span)
        projected[rows, :] = dot(mixer[rows, :], projections[...], NN)
        yield
        for head in range(heads):
            own = projected[rows, :]
            _, _, query_rot = head_forward(own, head, head_gains[0:1], cosine[...], sine[...])
            _, _, key_rot = head_forward(
                own, heads + head, head_gains[1:2], cosine[...], sine[...]
            )
            values = own[:, (2 * heads + head) * HDIM : (2 * heads + head + 1) * HDIM]
            probs = head_probs(query_rot, key_rot, seg_column[micro], seg_row[micro])
            attended[rows, head * HDIM : (head + 1) * HDIM] = dot(
                probs.astype(BF16), values.astype(BF16), NN
            ).astype(BF16)
            yield
        parts[rows, :] = dot(attended[rows, :], output_weight[...], NN).astype(BF16)
        yield


def backward_steps(
    branch,
    mixer,
    projected,
    attended,
    projections,
    output_weight,
    head_gains,
    cosine,
    sine,
    seg_column,
    seg_row,
    parts,
    projection_terms,
    output_terms,
    gain_terms,
    attended_grad,
    projected_grad,
):
    micros, span = seg_column.shape[0], seg_column.shape[1]
    heads = output_weight.shape[0] // HDIM
    scale = 1.0 / math.sqrt(HDIM)
    gain_terms[...] = jnp.zeros_like(gain_terms)
    for micro in range(micros):
        rows = pl.ds(micro * span, span)
        attended_grad[rows, :] = dot(branch[rows, :], output_weight[...], NT).astype(BF16)
        yield
        for head in range(heads):
            own = projected[rows, :]
            query_scale, query_unit, query_rot = head_forward(
                own, head, head_gains[0:1], cosine[...], sine[...]
            )
            key_scale, key_unit, key_rot = head_forward(
                own, heads + head, head_gains[1:2], cosine[...], sine[...]
            )
            values = own[:, (2 * heads + head) * HDIM : (2 * heads + head + 1) * HDIM]
            probs = head_probs(query_rot, key_rot, seg_column[micro], seg_row[micro])
            out_grad = attended_grad[rows, head * HDIM : (head + 1) * HDIM]
            prob_grad = dot(out_grad, values.astype(BF16), NT)
            row_delta = jnp.sum(probs * prob_grad, axis=-1, keepdims=True)
            score_grad = (probs * (prob_grad - row_delta)).astype(BF16)
            projected_grad[rows, (2 * heads + head) * HDIM : (2 * heads + head + 1) * HDIM] = dot(
                probs.astype(BF16), out_grad, TN
            ).astype(BF16)
            for which, (rot_grad, unit, unit_scale) in enumerate(
                (
                    (dot(score_grad, key_rot, NN) * scale, query_unit, query_scale),
                    (dot(score_grad, query_rot, TN) * scale, key_unit, key_scale),
                )
            ):
                unit_grad = turn(rot_grad, cosine[...], -sine[...])
                gain_terms[which : which + 1] += jnp.sum(unit_grad * unit, axis=0, keepdims=True)
                place = (which * heads + head) * HDIM
                projected_grad[rows, place : place + HDIM] = norm_back(
                    unit_grad * head_gains[which : which + 1], unit, unit_scale
                ).astype(BF16)
            yield
        parts[rows, :] = dot(projected_grad[rows, :], projections[...], NT).astype(BF16)
        yield
    tile = min(512, branch.shape[1])
    for start in range(0, branch.shape[1], tile):
        here = pl.ds(start, tile)
        output_terms[:, here] = dot(attended[...], branch[:, here], TN).astype(BF16)
        projection_terms[here, :] = dot(mixer[:, here], projected_grad[...], TN).astype(BF16)
        yield


def whole_kernel(steps):
    def kernel(*refs):
        for _ in steps(*refs):
            pass

    return kernel


def attention_forward(hidden, projections, output_weight, gain, head_gains, tables, segments):
    tokens, width = hidden.shape
    column_width = output_weight.shape[0]
    return pl.pallas_call(
        whole_kernel(forward_steps),
        in_specs=[RESIDENT] * 9,
        out_specs=[RESIDENT] * 4,
        out_shape=[
            jax.ShapeDtypeStruct((tokens, width), BF16),
            jax.ShapeDtypeStruct((tokens, 3 * column_width), F32),
            jax.ShapeDtypeStruct((tokens, column_width), BF16),
            jax.ShapeDtypeStruct((tokens, width), BF16),
        ],
        compiler_params=pltpu.CompilerParams(vmem_limit_bytes=VMEM_LIMIT),
        name="attention_forward",
    )(hidden, projections, output_weight, gain, head_gains, *tables, *segments)


def attention_backward(
    branch, mixer, projected, attended, projections, output_weight, head_gains, tables, segments
):
    tokens, width = branch.shape
    column_width = output_weight.shape[0]
    return pl.pallas_call(
        whole_kernel(backward_steps),
        in_specs=[RESIDENT] * 11,
        out_specs=[RESIDENT] * 4,
        out_shape=[
            jax.ShapeDtypeStruct((tokens, width), BF16),
            jax.ShapeDtypeStruct((width, 3 * column_width), BF16),
            jax.ShapeDtypeStruct((column_width, width), BF16),
            jax.ShapeDtypeStruct((8, HDIM), F32),
        ],
        scratch_shapes=[
            pltpu.VMEM((tokens, column_width), BF16),
            pltpu.VMEM((tokens, 3 * column_width), BF16),
        ],
        compiler_params=pltpu.CompilerParams(vmem_limit_bytes=VMEM_LIMIT),
        name="attention_backward",
    )(
        branch,
        mixer,
        projected,
        attended,
        projections,
        output_weight,
        head_gains,
        *tables,
        *segments,
    )


def units_kernel(
    span,
    rows_ref,
    upstream_ref,
    share_ref,
    gate_ref,
    up_ref,
    down_ref,
    hidden_ref,
    gate_pre_ref,
    up_pre_ref,
    dot_ref,
):
    half = pl.program_id(0)
    half_width = gate_ref.shape[2]
    lanes = lax.broadcasted_iota(jnp.int32, share_ref.shape, 1)
    share = jnp.sum(jnp.where(lanes == half, share_ref[...], 0.0), axis=1, keepdims=True)

    def body(step, carry):
        units = pl.ds(pl.multiple_of(step * span, span), span)
        gate_pre = dot(rows_ref[...], gate_ref[0, :, units], NN)
        up_pre = dot(rows_ref[...], up_ref[0, :, units], NN)
        units_grad = dot(upstream_ref[...], down_ref[0, units, :], NT)
        sigmoid_gate = 1.0 / (1.0 + jnp.exp(-gate_pre))
        swish_gate = gate_pre * sigmoid_gate
        activated = swish_gate * up_pre
        dots = jnp.sum(activated * units_grad, axis=1, keepdims=True)
        dot_ref[...] += jnp.where(lanes == half, dots, 0.0)
        hidden_ref[0, :, units] = (activated * share).astype(BF16)
        weighted = units_grad * share
        gate_pre_ref[0, :, units] = (
            weighted * up_pre * (sigmoid_gate * (1.0 + gate_pre * (1.0 - sigmoid_gate)))
        ).astype(BF16)
        up_pre_ref[0, :, units] = (weighted * swish_gate).astype(BF16)
        return carry

    @pl.when(half == 0)
    def _():
        dot_ref[...] = jnp.zeros_like(dot_ref)

    lax.fori_loop(0, half_width // span, body, 0)


def expert_units(rows, upstream, share, gate_all, up_all, down_all):
    tokens, width = rows.shape
    halves, _, units = gate_all.shape

    def each(*shape):
        return pl.BlockSpec((1,) + shape, lambda half: (half,) + (0,) * len(shape))

    whole = pl.BlockSpec(memory_space=pltpu.VMEM)
    return pl.pallas_call(
        functools.partial(units_kernel, 256 if tokens <= 1024 else 128),
        grid=(halves,),
        in_specs=[whole, whole, whole, each(width, units), each(width, units), each(units, width)],
        out_specs=[each(tokens, units), each(tokens, units), each(tokens, units), whole],
        out_shape=[
            jax.ShapeDtypeStruct((halves, tokens, units), BF16),
            jax.ShapeDtypeStruct((halves, tokens, units), BF16),
            jax.ShapeDtypeStruct((halves, tokens, units), BF16),
            jax.ShapeDtypeStruct(share.shape, F32),
        ],
        compiler_params=pltpu.CompilerParams(vmem_limit_bytes=VMEM_LIMIT),
        cost_estimate=pl.CostEstimate(
            flops=6 * tokens * width * units * halves,
            bytes_accessed=6 * width * units * halves,
            transcendentals=0,
        ),
    )(rows, upstream, share, gate_all, up_all, down_all)


def merge_kernel(gate_pre_ref, up_pre_ref, gate_ref, up_ref, grad_ref):
    halves = gate_pre_ref.shape[0]
    grad = dot(gate_pre_ref[0], gate_ref[0], NT) + dot(up_pre_ref[0], up_ref[0], NT)
    for half in range(1, halves):
        grad = grad + dot(gate_pre_ref[half], gate_ref[half], NT)
        grad = grad + dot(up_pre_ref[half], up_ref[half], NT)
    grad_ref[...] = grad.astype(BF16)


def expert_merge(gate_pre, up_pre, gate_all, up_all):
    halves, tokens, units = gate_pre.shape
    width = gate_all.shape[1]
    span = 256
    batch = min(tokens, 1024)
    slab = pl.BlockSpec(
        (halves, batch, units), lambda turn, step: (0, turn, 0), pipeline_mode=pl.Buffered(1)
    )
    tile = pl.BlockSpec((halves, span, units), lambda turn, step: (0, step, 0))
    return pl.pallas_call(
        merge_kernel,
        grid=(tokens // batch, width // span),
        in_specs=[slab, slab, tile, tile],
        out_specs=pl.BlockSpec((batch, span), lambda turn, step: (turn, step)),
        out_shape=jax.ShapeDtypeStruct((tokens, width), BF16),
        compiler_params=pltpu.CompilerParams(vmem_limit_bytes=VMEM_LIMIT),
        cost_estimate=pl.CostEstimate(
            flops=4 * tokens * width * units * halves,
            bytes_accessed=4 * width * units * halves,
            transcendentals=0,
        ),
    )(gate_pre, up_pre, gate_all, up_all)


def output_kernel(hidden_ref, down_ref, out_ref):
    halves = hidden_ref.shape[0]
    out = dot(hidden_ref[0], down_ref[0], NN)
    for half in range(1, halves):
        out = out + dot(hidden_ref[half], down_ref[half], NN)
    out_ref[...] = out.astype(BF16)


def expert_output(hidden, down_all):
    halves, tokens, units = hidden.shape
    width = down_all.shape[2]
    span = 256
    batch = min(tokens, 1024)
    slab = pl.BlockSpec(
        (halves, batch, units), lambda turn, step: (0, turn, 0), pipeline_mode=pl.Buffered(1)
    )
    return pl.pallas_call(
        output_kernel,
        grid=(tokens // batch, width // span),
        in_specs=[slab, pl.BlockSpec((halves, units, span), lambda turn, step: (0, 0, step))],
        out_specs=pl.BlockSpec((batch, span), lambda turn, step: (turn, step)),
        out_shape=jax.ShapeDtypeStruct((tokens, width), BF16),
        compiler_params=pltpu.CompilerParams(vmem_limit_bytes=VMEM_LIMIT),
        cost_estimate=pl.CostEstimate(
            flops=2 * tokens * width * units * halves,
            bytes_accessed=2 * width * units * halves,
            transcendentals=0,
        ),
    )(hidden, down_all)


def weights_kernel(
    span,
    rows_ref,
    upstream_ref,
    hidden_ref,
    gate_pre_ref,
    up_pre_ref,
    gate_grad_ref,
    up_grad_ref,
    down_grad_ref,
):
    def body(step, carry):
        units = pl.ds(pl.multiple_of(step * span, span), span)
        gate_grad_ref[0, :, units] = dot(rows_ref[...], gate_pre_ref[0, :, units], TN).astype(BF16)
        up_grad_ref[0, :, units] = dot(rows_ref[...], up_pre_ref[0, :, units], TN).astype(BF16)
        down_grad_ref[0, units, :] = dot(
            hidden_ref[0, :, units], upstream_ref[...], TN
        ).astype(BF16)
        return carry

    lax.fori_loop(0, gate_grad_ref.shape[2] // span, body, 0)


def expert_weights(rows, upstream, hidden, gate_pre, up_pre):
    tokens, width = rows.shape
    halves, _, units = hidden.shape

    def each(*shape):
        return pl.BlockSpec((1,) + shape, lambda half: (half,) + (0,) * len(shape))

    whole = pl.BlockSpec(memory_space=pltpu.VMEM)
    slab = each(tokens, units)
    return pl.pallas_call(
        functools.partial(weights_kernel, 256),
        grid=(halves,),
        in_specs=[whole, whole, slab, slab, slab],
        out_specs=[each(width, units), each(width, units), each(units, width)],
        out_shape=[
            jax.ShapeDtypeStruct((halves, width, units), BF16),
            jax.ShapeDtypeStruct((halves, width, units), BF16),
            jax.ShapeDtypeStruct((halves, units, width), BF16),
        ],
        compiler_params=pltpu.CompilerParams(vmem_limit_bytes=VMEM_LIMIT),
        cost_estimate=pl.CostEstimate(
            flops=6 * tokens * width * units * halves,
            bytes_accessed=6 * width * units * halves,
            transcendentals=0,
        ),
    )(rows, upstream, hidden, gate_pre, up_pre)


def per_device(
    groups,
    shards,
    wide,
    inputs,
    segment_ids,
    routes,
    cotangent,
    query_weight,
    key_weight,
    value_weight,
    output_weight,
    router_weight,
    attention_gain,
    expert_gain,
    query_gain,
    key_gain,
    gate_weight,
    up_weight,
    down_weight,
):
    micros, rows, width = inputs.shape
    deep = shards // wide
    span = shards * rows
    tokens = micros * span
    experts = router_weight.shape[1]
    column_width = width // shards
    shard_place = lax.axis_index("shard")
    layout = (groups, deep, shards // deep)

    gate_all = lax.all_gather(gate_weight, "expert", axis=0, tiled=True)
    up_all = lax.all_gather(up_weight, "expert", axis=0, tiled=True)
    down_all = lax.all_gather(down_weight, "expert", axis=0, tiled=True)

    cuts = [
        column_width * experts,
        column_width,
        column_width,
        HDIM // shards,
        HDIM // shards,
        routes.size,
    ]
    starts = [sum(cuts[:place]) for place in range(len(cuts))]
    small_own = jnp.concatenate(
        [
            router_weight.reshape(-1),
            attention_gain,
            expert_gain,
            query_gain,
            key_gain,
            routes.reshape(-1).astype(BF16),
        ]
    )
    small_own = jnp.pad(small_own, (0, -sum(cuts) % 2048)).reshape(-1, 128)
    (projections, small), (hidden_all, upstream_all) = fuse(
        [
            Columns((query_weight, key_weight, value_weight), small_own, layout),
            Chain(Gather(inputs, layout), Gather(cotangent, layout)),
        ],
        layout,
        0,
        "entry",
    )
    hidden_all = hidden_all.reshape(tokens, width)
    upstream_all = upstream_all.reshape(tokens, width)
    projections = projections.reshape(width, 3 * column_width)
    small = small.reshape(shards, -1)
    router_full, attn_gain, expert_gain_full, query_gain_full, key_gain_full, routes_all = (
        small[:, start : start + length]
        for start, length in zip(starts, cuts, strict=True)
    )
    router_full = router_full.reshape(width, experts)
    attn_gain = attn_gain.reshape(-1).astype(F32)
    expert_gain_full = expert_gain_full.reshape(-1).astype(F32)
    query_gain_full = query_gain_full.reshape(-1).astype(F32)
    key_gain_full = key_gain_full.reshape(-1).astype(F32)
    routes_all = routes_all.reshape(shards, micros, rows, -1).transpose(1, 0, 2, 3)
    routes_all = routes_all.reshape(tokens, -1).astype(jnp.int32)

    head_gains = jnp.pad(jnp.stack([query_gain_full, key_gain_full]), ((0, 6), (0, 0)))
    tables = rotary(span)
    segments = (segment_ids[:, :, None], segment_ids[:, None, :])
    mixer_all, projected, attended, middle_parts = attention_forward(
        hidden_all, projections, output_weight, attn_gain[None], head_gains, tables, segments
    )
    hidden = inputs.astype(F32)
    ((middle_total,),) = fuse(
        [Scatter(middle_parts.reshape(micros, shards, rows, width), layout)], layout, 1, "middle"
    )
    middle = hidden + middle_total

    scale_second = rms_scale(middle)
    normed_second = middle * scale_second
    expert_input = (normed_second * expert_gain_full).astype(BF16)
    ((expert_all,),) = fuse([Gather(expert_input, layout)], layout, 2, "experts_in")
    expert_all = expert_all.reshape(tokens, width)
    logits = jnp.dot(expert_all, router_full, preferred_element_type=F32)
    choose = (routes_all[:, :, None] == jnp.arange(experts, dtype=jnp.int32)).astype(F32)
    share = softmax_rows(jnp.sum(choose * logits[:, None, :], axis=-1))
    share_wide = jnp.sum(choose * share[:, :, None], axis=1)
    served = (jnp.arange(groups, dtype=jnp.int32) * shards + shard_place) // 2
    serves = (served[:, None] == jnp.arange(experts, dtype=jnp.int32)).astype(F32)
    share_own = jnp.pad(
        jnp.dot(share_wide, serves.T, precision=PRECISE), ((0, 0), (0, 128 - groups))
    )
    activated, gate_pre, up_pre, dots = expert_units(
        expert_all, upstream_all, share_own, gate_all, up_all, down_all
    )
    early = tokens <= 1024
    expert_grad_parts = expert_merge(gate_pre, up_pre, gate_all, up_all)
    if not early:
        gate_pre, expert_grad_parts = lax.optimization_barrier((gate_pre, expert_grad_parts))
        gate_terms, up_terms, down_terms = expert_weights(
            expert_all, upstream_all, activated, gate_pre, up_pre
        )
        out_parts = expert_output(activated, down_all)

    halves = groups * shards
    lanes = 2 * halves + -2 * halves % 128
    columns = jnp.arange(groups, dtype=jnp.int32) * shards + shard_place
    columns = (columns[:, None] == jnp.arange(halves, dtype=jnp.int32)).astype(F32)
    placed = jnp.dot(dots[:, :groups], columns, precision=PRECISE)
    placed_high = placed.astype(BF16)
    placed_low = (placed - placed_high.astype(F32)).astype(BF16)
    placed = jnp.pad(
        jnp.concatenate([placed_high, placed_low], axis=1), ((0, 0), (0, lanes - 2 * halves))
    )
    returned = [
        Scatter(placed.reshape(micros, shards, rows, lanes), layout),
        Scatter(expert_grad_parts.reshape(micros, shards, rows, width), layout),
    ]
    if early:
        returned.append(
            ExpertWeights(
                expert_all, upstream_all, activated, gate_pre, up_pre, down_all, layout
            )
        )
        (dot_total,), (expert_grad,), (_, up_terms, down_terms, out_parts, gate_grad) = fuse(
            returned, layout, 3, "experts_out"
        )
    else:
        returned.append(ExpertScatter(gate_terms, layout))
        (dot_total,), (expert_grad,), (gate_grad,) = fuse(returned, layout, 3, "experts_out")

    def own_rows(values):
        return lax.dynamic_slice_in_dim(
            values.reshape((micros, span) + values.shape[1:]), shard_place * rows, rows, 1
        )

    own_choose, own_share = own_rows(choose), own_rows(share)
    share_grad_wide = dot_total[..., :halves] + dot_total[..., halves : 2 * halves]
    share_grad_wide = share_grad_wide.reshape(micros, rows, experts, 2).sum(axis=-1)
    share_grad = jnp.sum(own_choose * share_grad_wide[:, :, None, :], axis=-1)
    chosen_grad = own_share * (
        share_grad - jnp.sum(own_share * share_grad, axis=-1, keepdims=True)
    )
    own_logits_grad = jnp.sum(own_choose * chosen_grad[..., None], axis=2)
    expert_grad = expert_grad + jnp.dot(
        own_logits_grad, router_full.astype(F32).T, precision=PRECISE
    )
    expert_gain_term = jnp.sum(expert_grad * normed_second, axis=(0, 1))
    middle_grad = cotangent.astype(F32) + norm_back(
        expert_grad * expert_gain_full, normed_second, scale_second
    )
    router_term = jnp.einsum(
        "mtd,mte->de", expert_input.astype(F32), own_logits_grad, precision=PRECISE
    )
    (branch_all,), (up_grad,) = fuse(
        [Gather(middle_grad.astype(BF16), layout), ExpertScatter(up_terms, layout)],
        layout,
        4,
        "branch",
    )
    branch_all = branch_all.reshape(tokens, width)

    mixer_parts, projection_terms, output_term, head_gain_terms = attention_backward(
        branch_all,
        mixer_all,
        projected,
        attended,
        projections,
        output_weight,
        head_gains,
        tables,
        segments,
    )
    (mixer_grad,), (down_grad,) = fuse(
        [
            Scatter(mixer_parts.reshape(micros, shards, rows, width), layout),
            ExpertScatter(down_terms, layout),
        ],
        layout,
        5,
        "mixer",
    )
    scale_first = rms_scale(hidden)
    normed_first = hidden * scale_first
    attn_gain_term = jnp.sum(mixer_grad * normed_first, axis=(0, 1))
    hidden_grad = middle_grad + norm_back(mixer_grad * attn_gain, normed_first, scale_first)

    part = column_width // groups
    tail = jnp.concatenate(
        [
            term.reshape(shards, -1)
            for term in (
                router_term,
                attn_gain_term,
                expert_gain_term,
                head_gain_terms[0],
                head_gain_terms[1],
            )
        ],
        axis=1,
    )
    tail = jnp.pad(tail, ((0, 0), (0, -tail.shape[1] % 1024))).reshape(shards, -1, 128)
    (outs,), (output_grad, tail, query_grad, key_grad, value_grad) = fuse(
        [
            Scatter(out_parts.reshape(micros, shards, rows, width), layout),
            Rows(
                projection_terms.reshape(shards, groups, part, 3 * column_width),
                output_term.reshape(groups, part, width),
                tail,
                layout,
            ),
        ],
        layout,
        6,
        "exit",
    )
    result = middle + outs
    tail = tail.reshape(-1)
    tails = [
        tail[start : start + length]
        for start, length in zip(starts[:5], cuts[:5], strict=True)
    ]
    return (
        result.astype(BF16),
        hidden_grad.astype(BF16),
        query_grad.astype(F32).reshape(column_width, width),
        key_grad.astype(F32).reshape(column_width, width),
        value_grad.astype(F32).reshape(column_width, width),
        output_grad.astype(F32).reshape(column_width, width),
        tails[0].reshape(column_width, experts),
        tails[1],
        tails[2],
        tails[3],
        tails[4],
        gate_grad.astype(F32)[None],
        up_grad.astype(F32)[None],
        down_grad.astype(F32)[None],
    )


def solution(mesh):
    groups, shards = mesh.shape["expert"], mesh.shape["shard"]
    wide = shards // 4 if shards % 4 == 0 else 1
    in_specs = (
        P(None, ("expert", "shard"), None),
        P(None, "expert"),
        P(None, ("expert", "shard"), None),
        P(None, ("expert", "shard"), None),
        P("shard", None),
        P("shard", None),
        P("shard", None),
        P("shard", None),
        P("shard", None),
        P("shard"),
        P("shard"),
        P("shard"),
        P("shard"),
        P(("expert", "shard"), None, None),
        P(("expert", "shard"), None, None),
        P(("expert", "shard"), None, None),
    )
    out_specs = (
        P(None, ("expert", "shard"), None),
        P(None, ("expert", "shard"), None),
        P("shard", None),
        P("shard", None),
        P("shard", None),
        P("shard", None),
        P("shard", None),
        P("shard"),
        P("shard"),
        P("shard"),
        P("shard"),
        P(("expert", "shard"), None, None),
        P(("expert", "shard"), None, None),
        P(("expert", "shard"), None, None),
    )
    return jax.shard_map(
        functools.partial(per_device, groups, shards, wide),
        mesh=mesh,
        in_specs=in_specs,
        out_specs=out_specs,
        check_vma=False,
    )
```

```python
import functools
import math

import jax
import jax.numpy as jnp
from jax import lax
from jax.experimental import pallas as pl
from jax.experimental.pallas import tpu as pltpu
from jax.sharding import PartitionSpec as P

HDIM = 128
EPSILON = 1e-05
ROPE_BASE = 10000.0
MASK_FILL = -1e30
PRECISE = lax.Precision.HIGHEST
MESH = pl.DeviceIdType.MESH
F32 = jnp.float32
BF16 = jnp.bfloat16
NN = (((1,), (0,)), ((), ()))
NT = (((1,), (1,)), ((), ()))
TN = (((0,), (0,)), ((), ()))
VMEM_LIMIT = 63 << 20
LINK_COST = pl.CostEstimate(flops=60 * 10**9, bytes_accessed=8 << 20, transcendentals=0)


def dot(left, right, dims):
    return lax.dot_general(left, right, dims, preferred_element_type=F32)


def rms_scale(values):
    return lax.rsqrt(jnp.mean(values * values, axis=-1, keepdims=True) + EPSILON)


def norm_back(normed_grad, normed, inv_scale):
    return inv_scale * (
        normed_grad - normed * jnp.mean(normed_grad * normed, axis=-1, keepdims=True)
    )


def rotary(span):
    steps = jnp.arange(HDIM // 2, dtype=jnp.int32).astype(F32)
    freqs = jnp.power(ROPE_BASE, -2.0 * steps / HDIM)
    theta = jnp.arange(span, dtype=jnp.int32).astype(F32)[:, None] * freqs[None, :]
    cosine, sine = jnp.cos(theta), jnp.sin(theta)
    return (
        jnp.concatenate([cosine, cosine], axis=1),
        jnp.concatenate([-sine, sine], axis=1),
    )


def softmax_rows(scores):
    row_peak = jnp.max(scores, axis=-1, keepdims=True)
    exponent = jnp.exp(scores - row_peak)
    return exponent / jnp.sum(exponent, axis=-1, keepdims=True)


class Place:
    def __init__(self, groups, deep, wide):
        self.deep, self.wide = deep, wide
        self.shards, self.groups, self.layers = deep * wide, groups, groups // 2
        group, me = lax.axis_index("expert"), lax.axis_index("shard")
        self.group, self.me = group, me
        self.layer, self.core = group // 2, lax.rem(group, 2)
        self.row, self.column = me // wide, lax.rem(me, wide)

    def peer(self, layer_step=0, core_step=0, row_step=0, column_step=0):
        group, me = self.group, self.me
        if layer_step or core_step:
            group = lax.rem(self.layer + layer_step, self.layers) * 2 + (
                1 - self.core if core_step else self.core
            )
        if row_step or column_step:
            me = lax.rem(self.row + row_step, self.deep) * self.wide + lax.rem(
                self.column + column_step, self.wide
            )
        return group, me

    def grid_place(self, row_step, column_step):
        return self.peer(0, 0, row_step, column_step)[1]

    def back(self, layer_step=0, core_step=0, row_step=0, column_step=0):
        return self.peer(
            (self.layers - layer_step) % self.layers,
            core_step,
            (self.deep - row_step) % self.deep,
            (self.wide - column_step) % self.wide,
        )


def send_to(peer, source, target, send_sem, recv_sem):
    return pltpu.make_async_remote_copy(
        src_ref=source,
        dst_ref=target,
        send_sem=send_sem,
        recv_sem=recv_sem,
        device_id=peer,
        device_id_type=MESH,
    )


def dma(*shape):
    return pltpu.SemaphoreType.DMA(tuple(max(1, size) for size in shape))


ANYWHERE = pl.BlockSpec(memory_space=pl.ANY)
RESIDENT = pl.BlockSpec(memory_space=pltpu.VMEM)


def grid_steps(deep, wide):
    steps = {(0, 0, row, 0) for row in range(1, deep)}
    return steps | {(0, 0, 0, column) for column in range(1, wide)}


def shard_steps(deep, wide):
    return {
        (0, 0, row, column) for row in range(deep) for column in range(wide) if row or column
    }


def expert_steps(layers):
    return {(step, 0, 0, 0) for step in range(1, layers)} | {(0, 1, 0, 0)}


def fuse(parts, layout, collective_id, name):
    groups, deep, wide = layout
    operands = [operand for part in parts for operand in part.operands]
    in_specs = [spec for part in parts for spec in part.in_specs]
    out_shape = [out for part in parts for out in part.outs]
    out_specs = [spec for part in parts for spec in part.out_specs]
    scratch = [buffer for part in parts for buffer in part.scratch]
    steps = sorted(set().union(*(part.steps for part in parts)))

    def kernel(*refs):
        place = Place(groups, deep, wide)
        barrier = pltpu.get_barrier_semaphore()
        for step in steps:
            pl.semaphore_signal(
                barrier, inc=1, device_id=place.peer(*step), device_id_type=MESH
            )
        pl.semaphore_wait(barrier, len(steps))
        ins = list(refs[: len(operands)])
        outs = list(refs[len(operands) : len(operands) + len(out_shape)])
        buffers = list(refs[len(operands) + len(out_shape) :])
        running = []
        for part in parts:
            part_ins = [ins.pop(0) for _ in part.operands]
            part_outs = [outs.pop(0) for _ in part.outs]
            part_buffers = [buffers.pop(0) for _ in part.scratch]
            running.append(part.run(place, *part_ins, *part_outs, *part_buffers))
        late = [
            run for run, part in zip(running, parts, strict=True) if isinstance(part, ExpertScatter)
        ]
        first = [run for run in running if run not in late]
        for run in late:
            next(run)
        for index, _ in enumerate(together(*first)):
            if index in (1, 2):
                for run in late:
                    next(run)
        for run in late:
            for _ in run:
                pass

    results = pl.pallas_call(
        kernel,
        out_shape=out_shape,
        in_specs=in_specs,
        out_specs=out_specs,
        scratch_shapes=scratch,
        compiler_params=pltpu.CompilerParams(
            collective_id=collective_id, has_side_effects=True, vmem_limit_bytes=VMEM_LIMIT
        ),
        cost_estimate=LINK_COST,
        name=name,
    )(*operands)
    results = list(results)
    return [[results.pop(0) for _ in part.outs] for part in parts]


END = object()


def together(*runs):
    runs = list(runs)
    while runs:
        for run in list(runs):
            if next(run, END) is END:
                runs.remove(run)
        yield


def until(run, token):
    for value in run:
        if value == token:
            return
        yield


def gather_scratch(pieces, deep, wide):
    return [
        dma(pieces, 2, deep - 1),
        dma(pieces, 2, deep - 1),
        dma(pieces, 2 * deep, wide - 1),
        dma(pieces, 2 * deep, wide - 1),
        dma(1),
    ]


def start_all(copies):
    for copy in copies:
        copy.start()


def end_all(copies):
    for copy in copies:
        copy.wait_send()


def gather_steps(place, own, whole, row_send, row_recv, col_send, col_recv, local):
    pieces, rows, _ = own.shape
    deep, wide, shards = place.deep, place.wide, place.shards
    row, column = place.row, place.column
    ends = []

    def slot(piece, source_row, source_column):
        source = piece * shards + source_row * wide + source_column
        return whole.at[pl.ds(pl.multiple_of(source * rows, rows), rows)]

    def known(piece, step, source_row):
        return slot(piece, source_row, column) if step else own.at[piece]

    def hop(piece, way, step, source_row):
        return send_to(
            (place.group, (row + 1 - 2 * way) * wide + column),
            known(piece, step, source_row),
            slot(piece, source_row, column),
            row_send.at[piece, way, step],
            row_recv.at[piece, way, step],
        )

    def across(piece, step, way, move, source_row, source_column):
        key = 2 * step - 1 + way if step else 0
        return send_to(
            place.peer(0, 0, 0, move),
            known(piece, step, source_row),
            slot(piece, source_row, source_column),
            col_send.at[piece, key, move - 1],
            col_recv.at[piece, key, move - 1],
        )

    def start_if(condition, copies):
        pl.when(condition)(functools.partial(start_all, copies))
        ends.append((condition, copies))

    def forward(piece, step, way, condition, source_row):
        start_if(
            condition,
            [across(piece, step, way, move, source_row, column) for move in range(1, wide)],
        )

    def begin(piece):
        start_if(row < deep - 1, [hop(piece, 0, 0, row)])
        start_if(row > 0, [hop(piece, 1, 0, row)])
        forward(piece, 0, 0, row >= 0, row)

    here = [
        pltpu.make_async_copy(own.at[piece], slot(piece, row, column), local.at[0])
        for piece in range(pieces)
    ]
    begin(0)
    for copy in here:
        copy.start()
    yield 0
    for piece in range(pieces):
        sources = []
        for step in range(1, deep):
            for way in (0, 1):
                source_row = row - step if way == 0 else row + step
                there = source_row >= 0 if way == 0 else source_row < deep
                onward = row < deep - 1 if way == 0 else row > 0
                pl.when(there)(hop(piece, way, step - 1, source_row).wait_recv)
                if step < deep - 1:
                    start_if(there & onward, [hop(piece, way, step, source_row)])
                forward(piece, step, way, there, source_row)
                sources.append((step, way, there, source_row))
            if step == 1 and piece + 1 < pieces:
                begin(piece + 1)
            yield 0
        for step, way, there, source_row in [(0, 0, row >= 0, row)] + sources:
            for move in range(1, wide):
                source_column = lax.rem(column + wide - move, wide)
                copy = across(piece, step, way, move, source_row, source_column)
                pl.when(there)(copy.wait_recv)
            if way or not step:
                yield 0
        if piece == 0:
            for copy in here:
                copy.wait()
        yield piece + 1
    for condition, copies in ends:
        pl.when(condition)(functools.partial(end_all, copies))


class Gather:
    def __init__(self, own, layout):
        _, deep, wide = layout
        pieces, rows, width = own.shape
        self.operands, self.in_specs = [own], [ANYWHERE]
        self.outs = [jax.ShapeDtypeStruct((pieces * deep * wide * rows, width), own.dtype)]
        self.out_specs = [ANYWHERE]
        self.scratch = gather_scratch(pieces, deep, wide)
        self.steps = grid_steps(deep, wide)
        self.run = gather_steps


def scatter_scratch(rows, width, deep, wide):
    return [
        pltpu.VMEM((deep, max(1, wide - 1), rows, width), BF16),
        pltpu.VMEM((deep + 1, rows, width), BF16),
        dma(2 * deep, wide - 1),
        dma(2 * deep, wide - 1),
        dma(2 * deep),
        dma(2 * deep),
    ]


def scatter_steps(
    place, parts, piece, total, landed, summed, col_send, col_recv, row_send, row_recv
):
    deep, wide, shards = place.deep, place.wide, place.shards
    row, column = place.row, place.column
    rows = total.shape[0]
    ends = []

    def block(target_row, target_column):
        target = piece * shards + target_row * wide + target_column
        return pl.ds(pl.multiple_of(target * rows, rows), rows)

    def along_row(key, target_row, move):
        target_column = lax.rem(column + move, wide)
        return send_to(
            place.peer(0, 0, 0, move),
            parts.at[block(target_row, target_column)],
            landed.at[target_row, move - 1],
            col_send.at[key, move - 1],
            col_recv.at[key, move - 1],
        )

    def hop(key, step, way, target_row):
        return send_to(
            (place.group, (row + 1 - 2 * way) * wide + column),
            landed.at[target_row, 0],
            summed.at[deep if step == 1 and way else target_row],
            row_send.at[key],
            row_recv.at[key],
        )

    order = []
    for step in range(deep - 1, 0, -1):
        for way in (0, 1):
            target_row = row - step if way else row + step
            there = target_row >= 0 if way else target_row < deep
            order.append((2 * step + way, step, way, target_row, there))
    order.append((0, 0, 0, row, row >= 0))

    def send_row(index):
        key, _, _, target_row, there = order[index]
        copies = [along_row(key, target_row, move) for move in range(1, wide)]
        pl.when(there)(functools.partial(start_all, copies))
        ends.append((there, copies))

    def fold(index):
        key, step, way, target_row, there = order[index]

        def body():
            for move in range(1, wide):
                along_row(key, target_row, move).wait_recv()
            value = parts[block(target_row, column), :].astype(F32)
            for move in range(1, wide):
                value = value + landed[target_row, move - 1].astype(F32)
            if step:
                landed[target_row, 0] = value.astype(BF16)
            else:
                total[...] = value

        pl.when(there)(body)

    def join(index):
        key, step, way, target_row, there = order[index]
        behind = row < deep - 1 if way else row > 0

        def body():
            hop(key + 2, step + 1, way, target_row).wait_recv()
            landed[target_row, 0] = (
                landed[target_row, 0].astype(F32) + summed[target_row].astype(F32)
            ).astype(BF16)

        if step < deep - 1:
            pl.when(there & behind)(body)
        copy = hop(key, step, way, target_row)
        pl.when(there)(copy.start)
        ends.append((there, [copy]))

    def finish(way):
        def body():
            hop(2 + way, 1, way, row).wait_recv()
            total[...] = total[...] + summed[deep if way else row].astype(F32)

        pl.when(row < deep - 1 if way else row > 0)(body)

    ahead = 4
    for index in range(min(ahead, len(order))):
        send_row(index)
    yield
    for index in range(len(order)):
        fold(index)
        if index + ahead < len(order):
            send_row(index + ahead)
        if index < len(order) - 1:
            join(index)
        if index % 2:
            yield
    yield
    for way in (0, 1):
        finish(way)
        yield
    for there, copies in ends:
        pl.when(there)(functools.partial(end_all, copies))


def scatter_pieces(runs, deep):
    running = []
    for run in runs:
        running.append(run)
        for _ in range(deep + 1):
            for each in list(running):
                if next(each, END) is END:
                    running.remove(each)
            yield
    yield from together(*running)


class Scatter:
    def __init__(self, parts, pieces, layout):
        _, deep, wide = layout
        tokens, width = parts.shape
        rows = tokens // (pieces * deep * wide)
        self.pieces = pieces
        self.operands, self.in_specs = [parts], [RESIDENT]
        self.outs = [jax.ShapeDtypeStruct((pieces, rows, width), F32)]
        self.out_specs = [RESIDENT]
        self.scratch = scatter_scratch(rows, width, deep, wide) * pieces
        self.steps = grid_steps(deep, wide)

    def run(self, place, parts, total, *scratch):
        each = len(scratch) // self.pieces
        runs = [
            scatter_steps(
                place,
                parts,
                piece,
                total.at[piece],
                *scratch[piece * each : (piece + 1) * each],
            )
            for piece in range(self.pieces)
        ]
        yield from scatter_pieces(runs, place.deep)


class Chain:
    def __init__(self, *parts):
        self.parts = parts
        for name in ("operands", "in_specs", "outs", "out_specs", "scratch"):
            setattr(self, name, [item for part in parts for item in getattr(part, name)])
        self.steps = set().union(*(part.steps for part in parts))

    def run(self, place, *refs):
        refs = list(refs)
        taken = [[] for _ in self.parts]
        for name in ("operands", "outs", "scratch"):
            for part, own in zip(self.parts, taken, strict=True):
                own.extend(refs.pop(0) for _ in getattr(part, name))
        for part, own in zip(self.parts, taken, strict=True):
            yield from part.run(place, *own)


class ExpertScatter:
    def __init__(self, terms, layout, chunks=2):
        groups = layout[0]
        layers = groups // 2
        _, rows, width = terms.shape
        part = rows // chunks
        self.operands, self.in_specs = [terms], [ANYWHERE]
        self.outs = [jax.ShapeDtypeStruct((rows, width), BF16)]
        self.out_specs = [RESIDENT]
        self.scratch = [
            pltpu.VMEM((chunks, layers, part, width), BF16),
            pltpu.VMEM((chunks, layers, part, width), BF16),
            pltpu.VMEM((chunks, max(1, layers - 1), part, width), BF16),
            dma(chunks, layers),
            dma(chunks, layers),
            dma(chunks, layers),
            dma(chunks, layers - 1),
            dma(chunks, layers - 1),
        ]
        self.steps = expert_steps(layers)

    def run(
        self,
        place,
        terms,
        total,
        mine,
        landed,
        summed,
        local,
        core_send,
        core_recv,
        layer_send,
        layer_recv,
    ):
        chunks, layers, part, _ = mine.shape
        span = min(part, 128)
        sends = []

        def entry(turn, core):
            return lax.rem(place.layer + turn, layers) * 2 + core

        def block(chunk, turn, core):
            return terms.at[entry(turn, core), pl.ds(chunk * part, part)]

        def load(chunk, turn):
            return pltpu.make_async_copy(
                block(chunk, turn, place.core), mine.at[chunk, turn], local.at[chunk, turn]
            )

        def across(chunk, turn):
            return send_to(
                place.peer(0, 1, 0, 0),
                block(chunk, turn, 1 - place.core),
                landed.at[chunk, turn],
                core_send.at[chunk, turn],
                core_recv.at[chunk, turn],
            )

        def along(chunk, turn):
            return send_to(
                place.peer(turn, 0, 0, 0),
                mine.at[chunk, turn],
                summed.at[chunk, turn - 1],
                layer_send.at[chunk, turn - 1],
                layer_recv.at[chunk, turn - 1],
            )

        order = [*range(1, layers), 0]
        for chunk in range(chunks):
            for turn in order:
                load(chunk, turn).start()
                sends.append(across(chunk, turn))
                sends[-1].start()
        yield
        for chunk in range(chunks):
            for turn in order[:-1]:
                load(chunk, turn).wait()
                across(chunk, turn).wait_recv()

                def merge(step, carry, chunk=chunk, turn=turn):
                    rows = pl.ds(pl.multiple_of(step * span, span), span)
                    value = mine[chunk, turn, rows].astype(F32)
                    value = value + landed[chunk, turn, rows].astype(F32)
                    mine[chunk, turn, rows] = value.astype(BF16)
                    return carry

                lax.fori_loop(0, part // span, merge, 0)
                sends.append(along(chunk, turn))
                sends[-1].start()
                yield
        for chunk in range(chunks):
            load(chunk, 0).wait()
            across(chunk, 0).wait_recv()
            for turn in order[:-1]:
                along(chunk, turn).wait_recv()

            def finish(step, carry, chunk=chunk):
                rows = pl.ds(pl.multiple_of(step * span, span), span)
                here = pl.ds(pl.multiple_of(chunk * part + step * span, span), span)
                value = mine[chunk, 0, rows].astype(F32) + landed[chunk, 0, rows].astype(F32)
                for turn in order[:-1]:
                    value = value + summed[chunk, turn - 1, rows].astype(F32)
                total[here] = value.astype(BF16)
                return carry

            lax.fori_loop(0, part // span, finish, 0)
            yield
        for copy in sends:
            copy.wait_send()


class Experts:
    SPAN = 256

    def __init__(self, own, upstream, mask, router, gate_all, up_all, down_all, layout):
        _, deep, wide = layout
        pieces, rows, width = own.shape
        halves, _, units = gate_all.shape
        tokens, lanes = mask.shape
        self.operands = [own, upstream, mask, router, gate_all, up_all, down_all]
        self.in_specs = [ANYWHERE, ANYWHERE, RESIDENT, RESIDENT] + [ANYWHERE] * 3
        self.outs = [
            jax.ShapeDtypeStruct((halves, width, units), BF16),
            jax.ShapeDtypeStruct((halves, width, units), BF16),
            jax.ShapeDtypeStruct((halves, units, width), BF16),
            jax.ShapeDtypeStruct((tokens, width), BF16),
            jax.ShapeDtypeStruct((tokens, lanes), F32),
            jax.ShapeDtypeStruct((pieces, rows, width), F32),
            jax.ShapeDtypeStruct((pieces, rows, lanes), F32),
        ]
        self.out_specs = [ANYWHERE] * 4 + [RESIDENT] * 3
        gathers = gather_scratch(pieces, deep, wide)
        scatters = scatter_scratch(rows, width, deep, wide)
        dots = scatter_scratch(rows, lanes, deep, wide)
        self.sizes = [len(gathers), len(scatters)]
        acts = pltpu.VMEM((halves, tokens, units), BF16)
        self.scratch = [
            pltpu.VMEM((tokens, width), BF16),
            pltpu.VMEM((tokens, width), BF16),
            acts,
            acts,
            acts,
            pltpu.VMEM((halves, width, units), BF16),
            pltpu.VMEM((halves, width, units), BF16),
            pltpu.VMEM((halves, units, width), BF16),
            pltpu.VMEM((tokens, width), BF16),
            pltpu.VMEM((tokens, lanes), F32),
            pltpu.VMEM((tokens, lanes), BF16),
            dma(3, halves),
            dma(3, halves),
            dma(2),
            *gathers,
            *scatters * pieces,
            *dots * pieces,
        ]
        self.steps = grid_steps(deep, wide)

    def run(
        self,
        place,
        own,
        upstream_in,
        mask,
        router,
        gate_all,
        up_all,
        down_all,
        gate_terms,
        up_terms,
        down_terms,
        out,
        share,
        total,
        dot_total,
        rows,
        upstream,
        hidden,
        gate_pre,
        up_pre,
        gate_weight,
        up_weight,
        down_weight,
        parts,
        dots,
        placed,
        load_sem,
        store_sem,
        local_sem,
        *scratch,
    ):
        pieces = own.shape[0]
        halves, _, units = hidden.shape
        tokens, width = rows.shape
        lanes = mask.shape[1]
        count = tokens // pieces
        span = self.SPAN
        shards = place.shards
        scratch = list(scratch)

        def take(number):
            return [scratch.pop(0) for _ in range(number)]

        inward = gather_steps(place, own, rows, *take(self.sizes[0]))
        scatters = [
            scatter_steps(place, parts, piece, total.at[piece], *take(self.sizes[1]))
            for piece in range(pieces)
        ]
        dot_scatters = [
            scatter_steps(place, placed, piece, dot_total.at[piece], *take(self.sizes[1]))
            for piece in range(pieces)
        ]
        running = []

        def others():
            for each in list(running):
                if next(each, END) is END:
                    running.remove(each)

        kept = (gate_weight, up_weight, down_weight)

        def load(half):
            return [
                pltpu.make_async_copy(source.at[half], kept[which].at[half], load_sem.at[which, half])
                for which, source in enumerate((gate_all, up_all, down_all))
            ]

        def store(which, half):
            target = (gate_terms, up_terms, down_terms)[which]
            return pltpu.make_async_copy(
                kept[which].at[half], target.at[half], store_sem.at[which, half]
            )

        def wait_all(copies):
            for copy in copies:
                copy.wait()

        def shares(piece):
            here = pl.ds(piece * count, count)
            known = mask[here, :]
            logits = dot(rows[here, :], router[...], NN)
            peak = jnp.max(jnp.where(known > 0, logits, MASK_FILL), axis=1, keepdims=True)
            exponent = jnp.where(known > 0, jnp.exp(jnp.minimum(logits - peak, 0.0)), 0.0)
            share[here, :] = exponent / jnp.sum(exponent, axis=1, keepdims=True)

        def units_of(piece):
            here = pl.ds(piece * count, count)
            which_lane = lax.broadcasted_iota(jnp.int32, (count, lanes), 1)
            for half in range(halves):
                if piece == 0:
                    wait_all(load(half))
                column = half * shards + place.me
                chosen = jnp.where(which_lane == column // 2, share[here, :], 0.0)
                weight = jnp.sum(chosen, axis=1, keepdims=True)
                for step in range(units // span):
                    there = pl.ds(step * span, span)
                    gate = dot(rows[here, :], gate_weight[half, :, there], NN)
                    up = dot(rows[here, :], up_weight[half, :, there], NN)
                    grad = dot(upstream[here, :], down_weight[half, there, :], NT)
                    sigmoid_gate = 1.0 / (1.0 + jnp.exp(-gate))
                    swish_gate = gate * sigmoid_gate
                    activated = swish_gate * up
                    products = jnp.sum(activated * grad, axis=1, keepdims=True)
                    dots[here, :] += jnp.where(which_lane == column, products, 0.0)
                    hidden[half, here, there] = (activated * weight).astype(BF16)
                    grad = grad * weight
                    gate_pre[half, here, there] = (
                        grad * up * (sigmoid_gate * (1.0 + gate * (1.0 - sigmoid_gate)))
                    ).astype(BF16)
                    up_pre[half, here, there] = (grad * swish_gate).astype(BF16)
                    yield

        def merge(piece):
            here = pl.ds(piece * count, count)
            for step in range(width // span):
                there = pl.ds(step * span, span)
                value = dot(gate_pre[0, here, :], gate_weight[0, there, :], NT)
                value = value + dot(up_pre[0, here, :], up_weight[0, there, :], NT)
                for half in range(1, halves):
                    value = value + dot(gate_pre[half, here, :], gate_weight[half, there, :], NT)
                    value = value + dot(up_pre[half, here, :], up_weight[half, there, :], NT)
                parts[here, there] = value.astype(BF16)
                yield

        def place_dots(piece):
            here = pl.ds(piece * count, count)
            value = dots[here, :]
            high = value.astype(BF16).astype(F32)
            low = pltpu.roll(value - high, lanes // 2, 1)
            placed[here, :] = (high + low).astype(BF16)

        def weights():
            ends = []

            def put(copy):
                copy.start()
                ends.append(copy)

            for which, grads in enumerate((gate_pre, up_pre)):
                for half in range(halves):
                    for step in range(units // span):
                        there = pl.ds(step * span, span)
                        kept[which][half, :, there] = dot(
                            rows[...], grads[half, :, there], TN
                        ).astype(BF16)
                        yield
                    put(store(which, half))
            for step in range(width // span):
                there = pl.ds(step * span, span)
                value = dot(hidden[0], down_weight[0, :, there], NN)
                for half in range(1, halves):
                    value = value + dot(hidden[half], down_weight[half, :, there], NN)
                rows[:, there] = value.astype(BF16)
                yield
            put(pltpu.make_async_copy(rows, out, local_sem.at[1]))
            for half in range(halves):
                for step in range(units // span):
                    there = pl.ds(step * span, span)
                    down_weight[half, there, :] = dot(
                        hidden[half, :, there], upstream[...], TN
                    ).astype(BF16)
                    yield
                put(store(2, half))
            wait_all(ends)

        next(inward)
        upstream_copy = pltpu.make_async_copy(upstream_in, upstream, local_sem.at[0])
        upstream_copy.start()
        for half in range(halves):
            start_all(load(half))
        dots[...] = jnp.zeros_like(dots)
        yield from until(inward, 1)
        upstream_copy.wait()
        running.append(inward)
        for piece in range(pieces):
            if piece:
                while inward in running:
                    others()
                    yield
            shares(piece)
            for index, _ in enumerate(units_of(piece)):
                if piece == 0 or index % 2:
                    others()
                yield
            place_dots(piece)
            running.append(dot_scatters[piece])
            next(dot_scatters[piece])
            for index, _ in enumerate(merge(piece)):
                if piece == 0 or index % 4 == 3:
                    others()
                yield
            running.append(scatters[piece])
            next(scatters[piece])
        for index, _ in enumerate(weights()):
            if index % 4 == 3:
                others()
                yield
        yield from together(*running)


class Columns:
    def __init__(self, weights, smalls, layout):
        groups, deep, wide = layout
        shards = deep * wide
        depth = weights[0].shape[0]
        self.operands, self.in_specs = [*weights, *smalls], [ANYWHERE] * 5
        self.outs = [
            jax.ShapeDtypeStruct((shards, groups, depth // groups, 3 * depth), BF16),
            *[jax.ShapeDtypeStruct((shards,) + small.shape, BF16) for small in smalls],
        ]
        self.out_specs = [ANYWHERE] * 3
        self.scratch = [
            dma(3, shards - 1),
            dma(3, shards - 1),
            dma(2, shards - 1),
            dma(2, shards - 1),
            dma(groups // 2 - 1),
            dma(groups // 2 - 1),
            dma(groups // 2),
            dma(groups // 2),
            dma(5),
        ]
        self.steps = shard_steps(deep, wide) | expert_steps(groups // 2)

    def run(
        self,
        place,
        query_weight,
        key_weight,
        value_weight,
        small,
        gains,
        projections,
        small_all,
        gains_all,
        weight_send,
        weight_recv,
        small_send,
        small_recv,
        layer_send,
        layer_recv,
        core_send,
        core_recv,
        local,
    ):
        weights = (query_weight, key_weight, value_weight)
        smalls = ((small, small_all), (gains, gains_all))
        layers, group, me = place.layers, place.group, place.me
        part = projections.shape[2]
        depth = query_weight.shape[0]
        steps = sorted(shard_steps(place.deep, place.wide))
        sends = []

        def block(which, target):
            return weights[which].at[
                pl.ds(pl.multiple_of(group * part, part), part),
                pl.ds(pl.multiple_of(target * depth, depth), depth),
            ]

        def slot(which, source):
            return projections.at[source, group, :, pl.ds(which * depth, depth)]

        def weight_copy(which, index):
            return send_to(
                place.peer(*steps[index]),
                block(which, place.peer(*steps[index])[1]),
                slot(which, me),
                weight_send.at[which, index],
                weight_recv.at[which, index],
            )

        def small_copy(which, index):
            return send_to(
                place.peer(*steps[index]),
                smalls[which][0],
                smalls[which][1].at[me],
                small_send.at[which, index],
                small_recv.at[which, index],
            )

        def slab_copy(peer, layer, core, send_sem, recv_sem):
            slab = projections.at[:, layer * 2 + core]
            return send_to(peer, slab, slab, send_sem, recv_sem)

        def layer_copy(step, layer):
            return slab_copy(
                place.peer(step, 0, 0, 0),
                layer,
                place.core,
                layer_send.at[step - 1],
                layer_recv.at[step - 1],
            )

        def core_copy(step, layer, core):
            return slab_copy(
                place.peer(0, 1, 0, 0), layer, core, core_send.at[step], core_recv.at[step]
            )

        here = [
            pltpu.make_async_copy(block(which, me), slot(which, me), local.at[which])
            for which in range(3)
        ]
        for which, (own, whole) in enumerate(smalls):
            here.append(pltpu.make_async_copy(own, whole.at[me], local.at[3 + which]))
        for copy in here:
            copy.start()
        for index in range(len(steps)):
            for which in range(3):
                sends.append(weight_copy(which, index))
                sends[-1].start()
            for which in (0, 1):
                sends.append(small_copy(which, index))
                sends[-1].start()
        yield
        for copy in here:
            copy.wait()
        for index in range(len(steps)):
            for which in range(3):
                weight_copy(which, index).wait_recv()
        for step in range(1, layers):
            sends.append(layer_copy(step, place.layer))
            sends[-1].start()
        sends.append(core_copy(0, place.layer, place.core))
        sends[-1].start()
        yield
        for step in range(1, layers):
            layer = lax.rem(place.layer + layers - step, layers)
            layer_copy(step, layer).wait_recv()
            sends.append(core_copy(step, layer, place.core))
            sends[-1].start()
            yield
        for step in range(layers):
            layer = lax.rem(place.layer + layers - step, layers)
            core_copy(step, layer, 1 - place.core).wait_recv()
            yield
        for index in range(len(steps)):
            for which in (0, 1):
                small_copy(which, index).wait_recv()
        for copy in sends:
            copy.wait_send()


class Rows:
    def __init__(self, terms, row_terms, tail, layout):
        groups, deep, wide = layout
        layers = groups // 2
        shards, _, part, width = terms.shape
        depth = row_terms.shape[2]
        self.operands = [terms, row_terms, tail]
        self.in_specs = [RESIDENT] * 3
        self.outs = [
            jax.ShapeDtypeStruct((groups, part, depth), BF16),
            jax.ShapeDtypeStruct(tail.shape[1:], F32),
            *[jax.ShapeDtypeStruct((groups, part, depth), BF16)] * 3,
        ]
        self.out_specs = [RESIDENT] * 5
        others = max(1, layers - 1)
        self.scratch = [
            pltpu.VMEM((groups, shards, part, width), BF16),
            pltpu.VMEM((layers, shards, part, width), BF16),
            pltpu.VMEM((others, shards, part, width), BF16),
            pltpu.VMEM((others, shards, part, width), BF16),
            pltpu.VMEM((shards, part, width), BF16),
            pltpu.VMEM((layers, part, depth), BF16),
            pltpu.VMEM((others, part, depth), BF16),
            pltpu.VMEM((others, part, depth), BF16),
            pltpu.VMEM(tail.shape, F32),
            pltpu.VMEM((groups,) + tail.shape[1:], F32),
            dma(2, layers),
            dma(2, layers),
            dma(2, others),
            dma(2, others),
            dma(shards - 1),
            dma(shards - 1),
            dma(2, others),
            dma(2, others),
            dma(2, layers),
            dma(2, layers),
            dma(shards - 1),
            dma(shards - 1),
            dma(groups - 1),
            dma(groups - 1),
        ]
        self.steps = shard_steps(deep, wide) | expert_steps(layers)
        self.steps |= {(layer, core, 0, 0) for layer in range(layers) for core in (0, 1)}
        self.steps -= {(0, 0, 0, 0)}

    def run(
        self,
        place,
        terms,
        row_terms,
        tail,
        whole_rows,
        tail_out,
        query_out,
        key_out,
        value_out,
        whole,
        landed,
        merged,
        summed,
        ready,
        landed_rows,
        merged_rows,
        summed_rows,
        tails,
        tail_sums,
        core_send,
        core_recv,
        layer_send,
        layer_recv,
        swap_send,
        swap_recv,
        out_send,
        out_recv,
        over_send,
        over_recv,
        tail_send,
        tail_recv,
        sum_send,
        sum_recv,
    ):
        layers, group, me, core = place.layers, place.group, place.me, place.core
        shards = place.shards
        steps = sorted(shard_steps(place.deep, place.wide))
        group_steps = [
            (layer, flip, 0, 0) for layer in range(layers) for flip in (0, 1) if layer or flip
        ]
        sends = []

        def start(copy):
            copy.start()
            sends.append(copy)

        def layer_at(turn):
            return lax.rem(place.layer + turn, layers)

        def tail_copy(index):
            peer = place.peer(*steps[index])
            return send_to(
                peer, tail.at[peer[1]], tails.at[me], tail_send.at[index], tail_recv.at[index]
            )

        def sum_copy(index):
            return send_to(
                place.peer(*group_steps[index]),
                tail_sums.at[group],
                tail_sums.at[group],
                sum_send.at[index],
                sum_recv.at[index],
            )

        def across(which, turn):
            entry = layer_at(turn) * 2 + 1 - core
            source = row_terms.at[entry] if which else terms.at[:, entry]
            target = landed_rows.at[turn] if which else landed.at[turn]
            return send_to(
                place.peer(0, 1, 0, 0),
                source,
                target,
                core_send.at[which, turn],
                core_recv.at[which, turn],
            )

        def along(which, turn):
            source = merged_rows.at[turn - 1] if which else merged.at[turn - 1]
            target = summed_rows.at[turn - 1] if which else summed.at[turn - 1]
            return send_to(
                place.peer(turn, 0, 0, 0),
                source,
                target,
                layer_send.at[which, turn - 1],
                layer_recv.at[which, turn - 1],
            )

        def swap(index):
            peer = place.peer(*steps[index])
            return send_to(
                peer,
                ready.at[peer[1]],
                whole.at[group, me],
                swap_send.at[index],
                swap_recv.at[index],
            )

        def out(which, turn, entry):
            slab = whole_rows.at[entry] if which else whole.at[entry]
            return send_to(
                place.peer(turn, 0, 0, 0),
                slab,
                slab,
                out_send.at[which, turn - 1],
                out_recv.at[which, turn - 1],
            )

        def over(which, turn, entry):
            slab = whole_rows.at[entry] if which else whole.at[entry]
            return send_to(
                place.peer(0, 1, 0, 0),
                slab,
                slab,
                over_send.at[which, turn],
                over_recv.at[which, turn],
            )

        order = [*range(1, layers), 0]
        for which in (0, 1):
            for turn in order:
                start(across(which, turn))
        for index in range(len(steps)):
            start(tail_copy(index))
        yield
        for which in (0, 1):
            for turn in order[:-1]:
                across(which, turn).wait_recv()
                entry = layer_at(turn) * 2 + core
                if which:
                    merged_rows[turn - 1] = (
                        row_terms[entry].astype(F32) + landed_rows[turn].astype(F32)
                    ).astype(BF16)
                else:
                    for shard in range(shards):
                        merged[turn - 1, shard] = (
                            terms[shard, entry].astype(F32) + landed[turn, shard].astype(F32)
                        ).astype(BF16)
                start(along(which, turn))
                yield
        for which in (0, 1):
            across(which, 0).wait_recv()
        for index in range(len(steps)):
            tail_copy(index).wait_recv()
        tails[me] = tail[me]
        tail_sum = tails[0]
        for shard in range(1, shards):
            tail_sum = tail_sum + tails[shard]
        tail_sums[group] = tail_sum
        for index in range(len(group_steps)):
            start(sum_copy(index))
        yield
        for turn in order[:-1]:
            along(0, turn).wait_recv()
        for shard in range(shards):
            value = terms[shard, group].astype(F32) + landed[0, shard].astype(F32)
            for turn in order[:-1]:
                value = value + summed[turn - 1, shard].astype(F32)
            ready[shard] = value.astype(BF16)
        for index in range(len(steps)):
            start(swap(index))
        whole[group, me] = ready[me]
        yield
        for turn in order[:-1]:
            along(1, turn).wait_recv()
        value = row_terms[group].astype(F32) + landed_rows[0].astype(F32)
        for turn in order[:-1]:
            value = value + summed_rows[turn - 1].astype(F32)
        whole_rows[group] = value.astype(BF16)
        for turn in order[:-1]:
            start(out(1, turn, group))
        start(over(1, 0, group))
        yield
        for index in range(len(steps)):
            swap(index).wait_recv()
        for turn in order[:-1]:
            start(out(0, turn, group))
        start(over(0, 0, group))
        yield
        for which in (1, 0):
            for turn in order[:-1]:
                entry = layer_at(layers - turn) * 2 + core
                out(which, turn, entry).wait_recv()
                start(over(which, turn, entry))
                yield
        for index in range(len(group_steps)):
            sum_copy(index).wait_recv()
        tail_sum = tail_sums[0]
        for index in range(1, place.groups):
            tail_sum = tail_sum + tail_sums[index]
        tail_out[...] = tail_sum
        depth = terms.shape[3] // 3
        for which in (1, 0):
            for turn in range(layers):
                entry = layer_at(layers - turn) * 2 + 1 - core
                over(which, turn, entry).wait_recv()
                yield
        for entry in range(place.groups):
            for shard in range(shards):
                here = pl.ds(shard * depth, depth)
                value = whole[entry, shard]
                query_out[entry, :, here] = value[:, :depth]
                key_out[entry, :, here] = value[:, depth : 2 * depth]
                value_out[entry, :, here] = value[:, 2 * depth :]
            yield
        for copy in sends:
            copy.wait_send()


def turn(values, cosine, sine):
    return values * cosine + pltpu.roll(values, HDIM // 2, 1) * sine


def head_forward(projected, place, gain, cosine, sine):
    proj = projected[:, place * HDIM : (place + 1) * HDIM]
    scale = rms_scale(proj)
    unit = proj * scale
    return scale, unit, turn(unit * gain, cosine, sine).astype(BF16)


def head_probs(query_rot, key_rot, seg_column, seg_row):
    scores = dot(query_rot, key_rot, NT) * (1.0 / math.sqrt(HDIM))
    scores = jnp.where(seg_column == seg_row, scores, MASK_FILL)
    exponent = jnp.exp(scores - jnp.max(scores, axis=-1, keepdims=True))
    return exponent * (1.0 / jnp.sum(exponent, axis=-1, keepdims=True))


def forward_steps(
    micro,
    hidden,
    projections,
    output_weight,
    gain,
    head_gains,
    cosine,
    sine,
    seg_column,
    seg_row,
    mixer,
    projected,
    attended,
    parts,
):
    span = seg_column.shape[1]
    depth = projections.shape[1] // 3
    heads = depth // HDIM
    tile = min(span, 256)
    rows = pl.ds(micro * span, span)
    for start in range(0, span, tile):
        here = pl.ds(micro * span + start, tile)
        values = hidden[here, :].astype(F32)
        mixer[here, :] = (values * rms_scale(values) * gain).astype(BF16)
    projected[rows, :] = dot(mixer[rows, :], projections[...], NN)
    yield
    for head in range(heads):
        own = projected[rows, :]
        _, _, query_rot = head_forward(own, head, head_gains[0], cosine[...], sine[...])
        _, _, key_rot = head_forward(own, heads + head, head_gains[1], cosine[...], sine[...])
        values = own[:, (2 * heads + head) * HDIM : (2 * heads + head + 1) * HDIM]
        probs = head_probs(query_rot, key_rot, seg_column[micro], seg_row[micro])
        attended[rows, head * HDIM : (head + 1) * HDIM] = dot(
            probs.astype(BF16), values.astype(BF16), NN
        ).astype(BF16)
        yield
    parts[rows, :] = dot(attended[rows, :], output_weight[...], NN).astype(BF16)
    yield


def backward_steps(
    micro,
    branch,
    projected,
    projections,
    output_weight,
    head_gains,
    cosine,
    sine,
    seg_column,
    seg_row,
    parts,
    gain_terms,
    attended_grad,
    projected_grad,
):
    span = seg_column.shape[1]
    heads = output_weight.shape[0] // HDIM
    scale = 1.0 / math.sqrt(HDIM)
    rows = pl.ds(micro * span, span)
    attended_grad[rows, :] = dot(branch[rows, :], output_weight[...], NT).astype(BF16)
    yield
    for head in range(heads):
        own = projected[rows, :]
        query_scale, query_unit, query_rot = head_forward(
            own, head, head_gains[0], cosine[...], sine[...]
        )
        key_scale, key_unit, key_rot = head_forward(
            own, heads + head, head_gains[1], cosine[...], sine[...]
        )
        values = own[:, (2 * heads + head) * HDIM : (2 * heads + head + 1) * HDIM]
        probs = head_probs(query_rot, key_rot, seg_column[micro], seg_row[micro])
        out_grad = attended_grad[rows, head * HDIM : (head + 1) * HDIM]
        prob_grad = dot(out_grad, values.astype(BF16), NT)
        row_delta = jnp.sum(probs * prob_grad, axis=-1, keepdims=True)
        score_grad = (probs * (prob_grad - row_delta)).astype(BF16)
        projected_grad[rows, (2 * heads + head) * HDIM : (2 * heads + head + 1) * HDIM] = dot(
            probs.astype(BF16), out_grad, TN
        ).astype(BF16)
        for which, (rot_grad, unit, unit_scale) in enumerate(
            (
                (dot(score_grad, key_rot, NN) * scale, query_unit, query_scale),
                (dot(score_grad, query_rot, TN) * scale, key_unit, key_scale),
            )
        ):
            unit_grad = turn(rot_grad, cosine[...], -sine[...])
            gain_terms[which : which + 1] += jnp.sum(unit_grad * unit, axis=0, keepdims=True)
            place = (which * heads + head) * HDIM
            projected_grad[rows, place : place + HDIM] = norm_back(
                unit_grad * head_gains[which], unit, unit_scale
            ).astype(BF16)
        yield
    parts[rows, :] = dot(projected_grad[rows, :], projections[...], NT).astype(BF16)
    yield


def weight_steps(branch, mixer, attended, projected_grad, projection_terms, output_terms):
    width = branch.shape[1]
    tile = min(512, width)
    for start in range(0, width, tile):
        here = pl.ds(start, tile)
        output_terms[:, here] = dot(attended[...], branch[:, here], TN).astype(BF16)
        projection_terms[here, :] = dot(mixer[:, here], projected_grad[...], TN).astype(BF16)
        yield


class AttentionForward:
    def __init__(
        self, weights, smalls, inputs, cotangent, output_weight, tables, segments, layout
    ):
        _, deep, wide = layout
        micros, rows, width = inputs.shape
        shards = deep * wide
        tokens = micros * shards * rows
        depth = output_weight.shape[0]
        self.columns = Columns(weights, smalls, layout)
        self.operands = [
            *self.columns.operands,
            inputs,
            cotangent,
            output_weight,
            *tables,
            *segments,
        ]
        self.in_specs = [*self.columns.in_specs, ANYWHERE, ANYWHERE, *[RESIDENT] * 5]
        self.outs = [
            *self.columns.outs[1:],
            jax.ShapeDtypeStruct((shards, depth, 3 * depth), BF16),
            jax.ShapeDtypeStruct((tokens, width), BF16),
            jax.ShapeDtypeStruct((tokens, width), BF16),
            jax.ShapeDtypeStruct((tokens, 3 * depth), F32),
            jax.ShapeDtypeStruct((tokens, depth), BF16),
            jax.ShapeDtypeStruct((micros, rows, width), F32),
        ]
        self.out_specs = [ANYWHERE, RESIDENT, RESIDENT, ANYWHERE, *[RESIDENT] * 4]
        gathers = gather_scratch(micros, deep, wide)
        scatters = scatter_scratch(rows, width, deep, wide)
        self.sizes = [len(self.columns.scratch), len(gathers), len(gathers), len(scatters)]
        columns_out = self.columns.outs[0]
        self.scratch = [
            pltpu.VMEM(columns_out.shape, BF16),
            pltpu.VMEM((tokens, width), BF16),
            pltpu.VMEM((tokens, width), BF16),
            pltpu.VMEM((1, width), F32),
            *self.columns.scratch,
            *gathers,
            *gathers,
            *scatters * micros,
        ]
        self.steps = self.columns.steps | grid_steps(deep, wide)

    def run(
        self,
        place,
        query_weight,
        key_weight,
        value_weight,
        small,
        gains,
        inputs,
        cotangent,
        output_weight,
        cosine,
        sine,
        seg_column,
        seg_row,
        small_all,
        gains_all,
        projections,
        upstream,
        mixer,
        projected,
        attended,
        total,
        swapped,
        hidden,
        parts,
        gain,
        *scratch,
    ):
        micros, shards, deep = inputs.shape[0], place.shards, place.deep
        scratch = list(scratch)

        def take(count):
            return [scratch.pop(0) for _ in range(count)]

        columns = self.columns.run(
            place,
            query_weight,
            key_weight,
            value_weight,
            small,
            gains,
            swapped,
            small_all,
            gains_all,
            *take(self.sizes[0]),
        )
        inward = gather_steps(place, inputs, hidden, *take(self.sizes[1]))
        upward = gather_steps(place, cotangent, upstream, *take(self.sizes[2]))
        scatters = [
            scatter_steps(place, parts, micro, total.at[micro], *take(self.sizes[3]))
            for micro in range(micros)
        ]
        next(columns)
        next(inward)
        next(columns)
        yield from until(inward, 1)
        yield from columns
        part, depth = swapped.shape[2], output_weight.shape[0]
        head_gains = jnp.zeros((1, 2 * HDIM), F32)
        for shard in range(shards):
            for group in range(place.groups):
                projections[shard, group * part : (group + 1) * part, :] = swapped[shard, group]
            known = gains_all[shard].astype(F32)
            gain[:, shard * depth : (shard + 1) * depth] = known[0:1, :depth]
            head_gains = head_gains + known[1:2, : 2 * HDIM]
        head_gains = (head_gains[:, :HDIM], head_gains[:, HDIM:])
        weight = projections[...].reshape(-1, projections.shape[2])
        running = []
        for micro in range(micros):
            for _ in forward_steps(
                micro,
                hidden,
                weight,
                output_weight,
                gain[...],
                head_gains,
                cosine,
                sine,
                seg_column,
                seg_row,
                mixer,
                projected,
                attended,
                parts,
            ):
                for each in list(running):
                    if next(each, END) is END:
                        running.remove(each)
                if micro + 1 < micros:
                    next(inward, END)
                yield
            if micro + 1 < micros:
                yield from until(inward, micro + 2)
            running.append(scatters[micro])
            next(scatters[micro])
        running.append(upward)
        yield from inward
        yield from together(*running)


class AttentionBackward:
    def __init__(
        self,
        branch,
        mixer,
        projected,
        attended,
        projections,
        output_weight,
        head_gains,
        tables,
        segments,
        beside,
        layout,
    ):
        _, deep, wide = layout
        micros, rows, width = branch.shape
        tokens = micros * deep * wide * rows
        depth = output_weight.shape[0]
        self.beside = beside
        self.operands = [
            branch,
            mixer,
            projected,
            attended,
            projections,
            output_weight,
            head_gains,
            *tables,
            *segments,
            *[operand for part in beside for operand in part.operands],
        ]
        self.in_specs = [ANYWHERE] + [RESIDENT] * 10
        self.in_specs += [spec for part in beside for spec in part.in_specs]
        self.outs = [
            jax.ShapeDtypeStruct((width, 3 * depth), BF16),
            jax.ShapeDtypeStruct((depth, width), BF16),
            jax.ShapeDtypeStruct((8, HDIM), F32),
            jax.ShapeDtypeStruct((micros, rows, width), F32),
            *[out for part in beside for out in part.outs],
        ]
        self.out_specs = [RESIDENT] * 4 + [spec for part in beside for spec in part.out_specs]
        gathers = gather_scratch(micros, deep, wide)
        scatters = scatter_scratch(rows, width, deep, wide)
        self.sizes = [len(gathers), len(scatters)]
        self.scratch = [
            pltpu.VMEM((tokens, width), BF16),
            pltpu.VMEM((tokens, width), BF16),
            pltpu.VMEM((tokens, depth), BF16),
            pltpu.VMEM((tokens, 3 * depth), BF16),
            *gathers,
            *scatters * micros,
            *[buffer for part in beside for buffer in part.scratch],
        ]
        self.steps = grid_steps(deep, wide).union(*(part.steps for part in beside))

    def run(self, place, *refs):
        refs = list(refs)

        def take(count):
            return [refs.pop(0) for _ in range(count)]

        (
            branch,
            mixer,
            projected,
            attended,
            projections,
            output_weight,
            head_gains,
            cosine,
            sine,
            seg_column,
            seg_row,
        ) = take(11)
        beside_in = [take(len(part.operands)) for part in self.beside]
        projection_terms, output_terms, gain_terms, total = take(4)
        beside_out = [take(len(part.outs)) for part in self.beside]
        branch_all, parts, attended_grad, projected_grad = take(4)
        micros = branch.shape[0]
        inward = gather_steps(place, branch, branch_all, *take(self.sizes[0]))
        scatters = [
            scatter_steps(place, parts, micro, total.at[micro], *take(self.sizes[1]))
            for micro in range(micros)
        ]
        sides = [
            part.run(place, *own_in, *own_out, *take(len(part.scratch)))
            for part, own_in, own_out in zip(self.beside, beside_in, beside_out, strict=True)
        ]
        next(inward)
        for side in sides:
            next(side)
        gain_terms[...] = jnp.zeros_like(gain_terms)
        gains = (head_gains[0:1], head_gains[1:2])
        yield from until(inward, 1)
        for side in sides[:1]:
            next(side)
            next(side)
        running = []
        for micro in range(micros):
            for _ in backward_steps(
                micro,
                branch_all,
                projected,
                projections,
                output_weight,
                gains,
                cosine,
                sine,
                seg_column,
                seg_row,
                parts,
                gain_terms,
                attended_grad,
                projected_grad,
            ):
                for each in list(running):
                    if next(each, END) is END:
                        running.remove(each)
                if micro + 1 < micros:
                    next(inward, END)
                yield
            running.append(scatters[micro])
            next(scatters[micro])
            if micro == 0:
                for side in sides[1:]:
                    next(side)
                    next(side)
            if micro + 1 < micros:
                yield from until(inward, micro + 2)
        running.append(inward)
        running.append(
            weight_steps(
                branch_all, mixer, attended, projected_grad, projection_terms, output_terms
            )
        )
        yield from together(*running)
        for side in sides:
            yield from side


def units_kernel(
    span,
    rows_ref,
    upstream_ref,
    share_ref,
    gate_ref,
    up_ref,
    down_ref,
    hidden_ref,
    gate_pre_ref,
    up_pre_ref,
    dot_ref,
):
    half = pl.program_id(0)
    half_width = gate_ref.shape[2]
    lanes = lax.broadcasted_iota(jnp.int32, share_ref.shape, 1)
    share = jnp.sum(jnp.where(lanes == half, share_ref[...], 0.0), axis=1, keepdims=True)

    def body(step, carry):
        units = pl.ds(pl.multiple_of(step * span, span), span)
        gate_pre = dot(rows_ref[...], gate_ref[0, :, units], NN)
        up_pre = dot(rows_ref[...], up_ref[0, :, units], NN)
        units_grad = dot(upstream_ref[...], down_ref[0, units, :], NT)
        sigmoid_gate = 1.0 / (1.0 + jnp.exp(-gate_pre))
        swish_gate = gate_pre * sigmoid_gate
        activated = swish_gate * up_pre
        dots = jnp.sum(activated * units_grad, axis=1, keepdims=True)
        dot_ref[...] += jnp.where(lanes == half, dots, 0.0)
        hidden_ref[0, :, units] = (activated * share).astype(BF16)
        weighted = units_grad * share
        gate_pre_ref[0, :, units] = (
            weighted * up_pre * (sigmoid_gate * (1.0 + gate_pre * (1.0 - sigmoid_gate)))
        ).astype(BF16)
        up_pre_ref[0, :, units] = (weighted * swish_gate).astype(BF16)
        return carry

    @pl.when(half == 0)
    def _():
        dot_ref[...] = jnp.zeros_like(dot_ref)

    lax.fori_loop(0, half_width // span, body, 0)


def expert_units(rows, upstream, share, gate_all, up_all, down_all):
    tokens, width = rows.shape
    halves, _, units = gate_all.shape

    def each(*shape):
        return pl.BlockSpec((1,) + shape, lambda half: (half,) + (0,) * len(shape))

    whole = pl.BlockSpec(memory_space=pltpu.VMEM)
    return pl.pallas_call(
        functools.partial(units_kernel, 256 if tokens <= 1024 else 128),
        grid=(halves,),
        in_specs=[whole, whole, whole, each(width, units), each(width, units), each(units, width)],
        out_specs=[each(tokens, units), each(tokens, units), each(tokens, units), whole],
        out_shape=[
            jax.ShapeDtypeStruct((halves, tokens, units), BF16),
            jax.ShapeDtypeStruct((halves, tokens, units), BF16),
            jax.ShapeDtypeStruct((halves, tokens, units), BF16),
            jax.ShapeDtypeStruct(share.shape, F32),
        ],
        compiler_params=pltpu.CompilerParams(vmem_limit_bytes=VMEM_LIMIT),
        cost_estimate=pl.CostEstimate(
            flops=6 * tokens * width * units * halves,
            bytes_accessed=6 * width * units * halves,
            transcendentals=0,
        ),
    )(rows, upstream, share, gate_all, up_all, down_all)


def merge_kernel(gate_pre_ref, up_pre_ref, gate_ref, up_ref, grad_ref):
    halves = gate_pre_ref.shape[0]
    grad = dot(gate_pre_ref[0], gate_ref[0], NT) + dot(up_pre_ref[0], up_ref[0], NT)
    for half in range(1, halves):
        grad = grad + dot(gate_pre_ref[half], gate_ref[half], NT)
        grad = grad + dot(up_pre_ref[half], up_ref[half], NT)
    grad_ref[...] = grad.astype(BF16)


def expert_merge(gate_pre, up_pre, gate_all, up_all):
    halves, tokens, units = gate_pre.shape
    width = gate_all.shape[1]
    span = 256
    batch = min(tokens, 1024)
    slab = pl.BlockSpec(
        (halves, batch, units), lambda turn, step: (0, turn, 0), pipeline_mode=pl.Buffered(1)
    )
    tile = pl.BlockSpec((halves, span, units), lambda turn, step: (0, step, 0))
    return pl.pallas_call(
        merge_kernel,
        grid=(tokens // batch, width // span),
        in_specs=[slab, slab, tile, tile],
        out_specs=pl.BlockSpec((batch, span), lambda turn, step: (turn, step)),
        out_shape=jax.ShapeDtypeStruct((tokens, width), BF16),
        compiler_params=pltpu.CompilerParams(vmem_limit_bytes=VMEM_LIMIT),
        cost_estimate=pl.CostEstimate(
            flops=4 * tokens * width * units * halves,
            bytes_accessed=4 * width * units * halves,
            transcendentals=0,
        ),
    )(gate_pre, up_pre, gate_all, up_all)


def output_kernel(hidden_ref, down_ref, out_ref):
    halves = hidden_ref.shape[0]
    out = dot(hidden_ref[0], down_ref[0], NN)
    for half in range(1, halves):
        out = out + dot(hidden_ref[half], down_ref[half], NN)
    out_ref[...] = out.astype(BF16)


def expert_output(hidden, down_all):
    halves, tokens, units = hidden.shape
    width = down_all.shape[2]
    span = 256
    batch = min(tokens, 1024)
    slab = pl.BlockSpec(
        (halves, batch, units), lambda turn, step: (0, turn, 0), pipeline_mode=pl.Buffered(1)
    )
    return pl.pallas_call(
        output_kernel,
        grid=(tokens // batch, width // span),
        in_specs=[slab, pl.BlockSpec((halves, units, span), lambda turn, step: (0, 0, step))],
        out_specs=pl.BlockSpec((batch, span), lambda turn, step: (turn, step)),
        out_shape=jax.ShapeDtypeStruct((tokens, width), BF16),
        compiler_params=pltpu.CompilerParams(vmem_limit_bytes=VMEM_LIMIT),
        cost_estimate=pl.CostEstimate(
            flops=2 * tokens * width * units * halves,
            bytes_accessed=2 * width * units * halves,
            transcendentals=0,
        ),
    )(hidden, down_all)


def weights_kernel(
    span,
    rows_ref,
    upstream_ref,
    hidden_ref,
    gate_pre_ref,
    up_pre_ref,
    gate_grad_ref,
    up_grad_ref,
    down_grad_ref,
):
    def body(step, carry):
        units = pl.ds(pl.multiple_of(step * span, span), span)
        gate_grad_ref[0, :, units] = dot(rows_ref[...], gate_pre_ref[0, :, units], TN).astype(BF16)
        up_grad_ref[0, :, units] = dot(rows_ref[...], up_pre_ref[0, :, units], TN).astype(BF16)
        down_grad_ref[0, units, :] = dot(
            hidden_ref[0, :, units], upstream_ref[...], TN
        ).astype(BF16)
        return carry

    lax.fori_loop(0, gate_grad_ref.shape[2] // span, body, 0)


def expert_weights(rows, upstream, hidden, gate_pre, up_pre):
    tokens, width = rows.shape
    halves, _, units = hidden.shape

    def each(*shape):
        return pl.BlockSpec((1,) + shape, lambda half: (half,) + (0,) * len(shape))

    whole = pl.BlockSpec(memory_space=pltpu.VMEM)
    slab = each(tokens, units)
    return pl.pallas_call(
        functools.partial(weights_kernel, 256),
        grid=(halves,),
        in_specs=[whole, whole, slab, slab, slab],
        out_specs=[each(width, units), each(width, units), each(units, width)],
        out_shape=[
            jax.ShapeDtypeStruct((halves, width, units), BF16),
            jax.ShapeDtypeStruct((halves, width, units), BF16),
            jax.ShapeDtypeStruct((halves, units, width), BF16),
        ],
        compiler_params=pltpu.CompilerParams(vmem_limit_bytes=VMEM_LIMIT),
        cost_estimate=pl.CostEstimate(
            flops=6 * tokens * width * units * halves,
            bytes_accessed=6 * width * units * halves,
            transcendentals=0,
        ),
    )(rows, upstream, hidden, gate_pre, up_pre)


def experts_in_turn(
    expert_input, upstream_all, choose, router_full, gate_all, up_all, down_all, layout, micros
):
    groups, deep, wide = layout
    shards = deep * wide
    experts = router_full.shape[1]
    shard_place = lax.axis_index("shard")
    ((expert_all,),) = fuse([Gather(expert_input, layout)], layout, 2, "experts_in")
    logits = jnp.dot(expert_all, router_full, preferred_element_type=F32)
    share = softmax_rows(jnp.sum(choose * logits[:, None, :], axis=-1))
    share_wide = jnp.sum(choose * share[:, :, None], axis=1)
    served = (jnp.arange(groups, dtype=jnp.int32) * shards + shard_place) // 2
    serves = (served[:, None] == jnp.arange(experts, dtype=jnp.int32)).astype(F32)
    share_own = jnp.pad(
        jnp.dot(share_wide, serves.T, precision=PRECISE), ((0, 0), (0, 128 - groups))
    )
    activated, gate_pre, up_pre, dots = expert_units(
        expert_all, upstream_all, share_own, gate_all, up_all, down_all
    )
    expert_grad_parts = expert_merge(gate_pre, up_pre, gate_all, up_all)
    gate_pre, expert_grad_parts = lax.optimization_barrier((gate_pre, expert_grad_parts))
    gate_terms, up_terms, down_terms = expert_weights(
        expert_all, upstream_all, activated, gate_pre, up_pre
    )
    out_parts = expert_output(activated, down_all)

    halves = groups * shards
    lanes = halves + -halves % 128
    columns = jnp.arange(groups, dtype=jnp.int32) * shards + shard_place
    columns = (columns[:, None] == jnp.arange(lanes, dtype=jnp.int32)).astype(F32)
    placed = jnp.dot(dots[:, :groups], columns, precision=PRECISE)
    placed_high = placed.astype(BF16)
    placed_low = (placed - placed_high.astype(F32)).astype(BF16)
    placed = jnp.concatenate([placed_high, placed_low], axis=1)
    (dot_total,), (expert_grad,) = fuse(
        [Scatter(placed, micros, layout), Scatter(expert_grad_parts, micros, layout)],
        layout,
        3,
        "experts_out",
    )
    return gate_terms, up_terms, down_terms, out_parts, share, expert_grad, dot_total, lanes


def per_device(
    groups,
    shards,
    wide,
    inputs,
    segment_ids,
    routes,
    cotangent,
    query_weight,
    key_weight,
    value_weight,
    output_weight,
    router_weight,
    attention_gain,
    expert_gain,
    query_gain,
    key_gain,
    gate_weight,
    up_weight,
    down_weight,
):
    micros, rows, width = inputs.shape
    deep = shards // wide
    span = shards * rows
    tokens = micros * span
    experts = router_weight.shape[1]
    column_width = width // shards
    shard_place = lax.axis_index("shard")
    layout = (groups, deep, shards // deep)

    gate_all = lax.all_gather(gate_weight, "expert", axis=0, tiled=True)
    up_all = lax.all_gather(up_weight, "expert", axis=0, tiled=True)
    down_all = lax.all_gather(down_weight, "expert", axis=0, tiled=True)

    cuts = [column_width * experts, routes.size]
    small_own = jnp.concatenate(
        [router_weight.reshape(-1), routes.reshape(-1).astype(BF16)]
    )
    small_own = jnp.pad(small_own, (0, -sum(cuts) % 2048)).reshape(-1, 128)

    def placed_row(gain):
        row = jnp.zeros((gain.shape[0] * shards,), BF16)
        return lax.dynamic_update_slice_in_dim(row, gain, shard_place * gain.shape[0], 0)

    gains_own = jnp.zeros((16, max(2 * column_width, 2 * HDIM)), BF16)
    gains_own = gains_own.at[0, : 2 * column_width].set(
        jnp.concatenate([attention_gain, expert_gain])
    )
    gains_own = gains_own.at[1, : 2 * HDIM].set(
        jnp.concatenate([placed_row(query_gain), placed_row(key_gain)])
    )

    tables = rotary(span)
    segments = (segment_ids[:, :, None], segment_ids[:, None, :])
    (
        (
            small,
            gains_all,
            projections,
            upstream_all,
            mixer_all,
            projected,
            attended,
            middle_total,
        ),
    ) = fuse(
        [
            AttentionForward(
                (query_weight, key_weight, value_weight),
                (small_own, gains_own),
                inputs,
                cotangent,
                output_weight,
                tables,
                segments,
                layout,
            )
        ],
        layout,
        0,
        "attention_forward",
    )
    projections = projections.reshape(width, 3 * column_width)
    small = small.reshape(shards, -1)
    router_full = small[:, : cuts[0]].reshape(width, experts)
    routes_all = small[:, cuts[0] : sum(cuts)].reshape(shards, micros, rows, -1)
    routes_all = routes_all.transpose(1, 0, 2, 3).reshape(tokens, -1).astype(jnp.int32)
    attn_gain = gains_all[:, 0, :column_width].reshape(-1).astype(F32)
    expert_gain_full = gains_all[:, 0, column_width : 2 * column_width].reshape(-1).astype(F32)
    head_gains = jnp.sum(gains_all[:, 1, : 2 * HDIM].astype(F32), axis=0).reshape(2, HDIM)
    head_gains = jnp.pad(head_gains, ((0, 6), (0, 0)))
    hidden = inputs.astype(F32)
    middle = hidden + middle_total

    scale_second = rms_scale(middle)
    normed_second = middle * scale_second
    expert_input = (normed_second * expert_gain_full).astype(BF16)
    early = tokens <= 1024 and 4 * groups * shards <= 256
    choose = (routes_all[:, :, None] == jnp.arange(experts, dtype=jnp.int32)).astype(F32)
    if early:
        mask = jnp.pad(jnp.sum(choose, axis=1), ((0, 0), (0, 128 - experts)))
        router_wide = jnp.pad(router_full, ((0, 0), (0, 128 - experts)))
        (
            (
                gate_terms,
                up_terms,
                down_terms,
                out_parts,
                share_wide,
                expert_grad,
                dot_total,
            ),
        ) = fuse(
            [
                Experts(
                    expert_input,
                    upstream_all,
                    mask,
                    router_wide,
                    gate_all,
                    up_all,
                    down_all,
                    layout,
                )
            ],
            layout,
            2,
            "experts",
        )
        share = jnp.sum(choose * share_wide[:, None, :experts], axis=-1)
        half_lanes = 64
    else:
        (
            gate_terms,
            up_terms,
            down_terms,
            out_parts,
            share,
            expert_grad,
            dot_total,
            half_lanes,
        ) = experts_in_turn(
            expert_input,
            upstream_all,
            choose,
            router_full,
            gate_all,
            up_all,
            down_all,
            layout,
            micros,
        )

    def own_rows(values):
        return lax.dynamic_slice_in_dim(
            values.reshape((micros, span) + values.shape[1:]), shard_place * rows, rows, 1
        )

    own_choose, own_share = own_rows(choose), own_rows(share)
    halves = groups * shards
    share_grad_wide = (
        dot_total[..., :halves] + dot_total[..., half_lanes : half_lanes + halves]
    )
    share_grad_wide = share_grad_wide.reshape(micros, rows, experts, 2).sum(axis=-1)
    share_grad = jnp.sum(own_choose * share_grad_wide[:, :, None, :], axis=-1)
    chosen_grad = own_share * (
        share_grad - jnp.sum(own_share * share_grad, axis=-1, keepdims=True)
    )
    own_logits_grad = jnp.sum(own_choose * chosen_grad[..., None], axis=2)
    expert_grad = expert_grad + jnp.dot(
        own_logits_grad, router_full.astype(F32).T, precision=PRECISE
    )
    expert_gain_term = jnp.sum(expert_grad * normed_second, axis=(0, 1))
    middle_grad = cotangent.astype(F32) + norm_back(
        expert_grad * expert_gain_full, normed_second, scale_second
    )
    router_term = jnp.einsum(
        "mtd,mte->de", expert_input.astype(F32), own_logits_grad, precision=PRECISE
    )

    beside = []
    if early:
        beside = [ExpertScatter(gate_terms, layout), ExpertScatter(up_terms, layout)]
    ((projection_terms, output_term, head_gain_terms, mixer_grad, *side_grads),) = fuse(
        [
            AttentionBackward(
                middle_grad.astype(BF16),
                mixer_all,
                projected,
                attended,
                projections,
                output_weight,
                head_gains,
                tables,
                segments,
                beside,
                layout,
            )
        ],
        layout,
        4,
        "attention_backward",
    )
    scale_first = rms_scale(hidden)
    normed_first = hidden * scale_first
    attn_gain_term = jnp.sum(mixer_grad * normed_first, axis=(0, 1))
    hidden_grad = middle_grad + norm_back(mixer_grad * attn_gain, normed_first, scale_first)

    part = column_width // groups
    tail = jnp.concatenate(
        [
            term.reshape(shards, -1)
            for term in (
                router_term,
                attn_gain_term,
                expert_gain_term,
                head_gain_terms[0],
                head_gain_terms[1],
            )
        ],
        axis=1,
    )
    tail = jnp.pad(tail, ((0, 0), (0, -tail.shape[1] % 1024))).reshape(shards, -1, 128)
    (output_grad, tail, query_grad, key_grad, value_grad), (outs,), *last_grads = fuse(
        [
            Rows(
                projection_terms.reshape(shards, groups, part, 3 * column_width),
                output_term.reshape(groups, part, width),
                tail,
                layout,
            ),
            Scatter(out_parts, micros, layout),
            *([ExpertScatter(down_terms, layout)] if early else []),
        ],
        layout,
        5,
        "exit",
    )
    if early:
        gate_grad, up_grad = side_grads
        ((down_grad,),) = last_grads
    else:
        gate_grad, up_grad, down_grad = (
            fuse([ExpertScatter(terms, layout)], layout, 6 + index, "weights")[0][0]
            for index, terms in enumerate((gate_terms, up_terms, down_terms))
        )
    result = middle + outs
    tail = tail.reshape(-1)
    lengths = [column_width * experts] + [column_width] * 2 + [HDIM // shards] * 2
    starts = [sum(lengths[:place]) for place in range(len(lengths))]
    tails = [
        tail[start : start + length] for start, length in zip(starts, lengths, strict=True)
    ]
    return (
        result.astype(BF16),
        hidden_grad.astype(BF16),
        query_grad.astype(F32).reshape(column_width, width),
        key_grad.astype(F32).reshape(column_width, width),
        value_grad.astype(F32).reshape(column_width, width),
        output_grad.astype(F32).reshape(column_width, width),
        tails[0].reshape(column_width, experts),
        tails[1],
        tails[2],
        tails[3],
        tails[4],
        gate_grad.astype(F32)[None],
        up_grad.astype(F32)[None],
        down_grad.astype(F32)[None],
    )


def solution(mesh):
    groups, shards = mesh.shape["expert"], mesh.shape["shard"]
    wide = shards // 4 if shards % 4 == 0 else 1
    in_specs = (
        P(None, ("expert", "shard"), None),
        P(None, "expert"),
        P(None, ("expert", "shard"), None),
        P(None, ("expert", "shard"), None),
        P("shard", None),
        P("shard", None),
        P("shard", None),
        P("shard", None),
        P("shard", None),
        P("shard"),
        P("shard"),
        P("shard"),
        P("shard"),
        P(("expert", "shard"), None, None),
        P(("expert", "shard"), None, None),
        P(("expert", "shard"), None, None),
    )
    out_specs = (
        P(None, ("expert", "shard"), None),
        P(None, ("expert", "shard"), None),
        P("shard", None),
        P("shard", None),
        P("shard", None),
        P("shard", None),
        P("shard", None),
        P("shard"),
        P("shard"),
        P("shard"),
        P("shard"),
        P(("expert", "shard"), None, None),
        P(("expert", "shard"), None, None),
        P(("expert", "shard"), None, None),
    )
    return jax.shard_map(
        functools.partial(per_device, groups, shards, wide),
        mesh=mesh,
        in_specs=in_specs,
        out_specs=out_specs,
        check_vma=False,
    )
```

```python
import functools
import math

import jax
import jax.numpy as jnp
from jax import lax
from jax.experimental import pallas as pl
from jax.experimental.pallas import tpu as pltpu
from jax.sharding import PartitionSpec as P

HDIM = 128
EPSILON = 1e-05
ROPE_BASE = 10000.0
MASK_FILL = -1e30
PRECISE = lax.Precision.HIGHEST
MESH = pl.DeviceIdType.MESH
F32 = jnp.float32
BF16 = jnp.bfloat16
NN = (((1,), (0,)), ((), ()))
NT = (((1,), (1,)), ((), ()))
TN = (((0,), (0,)), ((), ()))
VMEM_LIMIT = 63 << 20
LINK_COST = pl.CostEstimate(flops=60 * 10**9, bytes_accessed=8 << 20, transcendentals=0)


def dot(left, right, dims):
    return lax.dot_general(left, right, dims, preferred_element_type=F32)


def rms_scale(values):
    return lax.rsqrt(jnp.mean(values * values, axis=-1, keepdims=True) + EPSILON)


def norm_back(normed_grad, normed, inv_scale):
    return inv_scale * (
        normed_grad - normed * jnp.mean(normed_grad * normed, axis=-1, keepdims=True)
    )


def rotary(span):
    steps = jnp.arange(HDIM // 2, dtype=jnp.int32).astype(F32)
    freqs = jnp.power(ROPE_BASE, -2.0 * steps / HDIM)
    theta = jnp.arange(span, dtype=jnp.int32).astype(F32)[:, None] * freqs[None, :]
    cosine, sine = jnp.cos(theta), jnp.sin(theta)
    return (
        jnp.concatenate([cosine, cosine], axis=1),
        jnp.concatenate([-sine, sine], axis=1),
    )


def softmax_rows(scores):
    row_peak = jnp.max(scores, axis=-1, keepdims=True)
    exponent = jnp.exp(scores - row_peak)
    return exponent / jnp.sum(exponent, axis=-1, keepdims=True)


class Place:
    def __init__(self, groups, deep, wide):
        self.deep, self.wide = deep, wide
        self.shards, self.groups, self.layers = deep * wide, groups, groups // 2
        group, me = lax.axis_index("expert"), lax.axis_index("shard")
        self.group, self.me = group, me
        self.layer, self.core = group // 2, lax.rem(group, 2)
        self.row, self.column = me // wide, lax.rem(me, wide)

    def peer(self, layer_step=0, core_step=0, row_step=0, column_step=0):
        group, me = self.group, self.me
        if layer_step or core_step:
            group = lax.rem(self.layer + layer_step, self.layers) * 2 + (
                1 - self.core if core_step else self.core
            )
        if row_step or column_step:
            me = lax.rem(self.row + row_step, self.deep) * self.wide + lax.rem(
                self.column + column_step, self.wide
            )
        return group, me

    def grid_place(self, row_step, column_step):
        return self.peer(0, 0, row_step, column_step)[1]

    def back(self, layer_step=0, core_step=0, row_step=0, column_step=0):
        return self.peer(
            (self.layers - layer_step) % self.layers,
            core_step,
            (self.deep - row_step) % self.deep,
            (self.wide - column_step) % self.wide,
        )


def send_to(peer, source, target, send_sem, recv_sem):
    return pltpu.make_async_remote_copy(
        src_ref=source,
        dst_ref=target,
        send_sem=send_sem,
        recv_sem=recv_sem,
        device_id=peer,
        device_id_type=MESH,
    )


def dma(*shape):
    return pltpu.SemaphoreType.DMA(tuple(max(1, size) for size in shape))


ANYWHERE = pl.BlockSpec(memory_space=pl.ANY)
RESIDENT = pl.BlockSpec(memory_space=pltpu.VMEM)


def grid_steps(deep, wide):
    steps = {(0, 0, row, 0) for row in range(1, deep)}
    return steps | {(0, 0, 0, column) for column in range(1, wide)}


def shard_steps(deep, wide):
    return {
        (0, 0, row, column) for row in range(deep) for column in range(wide) if row or column
    }


def expert_steps(layers):
    return {(step, 0, 0, 0) for step in range(1, layers)} | {(0, 1, 0, 0)}


def fuse(parts, layout, collective_id, name):
    groups, deep, wide = layout
    operands = [operand for part in parts for operand in part.operands]
    in_specs = [spec for part in parts for spec in part.in_specs]
    out_shape = [out for part in parts for out in part.outs]
    out_specs = [spec for part in parts for spec in part.out_specs]
    scratch = [buffer for part in parts for buffer in part.scratch]
    steps = sorted(set().union(*(part.steps for part in parts)))

    def kernel(*refs):
        place = Place(groups, deep, wide)
        barrier = pltpu.get_barrier_semaphore()
        for step in steps:
            pl.semaphore_signal(
                barrier, inc=1, device_id=place.peer(*step), device_id_type=MESH
            )
        pl.semaphore_wait(barrier, len(steps))
        ins = list(refs[: len(operands)])
        outs = list(refs[len(operands) : len(operands) + len(out_shape)])
        buffers = list(refs[len(operands) + len(out_shape) :])
        running = []
        for part in parts:
            part_ins = [ins.pop(0) for _ in part.operands]
            part_outs = [outs.pop(0) for _ in part.outs]
            part_buffers = [buffers.pop(0) for _ in part.scratch]
            running.append(part.run(place, *part_ins, *part_outs, *part_buffers))
        late = [
            run for run, part in zip(running, parts, strict=True) if isinstance(part, ExpertScatter)
        ]
        first = [run for run in running if run not in late]
        for run in late:
            next(run)
        for index, _ in enumerate(together(*first)):
            if index in (1, 7):
                for run in late:
                    next(run)
        for run in late:
            for _ in run:
                pass

    results = pl.pallas_call(
        kernel,
        out_shape=out_shape,
        in_specs=in_specs,
        out_specs=out_specs,
        scratch_shapes=scratch,
        compiler_params=pltpu.CompilerParams(
            collective_id=collective_id, has_side_effects=True, vmem_limit_bytes=VMEM_LIMIT
        ),
        cost_estimate=LINK_COST,
        name=name,
    )(*operands)
    results = list(results)
    return [[results.pop(0) for _ in part.outs] for part in parts]


END = object()


def together(*runs):
    runs = list(runs)
    while runs:
        for run in list(runs):
            if next(run, END) is END:
                runs.remove(run)
        yield


def until(run, token):
    for value in run:
        if value == token:
            return
        yield


def gather_scratch(pieces, deep, wide):
    return [
        dma(pieces, 2, deep - 1),
        dma(pieces, 2, deep - 1),
        dma(pieces, 2 * deep, wide - 1),
        dma(pieces, 2 * deep, wide - 1),
        dma(1),
    ]


def start_all(copies):
    for copy in copies:
        copy.start()


def end_all(copies):
    for copy in copies:
        copy.wait_send()


def gather_steps(place, own, whole, row_send, row_recv, col_send, col_recv, local):
    pieces, rows, _ = own.shape
    deep, wide, shards = place.deep, place.wide, place.shards
    row, column = place.row, place.column
    ends = []

    def slot(piece, source_row, source_column):
        source = piece * shards + source_row * wide + source_column
        return whole.at[pl.ds(pl.multiple_of(source * rows, rows), rows)]

    def known(piece, step, source_row):
        return slot(piece, source_row, column) if step else own.at[piece]

    def hop(piece, way, step, source_row):
        return send_to(
            (place.group, (row + 1 - 2 * way) * wide + column),
            known(piece, step, source_row),
            slot(piece, source_row, column),
            row_send.at[piece, way, step],
            row_recv.at[piece, way, step],
        )

    def across(piece, step, way, move, source_row, source_column):
        key = 2 * step - 1 + way if step else 0
        return send_to(
            place.peer(0, 0, 0, move),
            known(piece, step, source_row),
            slot(piece, source_row, source_column),
            col_send.at[piece, key, move - 1],
            col_recv.at[piece, key, move - 1],
        )

    def start_if(condition, copies):
        pl.when(condition)(functools.partial(start_all, copies))
        ends.append((condition, copies))

    def forward(piece, step, way, condition, source_row):
        start_if(
            condition,
            [across(piece, step, way, move, source_row, column) for move in range(1, wide)],
        )

    def begin(piece):
        start_if(row < deep - 1, [hop(piece, 0, 0, row)])
        start_if(row > 0, [hop(piece, 1, 0, row)])
        forward(piece, 0, 0, row >= 0, row)

    here = [
        pltpu.make_async_copy(own.at[piece], slot(piece, row, column), local.at[0])
        for piece in range(pieces)
    ]
    begin(0)
    for copy in here:
        copy.start()
    yield 0
    for piece in range(pieces):
        sources = []
        for step in range(1, deep):
            for way in (0, 1):
                source_row = row - step if way == 0 else row + step
                there = source_row >= 0 if way == 0 else source_row < deep
                onward = row < deep - 1 if way == 0 else row > 0
                pl.when(there)(hop(piece, way, step - 1, source_row).wait_recv)
                if step < deep - 1:
                    start_if(there & onward, [hop(piece, way, step, source_row)])
                forward(piece, step, way, there, source_row)
                sources.append((step, way, there, source_row))
            if step == 1 and piece + 1 < pieces:
                begin(piece + 1)
            yield 0
        for step, way, there, source_row in [(0, 0, row >= 0, row)] + sources:
            for move in range(1, wide):
                source_column = lax.rem(column + wide - move, wide)
                copy = across(piece, step, way, move, source_row, source_column)
                pl.when(there)(copy.wait_recv)
            if way or not step:
                yield 0
        if piece == 0:
            for copy in here:
                copy.wait()
        yield piece + 1
    for condition, copies in ends:
        pl.when(condition)(functools.partial(end_all, copies))


class Gather:
    def __init__(self, own, layout):
        _, deep, wide = layout
        pieces, rows, width = own.shape
        self.operands, self.in_specs = [own], [ANYWHERE]
        self.outs = [jax.ShapeDtypeStruct((pieces * deep * wide * rows, width), own.dtype)]
        self.out_specs = [ANYWHERE]
        self.scratch = gather_scratch(pieces, deep, wide)
        self.steps = grid_steps(deep, wide)
        self.run = gather_steps


def scatter_scratch(rows, width, deep, wide):
    return [
        pltpu.VMEM((deep, max(1, wide - 1), rows, width), BF16),
        pltpu.VMEM((deep + 1, rows, width), BF16),
        dma(2 * deep, wide - 1),
        dma(2 * deep, wide - 1),
        dma(2 * deep),
        dma(2 * deep),
    ]


def scatter_steps(
    place, parts, piece, total, landed, summed, col_send, col_recv, row_send, row_recv
):
    deep, wide, shards = place.deep, place.wide, place.shards
    row, column = place.row, place.column
    rows = total.shape[0]
    ends = []

    def block(target_row, target_column):
        target = piece * shards + target_row * wide + target_column
        return pl.ds(pl.multiple_of(target * rows, rows), rows)

    def along_row(key, target_row, move):
        target_column = lax.rem(column + move, wide)
        return send_to(
            place.peer(0, 0, 0, move),
            parts.at[block(target_row, target_column)],
            landed.at[target_row, move - 1],
            col_send.at[key, move - 1],
            col_recv.at[key, move - 1],
        )

    def hop(key, step, way, target_row):
        return send_to(
            (place.group, (row + 1 - 2 * way) * wide + column),
            landed.at[target_row, 0],
            summed.at[deep if step == 1 and way else target_row],
            row_send.at[key],
            row_recv.at[key],
        )

    order = []
    for step in range(deep - 1, 0, -1):
        for way in (0, 1):
            target_row = row - step if way else row + step
            there = target_row >= 0 if way else target_row < deep
            order.append((2 * step + way, step, way, target_row, there))
    order.append((0, 0, 0, row, row >= 0))

    def send_row(index):
        key, _, _, target_row, there = order[index]
        copies = [along_row(key, target_row, move) for move in range(1, wide)]
        pl.when(there)(functools.partial(start_all, copies))
        ends.append((there, copies))

    def fold(index):
        key, step, way, target_row, there = order[index]

        def body():
            for move in range(1, wide):
                along_row(key, target_row, move).wait_recv()
            value = parts[block(target_row, column), :].astype(F32)
            for move in range(1, wide):
                value = value + landed[target_row, move - 1].astype(F32)
            if step:
                landed[target_row, 0] = value.astype(BF16)
            else:
                total[...] = value

        pl.when(there)(body)

    def join(index):
        key, step, way, target_row, there = order[index]
        behind = row < deep - 1 if way else row > 0

        def body():
            hop(key + 2, step + 1, way, target_row).wait_recv()
            landed[target_row, 0] = (
                landed[target_row, 0].astype(F32) + summed[target_row].astype(F32)
            ).astype(BF16)

        if step < deep - 1:
            pl.when(there & behind)(body)
        copy = hop(key, step, way, target_row)
        pl.when(there)(copy.start)
        ends.append((there, [copy]))

    def finish(way):
        def body():
            hop(2 + way, 1, way, row).wait_recv()
            total[...] = total[...] + summed[deep if way else row].astype(F32)

        pl.when(row < deep - 1 if way else row > 0)(body)

    ahead = 4
    for index in range(min(ahead, len(order))):
        send_row(index)
    yield
    for index in range(len(order)):
        fold(index)
        if index + ahead < len(order):
            send_row(index + ahead)
        if index < len(order) - 1:
            join(index)
        if index % 2:
            yield
    yield
    for way in (0, 1):
        finish(way)
        yield
    for there, copies in ends:
        pl.when(there)(functools.partial(end_all, copies))


def scatter_pieces(runs, deep):
    running = []
    for run in runs:
        running.append(run)
        for _ in range(deep + 1):
            for each in list(running):
                if next(each, END) is END:
                    running.remove(each)
            yield
    yield from together(*running)


class Scatter:
    def __init__(self, parts, pieces, layout):
        _, deep, wide = layout
        tokens, width = parts.shape
        rows = tokens // (pieces * deep * wide)
        self.pieces = pieces
        self.operands, self.in_specs = [parts], [RESIDENT]
        self.outs = [jax.ShapeDtypeStruct((pieces, rows, width), F32)]
        self.out_specs = [RESIDENT]
        self.scratch = scatter_scratch(rows, width, deep, wide) * pieces
        self.steps = grid_steps(deep, wide)

    def run(self, place, parts, total, *scratch):
        each = len(scratch) // self.pieces
        runs = [
            scatter_steps(
                place,
                parts,
                piece,
                total.at[piece],
                *scratch[piece * each : (piece + 1) * each],
            )
            for piece in range(self.pieces)
        ]
        yield from scatter_pieces(runs, place.deep)


class Chain:
    def __init__(self, *parts):
        self.parts = parts
        for name in ("operands", "in_specs", "outs", "out_specs", "scratch"):
            setattr(self, name, [item for part in parts for item in getattr(part, name)])
        self.steps = set().union(*(part.steps for part in parts))

    def run(self, place, *refs):
        refs = list(refs)
        taken = [[] for _ in self.parts]
        for name in ("operands", "outs", "scratch"):
            for part, own in zip(self.parts, taken, strict=True):
                own.extend(refs.pop(0) for _ in getattr(part, name))
        for part, own in zip(self.parts, taken, strict=True):
            yield from part.run(place, *own)


class ExpertScatter:
    def __init__(self, terms, layout, chunks=2):
        groups = layout[0]
        layers = groups // 2
        _, rows, width = terms.shape
        part = rows // chunks
        self.operands, self.in_specs = [terms], [ANYWHERE]
        self.outs = [jax.ShapeDtypeStruct((rows, width), BF16)]
        self.out_specs = [RESIDENT]
        self.scratch = [
            pltpu.VMEM((chunks, layers, part, width), BF16),
            pltpu.VMEM((chunks, layers, part, width), BF16),
            pltpu.VMEM((chunks, max(1, layers - 1), part, width), BF16),
            dma(chunks, layers),
            dma(chunks, layers),
            dma(chunks, layers),
            dma(chunks, layers - 1),
            dma(chunks, layers - 1),
        ]
        self.steps = expert_steps(layers)

    def run(
        self,
        place,
        terms,
        total,
        mine,
        landed,
        summed,
        local,
        core_send,
        core_recv,
        layer_send,
        layer_recv,
    ):
        chunks, layers, part, _ = mine.shape
        span = min(part, 128)
        sends = []

        def entry(turn, core):
            return lax.rem(place.layer + turn, layers) * 2 + core

        def block(chunk, turn, core):
            return terms.at[entry(turn, core), pl.ds(chunk * part, part)]

        def load(chunk, turn):
            return pltpu.make_async_copy(
                block(chunk, turn, place.core), mine.at[chunk, turn], local.at[chunk, turn]
            )

        def across(chunk, turn):
            return send_to(
                place.peer(0, 1, 0, 0),
                block(chunk, turn, 1 - place.core),
                landed.at[chunk, turn],
                core_send.at[chunk, turn],
                core_recv.at[chunk, turn],
            )

        def along(chunk, turn):
            return send_to(
                place.peer(turn, 0, 0, 0),
                mine.at[chunk, turn],
                summed.at[chunk, turn - 1],
                layer_send.at[chunk, turn - 1],
                layer_recv.at[chunk, turn - 1],
            )

        order = [*range(1, layers), 0]
        for chunk in range(chunks):
            for turn in order:
                load(chunk, turn).start()
                sends.append(across(chunk, turn))
                sends[-1].start()
        yield
        for chunk in range(chunks):
            for turn in order[:-1]:
                load(chunk, turn).wait()
                across(chunk, turn).wait_recv()

                def merge(step, carry, chunk=chunk, turn=turn):
                    rows = pl.ds(pl.multiple_of(step * span, span), span)
                    value = mine[chunk, turn, rows].astype(F32)
                    value = value + landed[chunk, turn, rows].astype(F32)
                    mine[chunk, turn, rows] = value.astype(BF16)
                    return carry

                lax.fori_loop(0, part // span, merge, 0)
                sends.append(along(chunk, turn))
                sends[-1].start()
                yield
        for chunk in range(chunks):
            load(chunk, 0).wait()
            across(chunk, 0).wait_recv()
            for turn in order[:-1]:
                along(chunk, turn).wait_recv()

            def finish(step, carry, chunk=chunk):
                rows = pl.ds(pl.multiple_of(step * span, span), span)
                here = pl.ds(pl.multiple_of(chunk * part + step * span, span), span)
                value = mine[chunk, 0, rows].astype(F32) + landed[chunk, 0, rows].astype(F32)
                for turn in order[:-1]:
                    value = value + summed[chunk, turn - 1, rows].astype(F32)
                total[here] = value.astype(BF16)
                return carry

            lax.fori_loop(0, part // span, finish, 0)
            yield
        for copy in sends:
            copy.wait_send()


class Experts:
    SPAN = 256

    def __init__(self, own, upstream, mask, router, gate_all, up_all, down_all, layout):
        _, deep, wide = layout
        pieces, rows, width = own.shape
        halves, _, units = gate_all.shape
        tokens, lanes = mask.shape
        self.operands = [own, upstream, mask, router, gate_all, up_all, down_all]
        self.in_specs = [ANYWHERE, ANYWHERE, RESIDENT, RESIDENT] + [ANYWHERE] * 3
        self.outs = [
            jax.ShapeDtypeStruct((halves, width, units), BF16),
            jax.ShapeDtypeStruct((halves, width, units), BF16),
            jax.ShapeDtypeStruct((halves, units, width), BF16),
            jax.ShapeDtypeStruct((tokens, width), BF16),
            jax.ShapeDtypeStruct((tokens, lanes), F32),
            jax.ShapeDtypeStruct((pieces, rows, width), F32),
            jax.ShapeDtypeStruct((pieces, rows, lanes), F32),
        ]
        self.out_specs = [ANYWHERE] * 4 + [RESIDENT] * 3
        gathers = gather_scratch(pieces, deep, wide)
        scatters = scatter_scratch(rows, width, deep, wide)
        dots = scatter_scratch(rows, lanes, deep, wide)
        self.sizes = [len(gathers), len(scatters)]
        acts = pltpu.VMEM((halves, tokens, units), BF16)
        self.scratch = [
            pltpu.VMEM((tokens, width), BF16),
            pltpu.VMEM((tokens, width), BF16),
            acts,
            acts,
            acts,
            pltpu.VMEM((halves, width, units), BF16),
            pltpu.VMEM((halves, width, units), BF16),
            pltpu.VMEM((halves, units, width), BF16),
            pltpu.VMEM((tokens, width), BF16),
            pltpu.VMEM((tokens, lanes), F32),
            pltpu.VMEM((tokens, lanes), BF16),
            dma(3, halves),
            dma(3, halves),
            dma(2),
            *gathers,
            *scatters * pieces,
            *dots * pieces,
        ]
        self.steps = grid_steps(deep, wide)

    def run(
        self,
        place,
        own,
        upstream_in,
        mask,
        router,
        gate_all,
        up_all,
        down_all,
        gate_terms,
        up_terms,
        down_terms,
        out,
        share,
        total,
        dot_total,
        rows,
        upstream,
        hidden,
        gate_pre,
        up_pre,
        gate_weight,
        up_weight,
        down_weight,
        parts,
        dots,
        placed,
        load_sem,
        store_sem,
        local_sem,
        *scratch,
    ):
        pieces = own.shape[0]
        halves, _, units = hidden.shape
        tokens, width = rows.shape
        lanes = mask.shape[1]
        count = tokens // pieces
        span = self.SPAN
        shards = place.shards
        scratch = list(scratch)

        def take(number):
            return [scratch.pop(0) for _ in range(number)]

        inward = gather_steps(place, own, rows, *take(self.sizes[0]))
        scatters = [
            scatter_steps(place, parts, piece, total.at[piece], *take(self.sizes[1]))
            for piece in range(pieces)
        ]
        dot_scatters = [
            scatter_steps(place, placed, piece, dot_total.at[piece], *take(self.sizes[1]))
            for piece in range(pieces)
        ]
        running = []

        def others():
            for each in list(running):
                if next(each, END) is END:
                    running.remove(each)

        kept = (gate_weight, up_weight, down_weight)

        def load(half):
            return [
                pltpu.make_async_copy(source.at[half], kept[which].at[half], load_sem.at[which, half])
                for which, source in enumerate((gate_all, up_all, down_all))
            ]

        def store(which, half):
            target = (gate_terms, up_terms, down_terms)[which]
            return pltpu.make_async_copy(
                kept[which].at[half], target.at[half], store_sem.at[which, half]
            )

        def wait_all(copies):
            for copy in copies:
                copy.wait()

        def shares(piece):
            here = pl.ds(piece * count, count)
            known = mask[here, :]
            logits = dot(rows[here, :], router[...], NN)
            peak = jnp.max(jnp.where(known > 0, logits, MASK_FILL), axis=1, keepdims=True)
            exponent = jnp.where(known > 0, jnp.exp(jnp.minimum(logits - peak, 0.0)), 0.0)
            share[here, :] = exponent / jnp.sum(exponent, axis=1, keepdims=True)

        def units_of(piece):
            here = pl.ds(piece * count, count)
            which_lane = lax.broadcasted_iota(jnp.int32, (count, lanes), 1)
            for half in range(halves):
                if piece == 0:
                    wait_all(load(half))
                column = half * shards + place.me
                chosen = jnp.where(which_lane == column // 2, share[here, :], 0.0)
                weight = jnp.sum(chosen, axis=1, keepdims=True)
                for step in range(units // span):
                    there = pl.ds(step * span, span)
                    gate = dot(rows[here, :], gate_weight[half, :, there], NN)
                    up = dot(rows[here, :], up_weight[half, :, there], NN)
                    grad = dot(upstream[here, :], down_weight[half, there, :], NT)
                    sigmoid_gate = 1.0 / (1.0 + jnp.exp(-gate))
                    swish_gate = gate * sigmoid_gate
                    activated = swish_gate * up
                    products = jnp.sum(activated * grad, axis=1, keepdims=True)
                    dots[here, :] += jnp.where(which_lane == column, products, 0.0)
                    hidden[half, here, there] = (activated * weight).astype(BF16)
                    grad = grad * weight
                    gate_pre[half, here, there] = (
                        grad * up * (sigmoid_gate * (1.0 + gate * (1.0 - sigmoid_gate)))
                    ).astype(BF16)
                    up_pre[half, here, there] = (grad * swish_gate).astype(BF16)
                    yield

        def merge(piece):
            here = pl.ds(piece * count, count)
            for step in range(width // span):
                there = pl.ds(step * span, span)
                value = dot(gate_pre[0, here, :], gate_weight[0, there, :], NT)
                value = value + dot(up_pre[0, here, :], up_weight[0, there, :], NT)
                for half in range(1, halves):
                    value = value + dot(gate_pre[half, here, :], gate_weight[half, there, :], NT)
                    value = value + dot(up_pre[half, here, :], up_weight[half, there, :], NT)
                parts[here, there] = value.astype(BF16)
                yield

        def place_dots(piece):
            here = pl.ds(piece * count, count)
            value = dots[here, :]
            high = value.astype(BF16).astype(F32)
            low = pltpu.roll(value - high, lanes // 2, 1)
            placed[here, :] = (high + low).astype(BF16)

        def weights():
            ends = []

            def put(copy):
                copy.start()
                ends.append(copy)

            for which, grads in enumerate((gate_pre, up_pre)):
                for half in range(halves):
                    for step in range(units // span):
                        there = pl.ds(step * span, span)
                        kept[which][half, :, there] = dot(
                            rows[...], grads[half, :, there], TN
                        ).astype(BF16)
                        yield
                    put(store(which, half))
            for step in range(width // span):
                there = pl.ds(step * span, span)
                value = dot(hidden[0], down_weight[0, :, there], NN)
                for half in range(1, halves):
                    value = value + dot(hidden[half], down_weight[half, :, there], NN)
                rows[:, there] = value.astype(BF16)
                yield
            put(pltpu.make_async_copy(rows, out, local_sem.at[1]))
            for half in range(halves):
                for step in range(units // span):
                    there = pl.ds(step * span, span)
                    down_weight[half, there, :] = dot(
                        hidden[half, :, there], upstream[...], TN
                    ).astype(BF16)
                    yield
                put(store(2, half))
            wait_all(ends)

        next(inward)
        upstream_copy = pltpu.make_async_copy(upstream_in, upstream, local_sem.at[0])
        upstream_copy.start()
        for half in range(halves):
            start_all(load(half))
        dots[...] = jnp.zeros_like(dots)
        yield from until(inward, 1)
        upstream_copy.wait()
        running.append(inward)
        for piece in range(pieces):
            if piece:
                while inward in running:
                    others()
                    yield
                running.extend([dot_scatters[piece - 1], scatters[piece - 1]])
                next(dot_scatters[piece - 1])
                next(scatters[piece - 1])
            shares(piece)
            for index, _ in enumerate(units_of(piece)):
                if piece == 0 or index % 2:
                    others()
                yield
            place_dots(piece)
            for index, _ in enumerate(merge(piece)):
                if piece == 0 or index % 4 == 3:
                    others()
                yield
        running.extend([dot_scatters[-1], scatters[-1]])
        next(dot_scatters[-1])
        next(scatters[-1])
        for index, _ in enumerate(weights()):
            if index % 4 == 3:
                others()
                yield
        yield from together(*running)


class Columns:
    def __init__(self, weights, smalls, layout):
        groups, deep, wide = layout
        shards = deep * wide
        depth = weights[0].shape[0]
        self.operands, self.in_specs = [*weights, *smalls], [ANYWHERE] * 5
        self.outs = [
            jax.ShapeDtypeStruct((shards, groups, depth // groups, 3 * depth), BF16),
            *[jax.ShapeDtypeStruct((shards,) + small.shape, BF16) for small in smalls],
        ]
        self.out_specs = [ANYWHERE] * 3
        self.scratch = [
            dma(3, shards - 1),
            dma(3, shards - 1),
            dma(2, shards - 1),
            dma(2, shards - 1),
            dma(groups // 2 - 1),
            dma(groups // 2 - 1),
            dma(groups // 2),
            dma(groups // 2),
            dma(5),
        ]
        self.steps = shard_steps(deep, wide) | expert_steps(groups // 2)

    def run(
        self,
        place,
        query_weight,
        key_weight,
        value_weight,
        small,
        gains,
        projections,
        small_all,
        gains_all,
        weight_send,
        weight_recv,
        small_send,
        small_recv,
        layer_send,
        layer_recv,
        core_send,
        core_recv,
        local,
    ):
        weights = (query_weight, key_weight, value_weight)
        smalls = ((small, small_all), (gains, gains_all))
        layers, group, me = place.layers, place.group, place.me
        part = projections.shape[2]
        depth = query_weight.shape[0]
        steps = sorted(shard_steps(place.deep, place.wide))
        sends = []

        def block(which, target):
            return weights[which].at[
                pl.ds(pl.multiple_of(group * part, part), part),
                pl.ds(pl.multiple_of(target * depth, depth), depth),
            ]

        def slot(which, source):
            return projections.at[source, group, :, pl.ds(which * depth, depth)]

        def weight_copy(which, index):
            return send_to(
                place.peer(*steps[index]),
                block(which, place.peer(*steps[index])[1]),
                slot(which, me),
                weight_send.at[which, index],
                weight_recv.at[which, index],
            )

        def small_copy(which, index):
            return send_to(
                place.peer(*steps[index]),
                smalls[which][0],
                smalls[which][1].at[me],
                small_send.at[which, index],
                small_recv.at[which, index],
            )

        def slab_copy(peer, layer, core, send_sem, recv_sem):
            slab = projections.at[:, layer * 2 + core]
            return send_to(peer, slab, slab, send_sem, recv_sem)

        def layer_copy(step, layer):
            return slab_copy(
                place.peer(step, 0, 0, 0),
                layer,
                place.core,
                layer_send.at[step - 1],
                layer_recv.at[step - 1],
            )

        def core_copy(step, layer, core):
            return slab_copy(
                place.peer(0, 1, 0, 0), layer, core, core_send.at[step], core_recv.at[step]
            )

        here = [
            pltpu.make_async_copy(block(which, me), slot(which, me), local.at[which])
            for which in range(3)
        ]
        for which, (own, whole) in enumerate(smalls):
            here.append(pltpu.make_async_copy(own, whole.at[me], local.at[3 + which]))
        for copy in here:
            copy.start()
        for index in range(len(steps)):
            for which in range(3):
                sends.append(weight_copy(which, index))
                sends[-1].start()
            for which in (0, 1):
                sends.append(small_copy(which, index))
                sends[-1].start()
        yield
        for copy in here:
            copy.wait()
        for index in range(len(steps)):
            for which in range(3):
                weight_copy(which, index).wait_recv()
        for step in range(1, layers):
            sends.append(layer_copy(step, place.layer))
            sends[-1].start()
        sends.append(core_copy(0, place.layer, place.core))
        sends[-1].start()
        yield
        for step in range(1, layers):
            layer = lax.rem(place.layer + layers - step, layers)
            layer_copy(step, layer).wait_recv()
            sends.append(core_copy(step, layer, place.core))
            sends[-1].start()
            yield
        for step in range(layers):
            layer = lax.rem(place.layer + layers - step, layers)
            core_copy(step, layer, 1 - place.core).wait_recv()
            yield
        for index in range(len(steps)):
            for which in (0, 1):
                small_copy(which, index).wait_recv()
        for copy in sends:
            copy.wait_send()


class Rows:
    def __init__(self, terms, row_terms, tail, layout):
        groups, deep, wide = layout
        layers = groups // 2
        shards, _, part, width = terms.shape
        depth = row_terms.shape[2]
        self.operands = [terms, row_terms, tail]
        self.in_specs = [RESIDENT] * 3
        self.outs = [
            jax.ShapeDtypeStruct((groups, part, depth), BF16),
            jax.ShapeDtypeStruct(tail.shape[1:], F32),
            *[jax.ShapeDtypeStruct((groups, part, depth), BF16)] * 3,
        ]
        self.out_specs = [RESIDENT] * 5
        others = max(1, layers - 1)
        self.scratch = [
            pltpu.VMEM((groups, shards, part, width), BF16),
            pltpu.VMEM((layers, shards, part, width), BF16),
            pltpu.VMEM((others, shards, part, width), BF16),
            pltpu.VMEM((others, shards, part, width), BF16),
            pltpu.VMEM((shards, part, width), BF16),
            pltpu.VMEM((layers, part, depth), BF16),
            pltpu.VMEM((others, part, depth), BF16),
            pltpu.VMEM((others, part, depth), BF16),
            pltpu.VMEM(tail.shape, F32),
            pltpu.VMEM((groups,) + tail.shape[1:], F32),
            dma(2, layers),
            dma(2, layers),
            dma(2, others),
            dma(2, others),
            dma(shards - 1),
            dma(shards - 1),
            dma(2, others),
            dma(2, others),
            dma(2, layers),
            dma(2, layers),
            dma(shards - 1),
            dma(shards - 1),
            dma(groups - 1),
            dma(groups - 1),
        ]
        self.steps = shard_steps(deep, wide) | expert_steps(layers)
        self.steps |= {(layer, core, 0, 0) for layer in range(layers) for core in (0, 1)}
        self.steps -= {(0, 0, 0, 0)}

    def run(
        self,
        place,
        terms,
        row_terms,
        tail,
        whole_rows,
        tail_out,
        query_out,
        key_out,
        value_out,
        whole,
        landed,
        merged,
        summed,
        ready,
        landed_rows,
        merged_rows,
        summed_rows,
        tails,
        tail_sums,
        core_send,
        core_recv,
        layer_send,
        layer_recv,
        swap_send,
        swap_recv,
        out_send,
        out_recv,
        over_send,
        over_recv,
        tail_send,
        tail_recv,
        sum_send,
        sum_recv,
    ):
        layers, group, me, core = place.layers, place.group, place.me, place.core
        shards = place.shards
        steps = sorted(shard_steps(place.deep, place.wide))
        group_steps = [
            (layer, flip, 0, 0) for layer in range(layers) for flip in (0, 1) if layer or flip
        ]
        sends = []

        def start(copy):
            copy.start()
            sends.append(copy)

        def layer_at(turn):
            return lax.rem(place.layer + turn, layers)

        def tail_copy(index):
            peer = place.peer(*steps[index])
            return send_to(
                peer, tail.at[peer[1]], tails.at[me], tail_send.at[index], tail_recv.at[index]
            )

        def sum_copy(index):
            return send_to(
                place.peer(*group_steps[index]),
                tail_sums.at[group],
                tail_sums.at[group],
                sum_send.at[index],
                sum_recv.at[index],
            )

        def across(which, turn):
            entry = layer_at(turn) * 2 + 1 - core
            source = row_terms.at[entry] if which else terms.at[:, entry]
            target = landed_rows.at[turn] if which else landed.at[turn]
            return send_to(
                place.peer(0, 1, 0, 0),
                source,
                target,
                core_send.at[which, turn],
                core_recv.at[which, turn],
            )

        def along(which, turn):
            source = merged_rows.at[turn - 1] if which else merged.at[turn - 1]
            target = summed_rows.at[turn - 1] if which else summed.at[turn - 1]
            return send_to(
                place.peer(turn, 0, 0, 0),
                source,
                target,
                layer_send.at[which, turn - 1],
                layer_recv.at[which, turn - 1],
            )

        def swap(index):
            peer = place.peer(*steps[index])
            return send_to(
                peer,
                ready.at[peer[1]],
                whole.at[group, me],
                swap_send.at[index],
                swap_recv.at[index],
            )

        def out(which, turn, entry):
            slab = whole_rows.at[entry] if which else whole.at[entry]
            return send_to(
                place.peer(turn, 0, 0, 0),
                slab,
                slab,
                out_send.at[which, turn - 1],
                out_recv.at[which, turn - 1],
            )

        def over(which, turn, entry):
            slab = whole_rows.at[entry] if which else whole.at[entry]
            return send_to(
                place.peer(0, 1, 0, 0),
                slab,
                slab,
                over_send.at[which, turn],
                over_recv.at[which, turn],
            )

        order = [*range(1, layers), 0]
        for which in (0, 1):
            for turn in order:
                start(across(which, turn))
        for index in range(len(steps)):
            start(tail_copy(index))
        yield
        for which in (0, 1):
            for turn in order[:-1]:
                across(which, turn).wait_recv()
                entry = layer_at(turn) * 2 + core
                if which:
                    merged_rows[turn - 1] = (
                        row_terms[entry].astype(F32) + landed_rows[turn].astype(F32)
                    ).astype(BF16)
                else:
                    for shard in range(shards):
                        merged[turn - 1, shard] = (
                            terms[shard, entry].astype(F32) + landed[turn, shard].astype(F32)
                        ).astype(BF16)
                start(along(which, turn))
                yield
        for which in (0, 1):
            across(which, 0).wait_recv()
        for index in range(len(steps)):
            tail_copy(index).wait_recv()
        tails[me] = tail[me]
        tail_sum = tails[0]
        for shard in range(1, shards):
            tail_sum = tail_sum + tails[shard]
        tail_sums[group] = tail_sum
        for index in range(len(group_steps)):
            start(sum_copy(index))
        yield
        for turn in order[:-1]:
            along(0, turn).wait_recv()
        for shard in range(shards):
            value = terms[shard, group].astype(F32) + landed[0, shard].astype(F32)
            for turn in order[:-1]:
                value = value + summed[turn - 1, shard].astype(F32)
            ready[shard] = value.astype(BF16)
        for index in range(len(steps)):
            start(swap(index))
        whole[group, me] = ready[me]
        yield
        for turn in order[:-1]:
            along(1, turn).wait_recv()
        value = row_terms[group].astype(F32) + landed_rows[0].astype(F32)
        for turn in order[:-1]:
            value = value + summed_rows[turn - 1].astype(F32)
        whole_rows[group] = value.astype(BF16)
        for turn in order[:-1]:
            start(out(1, turn, group))
        start(over(1, 0, group))
        yield
        for index in range(len(steps)):
            swap(index).wait_recv()
        for turn in order[:-1]:
            start(out(0, turn, group))
        start(over(0, 0, group))
        yield
        for which in (1, 0):
            for turn in order[:-1]:
                entry = layer_at(layers - turn) * 2 + core
                out(which, turn, entry).wait_recv()
                start(over(which, turn, entry))
                yield
        for index in range(len(group_steps)):
            sum_copy(index).wait_recv()
        tail_sum = tail_sums[0]
        for index in range(1, place.groups):
            tail_sum = tail_sum + tail_sums[index]
        tail_out[...] = tail_sum
        depth = terms.shape[3] // 3
        for which in (1, 0):
            for turn in range(layers):
                entry = layer_at(layers - turn) * 2 + 1 - core
                over(which, turn, entry).wait_recv()
                yield
        for entry in range(place.groups):
            for shard in range(shards):
                here = pl.ds(shard * depth, depth)
                value = whole[entry, shard]
                query_out[entry, :, here] = value[:, :depth]
                key_out[entry, :, here] = value[:, depth : 2 * depth]
                value_out[entry, :, here] = value[:, 2 * depth :]
            yield
        for copy in sends:
            copy.wait_send()


def turn(values, cosine, sine):
    return values * cosine + pltpu.roll(values, HDIM // 2, 1) * sine


def head_forward(projected, place, gain, cosine, sine):
    proj = projected[:, place * HDIM : (place + 1) * HDIM]
    scale = rms_scale(proj)
    unit = proj * scale
    return scale, unit, turn(unit * gain, cosine, sine).astype(BF16)


def head_probs(query_rot, key_rot, seg_column, seg_row):
    scores = dot(query_rot, key_rot, NT) * (1.0 / math.sqrt(HDIM))
    scores = jnp.where(seg_column == seg_row, scores, MASK_FILL)
    exponent = jnp.exp(scores - jnp.max(scores, axis=-1, keepdims=True))
    return exponent * (1.0 / jnp.sum(exponent, axis=-1, keepdims=True))


def forward_steps(
    micro,
    hidden,
    projections,
    output_weight,
    gain,
    head_gains,
    cosine,
    sine,
    seg_column,
    seg_row,
    mixer,
    projected,
    attended,
    parts,
):
    span = seg_column.shape[1]
    depth = projections.shape[1] // 3
    heads = depth // HDIM
    tile = min(span, 256)
    rows = pl.ds(micro * span, span)
    for start in range(0, span, tile):
        here = pl.ds(micro * span + start, tile)
        values = hidden[here, :].astype(F32)
        mixer[here, :] = (values * rms_scale(values) * gain).astype(BF16)
    projected[rows, :] = dot(mixer[rows, :], projections[...], NN)
    yield
    for head in range(heads):
        own = projected[rows, :]
        _, _, query_rot = head_forward(own, head, head_gains[0], cosine[...], sine[...])
        _, _, key_rot = head_forward(own, heads + head, head_gains[1], cosine[...], sine[...])
        values = own[:, (2 * heads + head) * HDIM : (2 * heads + head + 1) * HDIM]
        probs = head_probs(query_rot, key_rot, seg_column[micro], seg_row[micro])
        attended[rows, head * HDIM : (head + 1) * HDIM] = dot(
            probs.astype(BF16), values.astype(BF16), NN
        ).astype(BF16)
        yield
    parts[rows, :] = dot(attended[rows, :], output_weight[...], NN).astype(BF16)
    yield


def backward_steps(
    micro,
    branch,
    projected,
    projections,
    output_weight,
    head_gains,
    cosine,
    sine,
    seg_column,
    seg_row,
    parts,
    gain_terms,
    attended_grad,
    projected_grad,
):
    span = seg_column.shape[1]
    heads = output_weight.shape[0] // HDIM
    scale = 1.0 / math.sqrt(HDIM)
    rows = pl.ds(micro * span, span)
    attended_grad[rows, :] = dot(branch[rows, :], output_weight[...], NT).astype(BF16)
    yield
    for head in range(heads):
        own = projected[rows, :]
        query_scale, query_unit, query_rot = head_forward(
            own, head, head_gains[0], cosine[...], sine[...]
        )
        key_scale, key_unit, key_rot = head_forward(
            own, heads + head, head_gains[1], cosine[...], sine[...]
        )
        values = own[:, (2 * heads + head) * HDIM : (2 * heads + head + 1) * HDIM]
        probs = head_probs(query_rot, key_rot, seg_column[micro], seg_row[micro])
        out_grad = attended_grad[rows, head * HDIM : (head + 1) * HDIM]
        prob_grad = dot(out_grad, values.astype(BF16), NT)
        row_delta = jnp.sum(probs * prob_grad, axis=-1, keepdims=True)
        score_grad = (probs * (prob_grad - row_delta)).astype(BF16)
        projected_grad[rows, (2 * heads + head) * HDIM : (2 * heads + head + 1) * HDIM] = dot(
            probs.astype(BF16), out_grad, TN
        ).astype(BF16)
        for which, (rot_grad, unit, unit_scale) in enumerate(
            (
                (dot(score_grad, key_rot, NN) * scale, query_unit, query_scale),
                (dot(score_grad, query_rot, TN) * scale, key_unit, key_scale),
            )
        ):
            unit_grad = turn(rot_grad, cosine[...], -sine[...])
            gain_terms[which : which + 1] += jnp.sum(unit_grad * unit, axis=0, keepdims=True)
            place = (which * heads + head) * HDIM
            projected_grad[rows, place : place + HDIM] = norm_back(
                unit_grad * head_gains[which], unit, unit_scale
            ).astype(BF16)
        yield
    parts[rows, :] = dot(projected_grad[rows, :], projections[...], NT).astype(BF16)
    yield


def weight_steps(branch, mixer, attended, projected_grad, projection_terms, output_terms):
    width = branch.shape[1]
    tile = min(512, width)
    for start in range(0, width, tile):
        here = pl.ds(start, tile)
        output_terms[:, here] = dot(attended[...], branch[:, here], TN).astype(BF16)
        projection_terms[here, :] = dot(mixer[:, here], projected_grad[...], TN).astype(BF16)
        yield


class AttentionForward:
    def __init__(
        self, weights, smalls, inputs, cotangent, output_weight, tables, segments, layout
    ):
        _, deep, wide = layout
        micros, rows, width = inputs.shape
        shards = deep * wide
        tokens = micros * shards * rows
        depth = output_weight.shape[0]
        self.columns = Columns(weights, smalls, layout)
        self.operands = [
            *self.columns.operands,
            inputs,
            cotangent,
            output_weight,
            *tables,
            *segments,
        ]
        self.in_specs = [*self.columns.in_specs, ANYWHERE, ANYWHERE, *[RESIDENT] * 5]
        self.outs = [
            *self.columns.outs[1:],
            jax.ShapeDtypeStruct((shards, depth, 3 * depth), BF16),
            jax.ShapeDtypeStruct((tokens, width), BF16),
            jax.ShapeDtypeStruct((tokens, width), BF16),
            jax.ShapeDtypeStruct((tokens, 3 * depth), F32),
            jax.ShapeDtypeStruct((tokens, depth), BF16),
            jax.ShapeDtypeStruct((micros, rows, width), F32),
        ]
        self.out_specs = [ANYWHERE, RESIDENT, RESIDENT, ANYWHERE, *[RESIDENT] * 4]
        gathers = gather_scratch(micros, deep, wide)
        scatters = scatter_scratch(rows, width, deep, wide)
        self.sizes = [len(self.columns.scratch), len(gathers), len(gathers), len(scatters)]
        columns_out = self.columns.outs[0]
        self.scratch = [
            pltpu.VMEM(columns_out.shape, BF16),
            pltpu.VMEM((tokens, width), BF16),
            pltpu.VMEM((tokens, width), BF16),
            pltpu.VMEM((1, width), F32),
            *self.columns.scratch,
            *gathers,
            *gathers,
            *scatters * micros,
        ]
        self.steps = self.columns.steps | grid_steps(deep, wide)

    def run(
        self,
        place,
        query_weight,
        key_weight,
        value_weight,
        small,
        gains,
        inputs,
        cotangent,
        output_weight,
        cosine,
        sine,
        seg_column,
        seg_row,
        small_all,
        gains_all,
        projections,
        upstream,
        mixer,
        projected,
        attended,
        total,
        swapped,
        hidden,
        parts,
        gain,
        *scratch,
    ):
        micros, shards, deep = inputs.shape[0], place.shards, place.deep
        scratch = list(scratch)

        def take(count):
            return [scratch.pop(0) for _ in range(count)]

        columns = self.columns.run(
            place,
            query_weight,
            key_weight,
            value_weight,
            small,
            gains,
            swapped,
            small_all,
            gains_all,
            *take(self.sizes[0]),
        )
        inward = gather_steps(place, inputs, hidden, *take(self.sizes[1]))
        upward = gather_steps(place, cotangent, upstream, *take(self.sizes[2]))
        scatters = [
            scatter_steps(place, parts, micro, total.at[micro], *take(self.sizes[3]))
            for micro in range(micros)
        ]
        next(columns)
        next(inward)
        next(columns)
        yield from until(inward, 1)
        yield from columns
        part, depth = swapped.shape[2], output_weight.shape[0]
        head_gains = jnp.zeros((1, 2 * HDIM), F32)
        for shard in range(shards):
            for group in range(place.groups):
                projections[shard, group * part : (group + 1) * part, :] = swapped[shard, group]
            known = gains_all[shard].astype(F32)
            gain[:, shard * depth : (shard + 1) * depth] = known[0:1, :depth]
            head_gains = head_gains + known[1:2, : 2 * HDIM]
        head_gains = (head_gains[:, :HDIM], head_gains[:, HDIM:])
        weight = projections[...].reshape(-1, projections.shape[2])
        running = []
        for micro in range(micros):
            for _ in forward_steps(
                micro,
                hidden,
                weight,
                output_weight,
                gain[...],
                head_gains,
                cosine,
                sine,
                seg_column,
                seg_row,
                mixer,
                projected,
                attended,
                parts,
            ):
                for each in list(running):
                    if next(each, END) is END:
                        running.remove(each)
                if micro + 1 < micros:
                    next(inward, END)
                yield
            if micro + 1 < micros:
                yield from until(inward, micro + 2)
            running.append(scatters[micro])
            next(scatters[micro])
        running.append(upward)
        yield from inward
        yield from together(*running)


class AttentionBackward:
    def __init__(
        self,
        branch,
        mixer,
        projected,
        attended,
        projections,
        output_weight,
        head_gains,
        tables,
        segments,
        beside,
        layout,
    ):
        _, deep, wide = layout
        micros, rows, width = branch.shape
        tokens = micros * deep * wide * rows
        depth = output_weight.shape[0]
        self.beside = beside
        self.operands = [
            branch,
            mixer,
            projected,
            attended,
            projections,
            output_weight,
            head_gains,
            *tables,
            *segments,
            *[operand for part in beside for operand in part.operands],
        ]
        self.in_specs = [ANYWHERE] + [RESIDENT] * 10
        self.in_specs += [spec for part in beside for spec in part.in_specs]
        self.outs = [
            jax.ShapeDtypeStruct((width, 3 * depth), BF16),
            jax.ShapeDtypeStruct((depth, width), BF16),
            jax.ShapeDtypeStruct((8, HDIM), F32),
            jax.ShapeDtypeStruct((micros, rows, width), F32),
            *[out for part in beside for out in part.outs],
        ]
        self.out_specs = [RESIDENT] * 4 + [spec for part in beside for spec in part.out_specs]
        gathers = gather_scratch(micros, deep, wide)
        scatters = scatter_scratch(rows, width, deep, wide)
        self.sizes = [len(gathers), len(scatters)]
        self.scratch = [
            pltpu.VMEM((tokens, width), BF16),
            pltpu.VMEM((tokens, width), BF16),
            pltpu.VMEM((tokens, depth), BF16),
            pltpu.VMEM((tokens, 3 * depth), BF16),
            *gathers,
            *scatters * micros,
            *[buffer for part in beside for buffer in part.scratch],
        ]
        self.steps = grid_steps(deep, wide).union(*(part.steps for part in beside))

    def run(self, place, *refs):
        refs = list(refs)

        def take(count):
            return [refs.pop(0) for _ in range(count)]

        (
            branch,
            mixer,
            projected,
            attended,
            projections,
            output_weight,
            head_gains,
            cosine,
            sine,
            seg_column,
            seg_row,
        ) = take(11)
        beside_in = [take(len(part.operands)) for part in self.beside]
        projection_terms, output_terms, gain_terms, total = take(4)
        beside_out = [take(len(part.outs)) for part in self.beside]
        branch_all, parts, attended_grad, projected_grad = take(4)
        micros = branch.shape[0]
        inward = gather_steps(place, branch, branch_all, *take(self.sizes[0]))
        scatters = [
            scatter_steps(place, parts, micro, total.at[micro], *take(self.sizes[1]))
            for micro in range(micros)
        ]
        sides = [
            part.run(place, *own_in, *own_out, *take(len(part.scratch)))
            for part, own_in, own_out in zip(self.beside, beside_in, beside_out, strict=True)
        ]
        next(inward)
        for side in sides[:1]:
            next(side)
            for _ in range(2):
                next(inward)
                next(side)
        for side in sides[1:]:
            next(side)
        gain_terms[...] = jnp.zeros_like(gain_terms)
        gains = (head_gains[0:1], head_gains[1:2])
        yield from until(inward, 1)
        for side in sides[1:]:
            next(side)
            next(side)
        running = []
        for micro in range(micros):
            for _ in backward_steps(
                micro,
                branch_all,
                projected,
                projections,
                output_weight,
                gains,
                cosine,
                sine,
                seg_column,
                seg_row,
                parts,
                gain_terms,
                attended_grad,
                projected_grad,
            ):
                for each in list(running):
                    if next(each, END) is END:
                        running.remove(each)
                if micro + 1 < micros:
                    next(inward, END)
                yield
            if micro + 1 < micros:
                yield from until(inward, micro + 2)
            running.append(scatters[micro])
            next(scatters[micro])
        running.append(inward)
        running.append(
            weight_steps(
                branch_all, mixer, attended, projected_grad, projection_terms, output_terms
            )
        )
        yield from together(*running)
        for side in sides:
            yield from side


def units_kernel(
    span,
    rows_ref,
    upstream_ref,
    share_ref,
    gate_ref,
    up_ref,
    down_ref,
    hidden_ref,
    gate_pre_ref,
    up_pre_ref,
    dot_ref,
):
    half = pl.program_id(0)
    half_width = gate_ref.shape[2]
    lanes = lax.broadcasted_iota(jnp.int32, share_ref.shape, 1)
    share = jnp.sum(jnp.where(lanes == half, share_ref[...], 0.0), axis=1, keepdims=True)

    def body(step, carry):
        units = pl.ds(pl.multiple_of(step * span, span), span)
        gate_pre = dot(rows_ref[...], gate_ref[0, :, units], NN)
        up_pre = dot(rows_ref[...], up_ref[0, :, units], NN)
        units_grad = dot(upstream_ref[...], down_ref[0, units, :], NT)
        sigmoid_gate = 1.0 / (1.0 + jnp.exp(-gate_pre))
        swish_gate = gate_pre * sigmoid_gate
        activated = swish_gate * up_pre
        dots = jnp.sum(activated * units_grad, axis=1, keepdims=True)
        dot_ref[...] += jnp.where(lanes == half, dots, 0.0)
        hidden_ref[0, :, units] = (activated * share).astype(BF16)
        weighted = units_grad * share
        gate_pre_ref[0, :, units] = (
            weighted * up_pre * (sigmoid_gate * (1.0 + gate_pre * (1.0 - sigmoid_gate)))
        ).astype(BF16)
        up_pre_ref[0, :, units] = (weighted * swish_gate).astype(BF16)
        return carry

    @pl.when(half == 0)
    def _():
        dot_ref[...] = jnp.zeros_like(dot_ref)

    lax.fori_loop(0, half_width // span, body, 0)


def expert_units(rows, upstream, share, gate_all, up_all, down_all):
    tokens, width = rows.shape
    halves, _, units = gate_all.shape

    def each(*shape):
        return pl.BlockSpec((1,) + shape, lambda half: (half,) + (0,) * len(shape))

    whole = pl.BlockSpec(memory_space=pltpu.VMEM)
    return pl.pallas_call(
        functools.partial(units_kernel, 256 if tokens <= 1024 else 128),
        grid=(halves,),
        in_specs=[whole, whole, whole, each(width, units), each(width, units), each(units, width)],
        out_specs=[each(tokens, units), each(tokens, units), each(tokens, units), whole],
        out_shape=[
            jax.ShapeDtypeStruct((halves, tokens, units), BF16),
            jax.ShapeDtypeStruct((halves, tokens, units), BF16),
            jax.ShapeDtypeStruct((halves, tokens, units), BF16),
            jax.ShapeDtypeStruct(share.shape, F32),
        ],
        compiler_params=pltpu.CompilerParams(vmem_limit_bytes=VMEM_LIMIT),
        cost_estimate=pl.CostEstimate(
            flops=6 * tokens * width * units * halves,
            bytes_accessed=6 * width * units * halves,
            transcendentals=0,
        ),
    )(rows, upstream, share, gate_all, up_all, down_all)


def merge_kernel(gate_pre_ref, up_pre_ref, gate_ref, up_ref, grad_ref):
    halves = gate_pre_ref.shape[0]
    grad = dot(gate_pre_ref[0], gate_ref[0], NT) + dot(up_pre_ref[0], up_ref[0], NT)
    for half in range(1, halves):
        grad = grad + dot(gate_pre_ref[half], gate_ref[half], NT)
        grad = grad + dot(up_pre_ref[half], up_ref[half], NT)
    grad_ref[...] = grad.astype(BF16)


def expert_merge(gate_pre, up_pre, gate_all, up_all):
    halves, tokens, units = gate_pre.shape
    width = gate_all.shape[1]
    span = 256
    batch = min(tokens, 1024)
    slab = pl.BlockSpec(
        (halves, batch, units), lambda turn, step: (0, turn, 0), pipeline_mode=pl.Buffered(1)
    )
    tile = pl.BlockSpec((halves, span, units), lambda turn, step: (0, step, 0))
    return pl.pallas_call(
        merge_kernel,
        grid=(tokens // batch, width // span),
        in_specs=[slab, slab, tile, tile],
        out_specs=pl.BlockSpec((batch, span), lambda turn, step: (turn, step)),
        out_shape=jax.ShapeDtypeStruct((tokens, width), BF16),
        compiler_params=pltpu.CompilerParams(vmem_limit_bytes=VMEM_LIMIT),
        cost_estimate=pl.CostEstimate(
            flops=4 * tokens * width * units * halves,
            bytes_accessed=4 * width * units * halves,
            transcendentals=0,
        ),
    )(gate_pre, up_pre, gate_all, up_all)


def output_kernel(hidden_ref, down_ref, out_ref):
    halves = hidden_ref.shape[0]
    out = dot(hidden_ref[0], down_ref[0], NN)
    for half in range(1, halves):
        out = out + dot(hidden_ref[half], down_ref[half], NN)
    out_ref[...] = out.astype(BF16)


def expert_output(hidden, down_all):
    halves, tokens, units = hidden.shape
    width = down_all.shape[2]
    span = 256
    batch = min(tokens, 1024)
    slab = pl.BlockSpec(
        (halves, batch, units), lambda turn, step: (0, turn, 0), pipeline_mode=pl.Buffered(1)
    )
    return pl.pallas_call(
        output_kernel,
        grid=(tokens // batch, width // span),
        in_specs=[slab, pl.BlockSpec((halves, units, span), lambda turn, step: (0, 0, step))],
        out_specs=pl.BlockSpec((batch, span), lambda turn, step: (turn, step)),
        out_shape=jax.ShapeDtypeStruct((tokens, width), BF16),
        compiler_params=pltpu.CompilerParams(vmem_limit_bytes=VMEM_LIMIT),
        cost_estimate=pl.CostEstimate(
            flops=2 * tokens * width * units * halves,
            bytes_accessed=2 * width * units * halves,
            transcendentals=0,
        ),
    )(hidden, down_all)


def weights_kernel(
    span,
    rows_ref,
    upstream_ref,
    hidden_ref,
    gate_pre_ref,
    up_pre_ref,
    gate_grad_ref,
    up_grad_ref,
    down_grad_ref,
):
    def body(step, carry):
        units = pl.ds(pl.multiple_of(step * span, span), span)
        gate_grad_ref[0, :, units] = dot(rows_ref[...], gate_pre_ref[0, :, units], TN).astype(BF16)
        up_grad_ref[0, :, units] = dot(rows_ref[...], up_pre_ref[0, :, units], TN).astype(BF16)
        down_grad_ref[0, units, :] = dot(
            hidden_ref[0, :, units], upstream_ref[...], TN
        ).astype(BF16)
        return carry

    lax.fori_loop(0, gate_grad_ref.shape[2] // span, body, 0)


def expert_weights(rows, upstream, hidden, gate_pre, up_pre):
    tokens, width = rows.shape
    halves, _, units = hidden.shape

    def each(*shape):
        return pl.BlockSpec((1,) + shape, lambda half: (half,) + (0,) * len(shape))

    whole = pl.BlockSpec(memory_space=pltpu.VMEM)
    slab = each(tokens, units)
    return pl.pallas_call(
        functools.partial(weights_kernel, 256),
        grid=(halves,),
        in_specs=[whole, whole, slab, slab, slab],
        out_specs=[each(width, units), each(width, units), each(units, width)],
        out_shape=[
            jax.ShapeDtypeStruct((halves, width, units), BF16),
            jax.ShapeDtypeStruct((halves, width, units), BF16),
            jax.ShapeDtypeStruct((halves, units, width), BF16),
        ],
        compiler_params=pltpu.CompilerParams(vmem_limit_bytes=VMEM_LIMIT),
        cost_estimate=pl.CostEstimate(
            flops=6 * tokens * width * units * halves,
            bytes_accessed=6 * width * units * halves,
            transcendentals=0,
        ),
    )(rows, upstream, hidden, gate_pre, up_pre)


def experts_in_turn(
    expert_input, upstream_all, choose, router_full, gate_all, up_all, down_all, layout, micros
):
    groups, deep, wide = layout
    shards = deep * wide
    experts = router_full.shape[1]
    shard_place = lax.axis_index("shard")
    ((expert_all,),) = fuse([Gather(expert_input, layout)], layout, 2, "experts_in")
    logits = jnp.dot(expert_all, router_full, preferred_element_type=F32)
    share = softmax_rows(jnp.sum(choose * logits[:, None, :], axis=-1))
    share_wide = jnp.sum(choose * share[:, :, None], axis=1)
    served = (jnp.arange(groups, dtype=jnp.int32) * shards + shard_place) // 2
    serves = (served[:, None] == jnp.arange(experts, dtype=jnp.int32)).astype(F32)
    share_own = jnp.pad(
        jnp.dot(share_wide, serves.T, precision=PRECISE), ((0, 0), (0, 128 - groups))
    )
    activated, gate_pre, up_pre, dots = expert_units(
        expert_all, upstream_all, share_own, gate_all, up_all, down_all
    )
    expert_grad_parts = expert_merge(gate_pre, up_pre, gate_all, up_all)
    gate_pre, expert_grad_parts = lax.optimization_barrier((gate_pre, expert_grad_parts))
    gate_terms, up_terms, down_terms = expert_weights(
        expert_all, upstream_all, activated, gate_pre, up_pre
    )
    out_parts = expert_output(activated, down_all)

    halves = groups * shards
    lanes = halves + -halves % 128
    columns = jnp.arange(groups, dtype=jnp.int32) * shards + shard_place
    columns = (columns[:, None] == jnp.arange(lanes, dtype=jnp.int32)).astype(F32)
    placed = jnp.dot(dots[:, :groups], columns, precision=PRECISE)
    placed_high = placed.astype(BF16)
    placed_low = (placed - placed_high.astype(F32)).astype(BF16)
    placed = jnp.concatenate([placed_high, placed_low], axis=1)
    (dot_total,), (expert_grad,) = fuse(
        [Scatter(placed, micros, layout), Scatter(expert_grad_parts, micros, layout)],
        layout,
        3,
        "experts_out",
    )
    return gate_terms, up_terms, down_terms, out_parts, share, expert_grad, dot_total, lanes


def per_device(
    groups,
    shards,
    wide,
    inputs,
    segment_ids,
    routes,
    cotangent,
    query_weight,
    key_weight,
    value_weight,
    output_weight,
    router_weight,
    attention_gain,
    expert_gain,
    query_gain,
    key_gain,
    gate_weight,
    up_weight,
    down_weight,
):
    micros, rows, width = inputs.shape
    deep = shards // wide
    span = shards * rows
    tokens = micros * span
    experts = router_weight.shape[1]
    column_width = width // shards
    shard_place = lax.axis_index("shard")
    layout = (groups, deep, shards // deep)

    gate_all = lax.all_gather(gate_weight, "expert", axis=0, tiled=True)
    up_all = lax.all_gather(up_weight, "expert", axis=0, tiled=True)
    down_all = lax.all_gather(down_weight, "expert", axis=0, tiled=True)

    cuts = [column_width * experts, routes.size]
    small_own = jnp.concatenate(
        [router_weight.reshape(-1), routes.reshape(-1).astype(BF16)]
    )
    small_own = jnp.pad(small_own, (0, -sum(cuts) % 2048)).reshape(-1, 128)

    def placed_row(gain):
        row = jnp.zeros((gain.shape[0] * shards,), BF16)
        return lax.dynamic_update_slice_in_dim(row, gain, shard_place * gain.shape[0], 0)

    gains_own = jnp.zeros((16, max(2 * column_width, 2 * HDIM)), BF16)
    gains_own = gains_own.at[0, : 2 * column_width].set(
        jnp.concatenate([attention_gain, expert_gain])
    )
    gains_own = gains_own.at[1, : 2 * HDIM].set(
        jnp.concatenate([placed_row(query_gain), placed_row(key_gain)])
    )

    tables = rotary(span)
    segments = (segment_ids[:, :, None], segment_ids[:, None, :])
    (
        (
            small,
            gains_all,
            projections,
            upstream_all,
            mixer_all,
            projected,
            attended,
            middle_total,
        ),
    ) = fuse(
        [
            AttentionForward(
                (query_weight, key_weight, value_weight),
                (small_own, gains_own),
                inputs,
                cotangent,
                output_weight,
                tables,
                segments,
                layout,
            )
        ],
        layout,
        0,
        "attention_forward",
    )
    projections = projections.reshape(width, 3 * column_width)
    small = small.reshape(shards, -1)
    router_full = small[:, : cuts[0]].reshape(width, experts)
    routes_all = small[:, cuts[0] : sum(cuts)].reshape(shards, micros, rows, -1)
    routes_all = routes_all.transpose(1, 0, 2, 3).reshape(tokens, -1).astype(jnp.int32)
    attn_gain = gains_all[:, 0, :column_width].reshape(-1).astype(F32)
    expert_gain_full = gains_all[:, 0, column_width : 2 * column_width].reshape(-1).astype(F32)
    head_gains = jnp.sum(gains_all[:, 1, : 2 * HDIM].astype(F32), axis=0).reshape(2, HDIM)
    head_gains = jnp.pad(head_gains, ((0, 6), (0, 0)))
    hidden = inputs.astype(F32)
    middle = hidden + middle_total

    scale_second = rms_scale(middle)
    normed_second = middle * scale_second
    expert_input = (normed_second * expert_gain_full).astype(BF16)
    early = tokens <= 1024 and 4 * groups * shards <= 256
    choose = (routes_all[:, :, None] == jnp.arange(experts, dtype=jnp.int32)).astype(F32)
    if early:
        mask = jnp.pad(jnp.sum(choose, axis=1), ((0, 0), (0, 128 - experts)))
        router_wide = jnp.pad(router_full, ((0, 0), (0, 128 - experts)))
        (
            (
                gate_terms,
                up_terms,
                down_terms,
                out_parts,
                share_wide,
                expert_grad,
                dot_total,
            ),
        ) = fuse(
            [
                Experts(
                    expert_input,
                    upstream_all,
                    mask,
                    router_wide,
                    gate_all,
                    up_all,
                    down_all,
                    layout,
                )
            ],
            layout,
            2,
            "experts",
        )
        share = jnp.sum(choose * share_wide[:, None, :experts], axis=-1)
        half_lanes = 64
    else:
        (
            gate_terms,
            up_terms,
            down_terms,
            out_parts,
            share,
            expert_grad,
            dot_total,
            half_lanes,
        ) = experts_in_turn(
            expert_input,
            upstream_all,
            choose,
            router_full,
            gate_all,
            up_all,
            down_all,
            layout,
            micros,
        )

    def own_rows(values):
        return lax.dynamic_slice_in_dim(
            values.reshape((micros, span) + values.shape[1:]), shard_place * rows, rows, 1
        )

    own_choose, own_share = own_rows(choose), own_rows(share)
    halves = groups * shards
    share_grad_wide = (
        dot_total[..., :halves] + dot_total[..., half_lanes : half_lanes + halves]
    )
    share_grad_wide = share_grad_wide.reshape(micros, rows, experts, 2).sum(axis=-1)
    share_grad = jnp.sum(own_choose * share_grad_wide[:, :, None, :], axis=-1)
    chosen_grad = own_share * (
        share_grad - jnp.sum(own_share * share_grad, axis=-1, keepdims=True)
    )
    own_logits_grad = jnp.sum(own_choose * chosen_grad[..., None], axis=2)
    expert_grad = expert_grad + jnp.dot(
        own_logits_grad, router_full.astype(F32).T, precision=PRECISE
    )
    expert_gain_term = jnp.sum(expert_grad * normed_second, axis=(0, 1))
    middle_grad = cotangent.astype(F32) + norm_back(
        expert_grad * expert_gain_full, normed_second, scale_second
    )
    router_term = jnp.einsum(
        "mtd,mte->de", expert_input.astype(F32), own_logits_grad, precision=PRECISE
    )

    beside = []
    if early:
        beside = [ExpertScatter(gate_terms, layout), ExpertScatter(up_terms, layout)]
    ((projection_terms, output_term, head_gain_terms, mixer_grad, *side_grads),) = fuse(
        [
            AttentionBackward(
                middle_grad.astype(BF16),
                mixer_all,
                projected,
                attended,
                projections,
                output_weight,
                head_gains,
                tables,
                segments,
                beside,
                layout,
            )
        ],
        layout,
        4,
        "attention_backward",
    )
    scale_first = rms_scale(hidden)
    normed_first = hidden * scale_first
    attn_gain_term = jnp.sum(mixer_grad * normed_first, axis=(0, 1))
    hidden_grad = middle_grad + norm_back(mixer_grad * attn_gain, normed_first, scale_first)

    part = column_width // groups
    tail = jnp.concatenate(
        [
            term.reshape(shards, -1)
            for term in (
                router_term,
                attn_gain_term,
                expert_gain_term,
                head_gain_terms[0],
                head_gain_terms[1],
            )
        ],
        axis=1,
    )
    tail = jnp.pad(tail, ((0, 0), (0, -tail.shape[1] % 1024))).reshape(shards, -1, 128)
    (output_grad, tail, query_grad, key_grad, value_grad), (outs,), *last_grads = fuse(
        [
            Rows(
                projection_terms.reshape(shards, groups, part, 3 * column_width),
                output_term.reshape(groups, part, width),
                tail,
                layout,
            ),
            Scatter(out_parts, micros, layout),
            *([ExpertScatter(down_terms, layout)] if early else []),
        ],
        layout,
        5,
        "exit",
    )
    if early:
        gate_grad, up_grad = side_grads
        ((down_grad,),) = last_grads
    else:
        gate_grad, up_grad, down_grad = (
            fuse([ExpertScatter(terms, layout)], layout, 6 + index, "weights")[0][0]
            for index, terms in enumerate((gate_terms, up_terms, down_terms))
        )
    result = middle + outs
    tail = tail.reshape(-1)
    lengths = [column_width * experts] + [column_width] * 2 + [HDIM // shards] * 2
    starts = [sum(lengths[:place]) for place in range(len(lengths))]
    tails = [
        tail[start : start + length] for start, length in zip(starts, lengths, strict=True)
    ]
    return (
        result.astype(BF16),
        hidden_grad.astype(BF16),
        query_grad.astype(F32).reshape(column_width, width),
        key_grad.astype(F32).reshape(column_width, width),
        value_grad.astype(F32).reshape(column_width, width),
        output_grad.astype(F32).reshape(column_width, width),
        tails[0].reshape(column_width, experts),
        tails[1],
        tails[2],
        tails[3],
        tails[4],
        gate_grad.astype(F32)[None],
        up_grad.astype(F32)[None],
        down_grad.astype(F32)[None],
    )


def solution(mesh):
    groups, shards = mesh.shape["expert"], mesh.shape["shard"]
    wide = shards // 4 if shards % 4 == 0 else 1
    in_specs = (
        P(None, ("expert", "shard"), None),
        P(None, "expert"),
        P(None, ("expert", "shard"), None),
        P(None, ("expert", "shard"), None),
        P("shard", None),
        P("shard", None),
        P("shard", None),
        P("shard", None),
        P("shard", None),
        P("shard"),
        P("shard"),
        P("shard"),
        P("shard"),
        P(("expert", "shard"), None, None),
        P(("expert", "shard"), None, None),
        P(("expert", "shard"), None, None),
    )
    out_specs = (
        P(None, ("expert", "shard"), None),
        P(None, ("expert", "shard"), None),
        P("shard", None),
        P("shard", None),
        P("shard", None),
        P("shard", None),
        P("shard", None),
        P("shard"),
        P("shard"),
        P("shard"),
        P("shard"),
        P(("expert", "shard"), None, None),
        P(("expert", "shard"), None, None),
        P(("expert", "shard"), None, None),
    )
    return jax.shard_map(
        functools.partial(per_device, groups, shards, wide),
        mesh=mesh,
        in_specs=in_specs,
        out_specs=out_specs,
        check_vma=False,
    )
```

```python
import functools
import math

import jax
import jax.numpy as jnp
from jax import lax
from jax.experimental import pallas as pl
from jax.experimental.pallas import tpu as pltpu
from jax.sharding import PartitionSpec as P

HDIM = 128
EPSILON = 1e-05
ROPE_BASE = 10000.0
MASK_FILL = -1e30
PRECISE = lax.Precision.HIGHEST
MESH = pl.DeviceIdType.MESH
F32 = jnp.float32
BF16 = jnp.bfloat16
NN = (((1,), (0,)), ((), ()))
NT = (((1,), (1,)), ((), ()))
TN = (((0,), (0,)), ((), ()))
VMEM_LIMIT = 63 << 20
LINK_COST = pl.CostEstimate(flops=60 * 10**9, bytes_accessed=8 << 20, transcendentals=0)


def dot(left, right, dims):
    return lax.dot_general(left, right, dims, preferred_element_type=F32)


def rms_scale(values):
    return lax.rsqrt(jnp.mean(values * values, axis=-1, keepdims=True) + EPSILON)


def norm_back(normed_grad, normed, inv_scale):
    return inv_scale * (
        normed_grad - normed * jnp.mean(normed_grad * normed, axis=-1, keepdims=True)
    )


def rotary(span):
    steps = jnp.arange(HDIM // 2, dtype=jnp.int32).astype(F32)
    freqs = jnp.power(ROPE_BASE, -2.0 * steps / HDIM)
    theta = jnp.arange(span, dtype=jnp.int32).astype(F32)[:, None] * freqs[None, :]
    cosine, sine = jnp.cos(theta), jnp.sin(theta)
    return (
        jnp.concatenate([cosine, cosine], axis=1),
        jnp.concatenate([-sine, sine], axis=1),
    )


def softmax_rows(scores):
    row_peak = jnp.max(scores, axis=-1, keepdims=True)
    exponent = jnp.exp(scores - row_peak)
    return exponent / jnp.sum(exponent, axis=-1, keepdims=True)


class Place:
    def __init__(self, groups, deep, wide):
        self.deep, self.wide = deep, wide
        self.shards, self.groups, self.layers = deep * wide, groups, groups // 2
        group, me = lax.axis_index("expert"), lax.axis_index("shard")
        self.group, self.me = group, me
        self.layer, self.core = group // 2, lax.rem(group, 2)
        self.row, self.column = me // wide, lax.rem(me, wide)

    def peer(self, layer_step=0, core_step=0, row_step=0, column_step=0):
        group, me = self.group, self.me
        if layer_step or core_step:
            group = lax.rem(self.layer + layer_step, self.layers) * 2 + (
                1 - self.core if core_step else self.core
            )
        if row_step or column_step:
            me = lax.rem(self.row + row_step, self.deep) * self.wide + lax.rem(
                self.column + column_step, self.wide
            )
        return group, me

    def grid_place(self, row_step, column_step):
        return self.peer(0, 0, row_step, column_step)[1]

    def back(self, layer_step=0, core_step=0, row_step=0, column_step=0):
        return self.peer(
            (self.layers - layer_step) % self.layers,
            core_step,
            (self.deep - row_step) % self.deep,
            (self.wide - column_step) % self.wide,
        )


def send_to(peer, source, target, send_sem, recv_sem):
    return pltpu.make_async_remote_copy(
        src_ref=source,
        dst_ref=target,
        send_sem=send_sem,
        recv_sem=recv_sem,
        device_id=peer,
        device_id_type=MESH,
    )


def dma(*shape):
    return pltpu.SemaphoreType.DMA(tuple(max(1, size) for size in shape))


ANYWHERE = pl.BlockSpec(memory_space=pl.ANY)
RESIDENT = pl.BlockSpec(memory_space=pltpu.VMEM)


def grid_steps(deep, wide):
    steps = {(0, 0, row, 0) for row in range(1, deep)}
    return steps | {(0, 0, 0, column) for column in range(1, wide)}


def shard_steps(deep, wide):
    return {
        (0, 0, row, column) for row in range(deep) for column in range(wide) if row or column
    }


def expert_steps(layers):
    return {(step, 0, 0, 0) for step in range(1, layers)} | {(0, 1, 0, 0)}


def fuse(parts, layout, collective_id, name):
    groups, deep, wide = layout
    operands = [operand for part in parts for operand in part.operands]
    in_specs = [spec for part in parts for spec in part.in_specs]
    out_shape = [out for part in parts for out in part.outs]
    out_specs = [spec for part in parts for spec in part.out_specs]
    scratch = [buffer for part in parts for buffer in part.scratch]
    steps = sorted(set().union(*(part.steps for part in parts)))

    def kernel(*refs):
        place = Place(groups, deep, wide)
        barrier = pltpu.get_barrier_semaphore()
        for step in steps:
            pl.semaphore_signal(
                barrier, inc=1, device_id=place.peer(*step), device_id_type=MESH
            )
        pl.semaphore_wait(barrier, len(steps))
        ins = list(refs[: len(operands)])
        outs = list(refs[len(operands) : len(operands) + len(out_shape)])
        buffers = list(refs[len(operands) + len(out_shape) :])
        running = []
        for part in parts:
            part_ins = [ins.pop(0) for _ in part.operands]
            part_outs = [outs.pop(0) for _ in part.outs]
            part_buffers = [buffers.pop(0) for _ in part.scratch]
            running.append(part.run(place, *part_ins, *part_outs, *part_buffers))
        late = [
            run for run, part in zip(running, parts, strict=True) if isinstance(part, ExpertScatter)
        ]
        first = [run for run in running if run not in late]
        for run in late:
            next(run)
        for index, _ in enumerate(together(*first)):
            if index in (1, 7):
                for run in late:
                    next(run)
        for run in late:
            for _ in run:
                pass

    results = pl.pallas_call(
        kernel,
        out_shape=out_shape,
        in_specs=in_specs,
        out_specs=out_specs,
        scratch_shapes=scratch,
        compiler_params=pltpu.CompilerParams(
            collective_id=collective_id, has_side_effects=True, vmem_limit_bytes=VMEM_LIMIT
        ),
        cost_estimate=LINK_COST,
        name=name,
    )(*operands)
    results = list(results)
    return [[results.pop(0) for _ in part.outs] for part in parts]


END = object()


def together(*runs):
    runs = list(runs)
    while runs:
        for run in list(runs):
            if next(run, END) is END:
                runs.remove(run)
        yield


def until(run, token):
    for value in run:
        if value == token:
            return
        yield


def gather_scratch(pieces, deep, wide):
    return [
        dma(pieces, 2, deep - 1),
        dma(pieces, 2, deep - 1),
        dma(pieces, 2 * deep, wide - 1),
        dma(pieces, 2 * deep, wide - 1),
        dma(1),
    ]


def start_all(copies):
    for copy in copies:
        copy.start()


def end_all(copies):
    for copy in copies:
        copy.wait_send()


def gather_steps(place, own, whole, row_send, row_recv, col_send, col_recv, local):
    pieces, rows, _ = own.shape
    deep, wide, shards = place.deep, place.wide, place.shards
    row, column = place.row, place.column
    ends = []

    def slot(piece, source_row, source_column):
        source = piece * shards + source_row * wide + source_column
        return whole.at[pl.ds(pl.multiple_of(source * rows, rows), rows)]

    def known(piece, step, source_row):
        return slot(piece, source_row, column) if step else own.at[piece]

    def hop(piece, way, step, source_row):
        return send_to(
            (place.group, (row + 1 - 2 * way) * wide + column),
            known(piece, step, source_row),
            slot(piece, source_row, column),
            row_send.at[piece, way, step],
            row_recv.at[piece, way, step],
        )

    def across(piece, step, way, move, source_row, source_column):
        key = 2 * step - 1 + way if step else 0
        return send_to(
            place.peer(0, 0, 0, move),
            known(piece, step, source_row),
            slot(piece, source_row, source_column),
            col_send.at[piece, key, move - 1],
            col_recv.at[piece, key, move - 1],
        )

    def start_if(condition, copies):
        pl.when(condition)(functools.partial(start_all, copies))
        ends.append((condition, copies))

    def forward(piece, step, way, condition, source_row):
        start_if(
            condition,
            [across(piece, step, way, move, source_row, column) for move in range(1, wide)],
        )

    def begin(piece):
        start_if(row < deep - 1, [hop(piece, 0, 0, row)])
        start_if(row > 0, [hop(piece, 1, 0, row)])
        forward(piece, 0, 0, row >= 0, row)

    here = [
        pltpu.make_async_copy(own.at[piece], slot(piece, row, column), local.at[0])
        for piece in range(pieces)
    ]
    begin(0)
    for copy in here:
        copy.start()
    yield 0
    for piece in range(pieces):
        sources = []
        for step in range(1, deep):
            for way in (0, 1):
                source_row = row - step if way == 0 else row + step
                there = source_row >= 0 if way == 0 else source_row < deep
                onward = row < deep - 1 if way == 0 else row > 0
                pl.when(there)(hop(piece, way, step - 1, source_row).wait_recv)
                if step < deep - 1:
                    start_if(there & onward, [hop(piece, way, step, source_row)])
                forward(piece, step, way, there, source_row)
                sources.append((step, way, there, source_row))
            if step == 1 and piece + 1 < pieces:
                begin(piece + 1)
            yield 0
        for step, way, there, source_row in [(0, 0, row >= 0, row)] + sources:
            for move in range(1, wide):
                source_column = lax.rem(column + wide - move, wide)
                copy = across(piece, step, way, move, source_row, source_column)
                pl.when(there)(copy.wait_recv)
            if way or not step:
                yield 0
        if piece == 0:
            for copy in here:
                copy.wait()
        yield piece + 1
    for condition, copies in ends:
        pl.when(condition)(functools.partial(end_all, copies))


class Gather:
    def __init__(self, own, layout):
        _, deep, wide = layout
        pieces, rows, width = own.shape
        self.operands, self.in_specs = [own], [ANYWHERE]
        self.outs = [jax.ShapeDtypeStruct((pieces * deep * wide * rows, width), own.dtype)]
        self.out_specs = [ANYWHERE]
        self.scratch = gather_scratch(pieces, deep, wide)
        self.steps = grid_steps(deep, wide)
        self.run = gather_steps


def scatter_scratch(rows, width, deep, wide):
    return [
        pltpu.VMEM((deep, max(1, wide - 1), rows, width), BF16),
        pltpu.VMEM((deep + 1, rows, width), BF16),
        dma(2 * deep, wide - 1),
        dma(2 * deep, wide - 1),
        dma(2 * deep),
        dma(2 * deep),
    ]


def scatter_steps(
    place, parts, piece, total, landed, summed, col_send, col_recv, row_send, row_recv
):
    deep, wide, shards = place.deep, place.wide, place.shards
    row, column = place.row, place.column
    rows = total.shape[0]
    ends = []

    def block(target_row, target_column):
        target = piece * shards + target_row * wide + target_column
        return pl.ds(pl.multiple_of(target * rows, rows), rows)

    def along_row(key, target_row, move):
        target_column = lax.rem(column + move, wide)
        return send_to(
            place.peer(0, 0, 0, move),
            parts.at[block(target_row, target_column)],
            landed.at[target_row, move - 1],
            col_send.at[key, move - 1],
            col_recv.at[key, move - 1],
        )

    def hop(key, step, way, target_row):
        return send_to(
            (place.group, (row + 1 - 2 * way) * wide + column),
            landed.at[target_row, 0],
            summed.at[deep if step == 1 and way else target_row],
            row_send.at[key],
            row_recv.at[key],
        )

    order = []
    for step in range(deep - 1, 0, -1):
        for way in (0, 1):
            target_row = row - step if way else row + step
            there = target_row >= 0 if way else target_row < deep
            order.append((2 * step + way, step, way, target_row, there))
    order.append((0, 0, 0, row, row >= 0))

    def send_row(index):
        key, _, _, target_row, there = order[index]
        copies = [along_row(key, target_row, move) for move in range(1, wide)]
        pl.when(there)(functools.partial(start_all, copies))
        ends.append((there, copies))

    def fold(index):
        key, step, way, target_row, there = order[index]

        def body():
            for move in range(1, wide):
                along_row(key, target_row, move).wait_recv()
            value = parts[block(target_row, column), :].astype(F32)
            for move in range(1, wide):
                value = value + landed[target_row, move - 1].astype(F32)
            if step:
                landed[target_row, 0] = value.astype(BF16)
            else:
                total[...] = value

        pl.when(there)(body)

    def join(index):
        key, step, way, target_row, there = order[index]
        behind = row < deep - 1 if way else row > 0

        def body():
            hop(key + 2, step + 1, way, target_row).wait_recv()
            landed[target_row, 0] = (
                landed[target_row, 0].astype(F32) + summed[target_row].astype(F32)
            ).astype(BF16)

        if step < deep - 1:
            pl.when(there & behind)(body)
        copy = hop(key, step, way, target_row)
        pl.when(there)(copy.start)
        ends.append((there, [copy]))

    def finish(way):
        def body():
            hop(2 + way, 1, way, row).wait_recv()
            total[...] = total[...] + summed[deep if way else row].astype(F32)

        pl.when(row < deep - 1 if way else row > 0)(body)

    ahead = 4
    for index in range(min(ahead, len(order))):
        send_row(index)
    yield
    for index in range(len(order)):
        fold(index)
        if index + ahead < len(order):
            send_row(index + ahead)
        if index < len(order) - 1:
            join(index)
        if index % 2:
            yield
    yield
    for way in (0, 1):
        finish(way)
        yield
    for there, copies in ends:
        pl.when(there)(functools.partial(end_all, copies))


def scatter_pieces(runs, deep):
    running = []
    for run in runs:
        running.append(run)
        for _ in range(deep + 1):
            for each in list(running):
                if next(each, END) is END:
                    running.remove(each)
            yield
    yield from together(*running)


class Scatter:
    def __init__(self, parts, pieces, layout):
        _, deep, wide = layout
        tokens, width = parts.shape
        rows = tokens // (pieces * deep * wide)
        self.pieces = pieces
        self.operands, self.in_specs = [parts], [RESIDENT]
        self.outs = [jax.ShapeDtypeStruct((pieces, rows, width), F32)]
        self.out_specs = [RESIDENT]
        self.scratch = scatter_scratch(rows, width, deep, wide) * pieces
        self.steps = grid_steps(deep, wide)

    def run(self, place, parts, total, *scratch):
        each = len(scratch) // self.pieces
        runs = [
            scatter_steps(
                place,
                parts,
                piece,
                total.at[piece],
                *scratch[piece * each : (piece + 1) * each],
            )
            for piece in range(self.pieces)
        ]
        yield from scatter_pieces(runs, place.deep)


class Chain:
    def __init__(self, *parts):
        self.parts = parts
        for name in ("operands", "in_specs", "outs", "out_specs", "scratch"):
            setattr(self, name, [item for part in parts for item in getattr(part, name)])
        self.steps = set().union(*(part.steps for part in parts))

    def run(self, place, *refs):
        refs = list(refs)
        taken = [[] for _ in self.parts]
        for name in ("operands", "outs", "scratch"):
            for part, own in zip(self.parts, taken, strict=True):
                own.extend(refs.pop(0) for _ in getattr(part, name))
        for part, own in zip(self.parts, taken, strict=True):
            yield from part.run(place, *own)


class ExpertScatter:
    def __init__(self, terms, layout, chunks=2):
        groups = layout[0]
        layers = groups // 2
        _, rows, width = terms.shape
        part = rows // chunks
        self.operands, self.in_specs = [terms], [ANYWHERE]
        self.outs = [jax.ShapeDtypeStruct((rows, width), BF16)]
        self.out_specs = [RESIDENT]
        self.scratch = [
            pltpu.VMEM((chunks, layers, part, width), BF16),
            pltpu.VMEM((chunks, layers, part, width), BF16),
            pltpu.VMEM((chunks, max(1, layers - 1), part, width), BF16),
            dma(chunks, layers),
            dma(chunks, layers),
            dma(chunks, layers),
            dma(chunks, layers - 1),
            dma(chunks, layers - 1),
        ]
        self.steps = expert_steps(layers)

    def run(
        self,
        place,
        terms,
        total,
        mine,
        landed,
        summed,
        local,
        core_send,
        core_recv,
        layer_send,
        layer_recv,
    ):
        chunks, layers, part, _ = mine.shape
        span = min(part, 128)
        sends = []

        def entry(turn, core):
            return lax.rem(place.layer + turn, layers) * 2 + core

        def block(chunk, turn, core):
            return terms.at[entry(turn, core), pl.ds(chunk * part, part)]

        def load(chunk, turn):
            return pltpu.make_async_copy(
                block(chunk, turn, place.core), mine.at[chunk, turn], local.at[chunk, turn]
            )

        def across(chunk, turn):
            return send_to(
                place.peer(0, 1, 0, 0),
                block(chunk, turn, 1 - place.core),
                landed.at[chunk, turn],
                core_send.at[chunk, turn],
                core_recv.at[chunk, turn],
            )

        def along(chunk, turn):
            return send_to(
                place.peer(turn, 0, 0, 0),
                mine.at[chunk, turn],
                summed.at[chunk, turn - 1],
                layer_send.at[chunk, turn - 1],
                layer_recv.at[chunk, turn - 1],
            )

        order = [*range(1, layers), 0]
        for chunk in range(chunks):
            for turn in order:
                load(chunk, turn).start()
                sends.append(across(chunk, turn))
                sends[-1].start()
        yield
        for chunk in range(chunks):
            for turn in order[:-1]:
                load(chunk, turn).wait()
                across(chunk, turn).wait_recv()

                def merge(step, carry, chunk=chunk, turn=turn):
                    rows = pl.ds(pl.multiple_of(step * span, span), span)
                    value = mine[chunk, turn, rows].astype(F32)
                    value = value + landed[chunk, turn, rows].astype(F32)
                    mine[chunk, turn, rows] = value.astype(BF16)
                    return carry

                lax.fori_loop(0, part // span, merge, 0)
                sends.append(along(chunk, turn))
                sends[-1].start()
                yield
        for chunk in range(chunks):
            load(chunk, 0).wait()
            across(chunk, 0).wait_recv()
            for turn in order[:-1]:
                along(chunk, turn).wait_recv()

            def finish(step, carry, chunk=chunk):
                rows = pl.ds(pl.multiple_of(step * span, span), span)
                here = pl.ds(pl.multiple_of(chunk * part + step * span, span), span)
                value = mine[chunk, 0, rows].astype(F32) + landed[chunk, 0, rows].astype(F32)
                for turn in order[:-1]:
                    value = value + summed[chunk, turn - 1, rows].astype(F32)
                total[here] = value.astype(BF16)
                return carry

            lax.fori_loop(0, part // span, finish, 0)
            yield
        for copy in sends:
            copy.wait_send()


class Experts:
    SPAN = 256

    def __init__(self, own, upstream, mask, router, gate_all, up_all, down_all, layout):
        _, deep, wide = layout
        pieces, rows, width = own.shape
        halves, _, units = gate_all.shape
        tokens, lanes = mask.shape
        self.operands = [own, upstream, mask, router, gate_all, up_all, down_all]
        self.in_specs = [ANYWHERE, ANYWHERE, RESIDENT, RESIDENT] + [ANYWHERE] * 3
        self.outs = [
            jax.ShapeDtypeStruct((halves, width, units), BF16),
            jax.ShapeDtypeStruct((halves, width, units), BF16),
            jax.ShapeDtypeStruct((halves, units, width), BF16),
            jax.ShapeDtypeStruct((tokens, width), BF16),
            jax.ShapeDtypeStruct((tokens, lanes), F32),
            jax.ShapeDtypeStruct((pieces, rows, width), F32),
            jax.ShapeDtypeStruct((pieces, rows, lanes), F32),
        ]
        self.out_specs = [ANYWHERE] * 4 + [RESIDENT] * 3
        gathers = gather_scratch(pieces, deep, wide)
        scatters = scatter_scratch(rows, width, deep, wide)
        dots = scatter_scratch(rows, lanes, deep, wide)
        self.sizes = [len(gathers), len(scatters)]
        acts = pltpu.VMEM((halves, tokens, units), BF16)
        self.scratch = [
            pltpu.VMEM((tokens, width), BF16),
            pltpu.VMEM((tokens, width), BF16),
            acts,
            acts,
            acts,
            pltpu.VMEM((halves, width, units), BF16),
            pltpu.VMEM((halves, width, units), BF16),
            pltpu.VMEM((halves, units, width), BF16),
            pltpu.VMEM((tokens, width), BF16),
            pltpu.VMEM((tokens, lanes), F32),
            pltpu.VMEM((tokens, lanes), BF16),
            dma(3, halves),
            dma(3, halves),
            dma(2),
            *gathers,
            *scatters * pieces,
            *dots * pieces,
        ]
        self.steps = grid_steps(deep, wide)

    def run(
        self,
        place,
        own,
        upstream_in,
        mask,
        router,
        gate_all,
        up_all,
        down_all,
        gate_terms,
        up_terms,
        down_terms,
        out,
        share,
        total,
        dot_total,
        rows,
        upstream,
        hidden,
        gate_pre,
        up_pre,
        gate_weight,
        up_weight,
        down_weight,
        parts,
        dots,
        placed,
        load_sem,
        store_sem,
        local_sem,
        *scratch,
    ):
        pieces = own.shape[0]
        halves, _, units = hidden.shape
        tokens, width = rows.shape
        lanes = mask.shape[1]
        count = tokens // pieces
        span = self.SPAN
        shards = place.shards
        scratch = list(scratch)

        def take(number):
            return [scratch.pop(0) for _ in range(number)]

        inward = gather_steps(place, own, rows, *take(self.sizes[0]))
        scatters = [
            scatter_steps(place, parts, piece, total.at[piece], *take(self.sizes[1]))
            for piece in range(pieces)
        ]
        dot_scatters = [
            scatter_steps(place, placed, piece, dot_total.at[piece], *take(self.sizes[1]))
            for piece in range(pieces)
        ]
        running = []

        def others():
            for each in list(running):
                if next(each, END) is END:
                    running.remove(each)

        kept = (gate_weight, up_weight, down_weight)

        def load(half):
            return [
                pltpu.make_async_copy(source.at[half], kept[which].at[half], load_sem.at[which, half])
                for which, source in enumerate((gate_all, up_all, down_all))
            ]

        def store(which, half):
            target = (gate_terms, up_terms, down_terms)[which]
            return pltpu.make_async_copy(
                kept[which].at[half], target.at[half], store_sem.at[which, half]
            )

        def wait_all(copies):
            for copy in copies:
                copy.wait()

        def shares(piece):
            here = pl.ds(piece * count, count)
            known = mask[here, :]
            logits = dot(rows[here, :], router[...], NN)
            peak = jnp.max(jnp.where(known > 0, logits, MASK_FILL), axis=1, keepdims=True)
            exponent = jnp.where(known > 0, jnp.exp(jnp.minimum(logits - peak, 0.0)), 0.0)
            share[here, :] = exponent / jnp.sum(exponent, axis=1, keepdims=True)

        def units_of(piece):
            here = pl.ds(piece * count, count)
            which_lane = lax.broadcasted_iota(jnp.int32, (count, lanes), 1)
            for half in range(halves):
                if piece == 0:
                    wait_all(load(half))
                column = half * shards + place.me
                chosen = jnp.where(which_lane == column // 2, share[here, :], 0.0)
                weight = jnp.sum(chosen, axis=1, keepdims=True)
                for step in range(units // span):
                    there = pl.ds(step * span, span)
                    gate = dot(rows[here, :], gate_weight[half, :, there], NN)
                    up = dot(rows[here, :], up_weight[half, :, there], NN)
                    grad = dot(upstream[here, :], down_weight[half, there, :], NT)
                    sigmoid_gate = 1.0 / (1.0 + jnp.exp(-gate))
                    swish_gate = gate * sigmoid_gate
                    activated = swish_gate * up
                    products = jnp.sum(activated * grad, axis=1, keepdims=True)
                    dots[here, :] += jnp.where(which_lane == column, products, 0.0)
                    hidden[half, here, there] = (activated * weight).astype(BF16)
                    grad = grad * weight
                    gate_pre[half, here, there] = (
                        grad * up * (sigmoid_gate * (1.0 + gate * (1.0 - sigmoid_gate)))
                    ).astype(BF16)
                    up_pre[half, here, there] = (grad * swish_gate).astype(BF16)
                    yield

        def merge(piece):
            here = pl.ds(piece * count, count)
            for step in range(width // span):
                there = pl.ds(step * span, span)
                value = dot(gate_pre[0, here, :], gate_weight[0, there, :], NT)
                value = value + dot(up_pre[0, here, :], up_weight[0, there, :], NT)
                for half in range(1, halves):
                    value = value + dot(gate_pre[half, here, :], gate_weight[half, there, :], NT)
                    value = value + dot(up_pre[half, here, :], up_weight[half, there, :], NT)
                parts[here, there] = value.astype(BF16)
                yield

        def place_dots(piece):
            here = pl.ds(piece * count, count)
            value = dots[here, :]
            high = value.astype(BF16).astype(F32)
            low = pltpu.roll(value - high, lanes // 2, 1)
            placed[here, :] = (high + low).astype(BF16)

        def weights():
            ends = []

            def put(copy):
                copy.start()
                ends.append(copy)

            for which, grads in enumerate((gate_pre, up_pre)):
                for half in range(halves):
                    for step in range(units // span):
                        there = pl.ds(step * span, span)
                        kept[which][half, :, there] = dot(
                            rows[...], grads[half, :, there], TN
                        ).astype(BF16)
                        yield
                    put(store(which, half))
            for step in range(width // span):
                there = pl.ds(step * span, span)
                value = dot(hidden[0], down_weight[0, :, there], NN)
                for half in range(1, halves):
                    value = value + dot(hidden[half], down_weight[half, :, there], NN)
                rows[:, there] = value.astype(BF16)
                yield
            put(pltpu.make_async_copy(rows, out, local_sem.at[1]))
            for half in range(halves):
                for step in range(units // span):
                    there = pl.ds(step * span, span)
                    down_weight[half, there, :] = dot(
                        hidden[half, :, there], upstream[...], TN
                    ).astype(BF16)
                    yield
                put(store(2, half))
            wait_all(ends)

        next(inward)
        upstream_copy = pltpu.make_async_copy(upstream_in, upstream, local_sem.at[0])
        upstream_copy.start()
        for half in range(halves):
            start_all(load(half))
        dots[...] = jnp.zeros_like(dots)
        yield from until(inward, 1)
        upstream_copy.wait()
        running.append(inward)
        for piece in range(pieces):
            if piece:
                while inward in running:
                    others()
                    yield
                running.extend([dot_scatters[piece - 1], scatters[piece - 1]])
                next(dot_scatters[piece - 1])
                next(scatters[piece - 1])
            shares(piece)
            for index, _ in enumerate(units_of(piece)):
                if piece == 0 or index % 2:
                    others()
                yield
            place_dots(piece)
            for index, _ in enumerate(merge(piece)):
                if piece == 0 or index % 4 == 3:
                    others()
                yield
        running.extend([dot_scatters[-1], scatters[-1]])
        next(dot_scatters[-1])
        next(scatters[-1])
        for index, _ in enumerate(weights()):
            if index % 4 == 3:
                others()
                yield
        yield from together(*running)


class Columns:
    def __init__(self, weights, smalls, layout):
        groups, deep, wide = layout
        shards = deep * wide
        depth = weights[0].shape[0]
        self.operands, self.in_specs = [*weights, *smalls], [ANYWHERE] * 5
        self.outs = [
            jax.ShapeDtypeStruct((shards, groups, depth // groups, 3 * depth), BF16),
            *[jax.ShapeDtypeStruct((shards,) + small.shape, BF16) for small in smalls],
        ]
        self.out_specs = [ANYWHERE] * 3
        self.scratch = [
            dma(3, shards - 1),
            dma(3, shards - 1),
            dma(2, shards - 1),
            dma(2, shards - 1),
            dma(groups // 2 - 1),
            dma(groups // 2 - 1),
            dma(groups // 2),
            dma(groups // 2),
            dma(5),
        ]
        self.steps = shard_steps(deep, wide) | expert_steps(groups // 2)

    def run(
        self,
        place,
        query_weight,
        key_weight,
        value_weight,
        small,
        gains,
        projections,
        small_all,
        gains_all,
        weight_send,
        weight_recv,
        small_send,
        small_recv,
        layer_send,
        layer_recv,
        core_send,
        core_recv,
        local,
    ):
        weights = (query_weight, key_weight, value_weight)
        smalls = ((small, small_all), (gains, gains_all))
        layers, group, me = place.layers, place.group, place.me
        part = projections.shape[2]
        depth = query_weight.shape[0]
        steps = sorted(shard_steps(place.deep, place.wide))
        sends = []

        def block(which, target):
            return weights[which].at[
                pl.ds(pl.multiple_of(group * part, part), part),
                pl.ds(pl.multiple_of(target * depth, depth), depth),
            ]

        def slot(which, source):
            return projections.at[source, group, :, pl.ds(which * depth, depth)]

        def weight_copy(which, index):
            return send_to(
                place.peer(*steps[index]),
                block(which, place.peer(*steps[index])[1]),
                slot(which, me),
                weight_send.at[which, index],
                weight_recv.at[which, index],
            )

        def small_copy(which, index):
            return send_to(
                place.peer(*steps[index]),
                smalls[which][0],
                smalls[which][1].at[me],
                small_send.at[which, index],
                small_recv.at[which, index],
            )

        def slab_copy(peer, layer, core, send_sem, recv_sem):
            slab = projections.at[:, layer * 2 + core]
            return send_to(peer, slab, slab, send_sem, recv_sem)

        def layer_copy(step, layer):
            return slab_copy(
                place.peer(step, 0, 0, 0),
                layer,
                place.core,
                layer_send.at[step - 1],
                layer_recv.at[step - 1],
            )

        def core_copy(step, layer, core):
            return slab_copy(
                place.peer(0, 1, 0, 0), layer, core, core_send.at[step], core_recv.at[step]
            )

        here = [
            pltpu.make_async_copy(block(which, me), slot(which, me), local.at[which])
            for which in range(3)
        ]
        for which, (own, whole) in enumerate(smalls):
            here.append(pltpu.make_async_copy(own, whole.at[me], local.at[3 + which]))
        for copy in here:
            copy.start()
        for index in range(len(steps)):
            for which in range(3):
                sends.append(weight_copy(which, index))
                sends[-1].start()
            for which in (0, 1):
                sends.append(small_copy(which, index))
                sends[-1].start()
        yield
        for copy in here:
            copy.wait()
        for index in range(len(steps)):
            for which in range(3):
                weight_copy(which, index).wait_recv()
        for step in range(1, layers):
            sends.append(layer_copy(step, place.layer))
            sends[-1].start()
        sends.append(core_copy(0, place.layer, place.core))
        sends[-1].start()
        yield
        for step in range(1, layers):
            layer = lax.rem(place.layer + layers - step, layers)
            layer_copy(step, layer).wait_recv()
            sends.append(core_copy(step, layer, place.core))
            sends[-1].start()
            yield
        for step in range(layers):
            layer = lax.rem(place.layer + layers - step, layers)
            core_copy(step, layer, 1 - place.core).wait_recv()
            yield
        for index in range(len(steps)):
            for which in (0, 1):
                small_copy(which, index).wait_recv()
        for copy in sends:
            copy.wait_send()


class Rows:
    def __init__(self, terms, row_terms, tail, layout):
        groups, deep, wide = layout
        layers = groups // 2
        shards, _, part, width = terms.shape
        depth = row_terms.shape[2]
        self.operands = [terms, row_terms, tail]
        self.in_specs = [RESIDENT] * 3
        self.outs = [
            jax.ShapeDtypeStruct((groups, part, depth), BF16),
            jax.ShapeDtypeStruct(tail.shape[1:], F32),
            *[jax.ShapeDtypeStruct((groups, part, depth), BF16)] * 3,
        ]
        self.out_specs = [RESIDENT] * 5
        others = max(1, layers - 1)
        self.scratch = [
            pltpu.VMEM((groups, shards, part, width), BF16),
            pltpu.VMEM((layers, shards, part, width), BF16),
            pltpu.VMEM((others, shards, part, width), BF16),
            pltpu.VMEM((others, shards, part, width), BF16),
            pltpu.VMEM((shards, part, width), BF16),
            pltpu.VMEM((layers, part, depth), BF16),
            pltpu.VMEM((others, part, depth), BF16),
            pltpu.VMEM((others, part, depth), BF16),
            pltpu.VMEM(tail.shape, F32),
            pltpu.VMEM((groups,) + tail.shape[1:], F32),
            dma(2, layers),
            dma(2, layers),
            dma(2, others),
            dma(2, others),
            dma(shards - 1),
            dma(shards - 1),
            dma(2, others),
            dma(2, others),
            dma(2, layers),
            dma(2, layers),
            dma(shards - 1),
            dma(shards - 1),
            dma(groups - 1),
            dma(groups - 1),
        ]
        self.steps = shard_steps(deep, wide) | expert_steps(layers)
        self.steps |= {(layer, core, 0, 0) for layer in range(layers) for core in (0, 1)}
        self.steps -= {(0, 0, 0, 0)}

    def run(
        self,
        place,
        terms,
        row_terms,
        tail,
        whole_rows,
        tail_out,
        query_out,
        key_out,
        value_out,
        whole,
        landed,
        merged,
        summed,
        ready,
        landed_rows,
        merged_rows,
        summed_rows,
        tails,
        tail_sums,
        core_send,
        core_recv,
        layer_send,
        layer_recv,
        swap_send,
        swap_recv,
        out_send,
        out_recv,
        over_send,
        over_recv,
        tail_send,
        tail_recv,
        sum_send,
        sum_recv,
    ):
        layers, group, me, core = place.layers, place.group, place.me, place.core
        shards = place.shards
        steps = sorted(shard_steps(place.deep, place.wide))
        group_steps = [
            (layer, flip, 0, 0) for layer in range(layers) for flip in (0, 1) if layer or flip
        ]
        sends = []

        def start(copy):
            copy.start()
            sends.append(copy)

        def layer_at(turn):
            return lax.rem(place.layer + turn, layers)

        def tail_copy(index):
            peer = place.peer(*steps[index])
            return send_to(
                peer, tail.at[peer[1]], tails.at[me], tail_send.at[index], tail_recv.at[index]
            )

        def sum_copy(index):
            return send_to(
                place.peer(*group_steps[index]),
                tail_sums.at[group],
                tail_sums.at[group],
                sum_send.at[index],
                sum_recv.at[index],
            )

        def across(which, turn):
            entry = layer_at(turn) * 2 + 1 - core
            source = row_terms.at[entry] if which else terms.at[:, entry]
            target = landed_rows.at[turn] if which else landed.at[turn]
            return send_to(
                place.peer(0, 1, 0, 0),
                source,
                target,
                core_send.at[which, turn],
                core_recv.at[which, turn],
            )

        def along(which, turn):
            source = merged_rows.at[turn - 1] if which else merged.at[turn - 1]
            target = summed_rows.at[turn - 1] if which else summed.at[turn - 1]
            return send_to(
                place.peer(turn, 0, 0, 0),
                source,
                target,
                layer_send.at[which, turn - 1],
                layer_recv.at[which, turn - 1],
            )

        def swap(index):
            peer = place.peer(*steps[index])
            return send_to(
                peer,
                ready.at[peer[1]],
                whole.at[group, me],
                swap_send.at[index],
                swap_recv.at[index],
            )

        def out(which, turn, entry):
            slab = whole_rows.at[entry] if which else whole.at[entry]
            return send_to(
                place.peer(turn, 0, 0, 0),
                slab,
                slab,
                out_send.at[which, turn - 1],
                out_recv.at[which, turn - 1],
            )

        def over(which, turn, entry):
            slab = whole_rows.at[entry] if which else whole.at[entry]
            return send_to(
                place.peer(0, 1, 0, 0),
                slab,
                slab,
                over_send.at[which, turn],
                over_recv.at[which, turn],
            )

        order = [*range(1, layers), 0]
        for which in (0, 1):
            for turn in order:
                start(across(which, turn))
        for index in range(len(steps)):
            start(tail_copy(index))
        yield
        for which in (0, 1):
            for turn in order[:-1]:
                across(which, turn).wait_recv()
                entry = layer_at(turn) * 2 + core
                if which:
                    merged_rows[turn - 1] = (
                        row_terms[entry].astype(F32) + landed_rows[turn].astype(F32)
                    ).astype(BF16)
                else:
                    for shard in range(shards):
                        merged[turn - 1, shard] = (
                            terms[shard, entry].astype(F32) + landed[turn, shard].astype(F32)
                        ).astype(BF16)
                start(along(which, turn))
                yield
        for which in (0, 1):
            across(which, 0).wait_recv()
        for index in range(len(steps)):
            tail_copy(index).wait_recv()
        tails[me] = tail[me]
        tail_sum = tails[0]
        for shard in range(1, shards):
            tail_sum = tail_sum + tails[shard]
        tail_sums[group] = tail_sum
        for index in range(len(group_steps)):
            start(sum_copy(index))
        yield
        for turn in order[:-1]:
            along(0, turn).wait_recv()
        for shard in range(shards):
            value = terms[shard, group].astype(F32) + landed[0, shard].astype(F32)
            for turn in order[:-1]:
                value = value + summed[turn - 1, shard].astype(F32)
            ready[shard] = value.astype(BF16)
        for index in range(len(steps)):
            start(swap(index))
        whole[group, me] = ready[me]
        yield
        for turn in order[:-1]:
            along(1, turn).wait_recv()
        value = row_terms[group].astype(F32) + landed_rows[0].astype(F32)
        for turn in order[:-1]:
            value = value + summed_rows[turn - 1].astype(F32)
        whole_rows[group] = value.astype(BF16)
        for turn in order[:-1]:
            start(out(1, turn, group))
        start(over(1, 0, group))
        yield
        for index in range(len(steps)):
            swap(index).wait_recv()
        for turn in order[:-1]:
            start(out(0, turn, group))
        start(over(0, 0, group))
        yield
        for which in (1, 0):
            for turn in order[:-1]:
                entry = layer_at(layers - turn) * 2 + core
                out(which, turn, entry).wait_recv()
                start(over(which, turn, entry))
                yield
        for index in range(len(group_steps)):
            sum_copy(index).wait_recv()
        tail_sum = tail_sums[0]
        for index in range(1, place.groups):
            tail_sum = tail_sum + tail_sums[index]
        tail_out[...] = tail_sum
        depth = terms.shape[3] // 3
        for which in (1, 0):
            for turn in range(layers):
                entry = layer_at(layers - turn) * 2 + 1 - core
                over(which, turn, entry).wait_recv()
                yield
        for entry in range(place.groups):
            for shard in range(shards):
                here = pl.ds(shard * depth, depth)
                value = whole[entry, shard]
                query_out[entry, :, here] = value[:, :depth]
                key_out[entry, :, here] = value[:, depth : 2 * depth]
                value_out[entry, :, here] = value[:, 2 * depth :]
            yield
        for copy in sends:
            copy.wait_send()


def turn(values, cosine, sine):
    return values * cosine + pltpu.roll(values, HDIM // 2, 1) * sine


def head_forward(projected, place, gain, cosine, sine):
    proj = projected[:, place * HDIM : (place + 1) * HDIM]
    scale = rms_scale(proj)
    unit = proj * scale
    return scale, unit, turn(unit * gain, cosine, sine).astype(BF16)


def head_probs(query_rot, key_rot, seg_column, seg_row):
    scores = dot(query_rot, key_rot, NT) * (1.0 / math.sqrt(HDIM))
    scores = jnp.where(seg_column == seg_row, scores, MASK_FILL)
    exponent = jnp.exp(scores - jnp.max(scores, axis=-1, keepdims=True))
    return exponent * (1.0 / jnp.sum(exponent, axis=-1, keepdims=True))


def forward_steps(
    micro,
    hidden,
    projections,
    output_weight,
    gain,
    head_gains,
    cosine,
    sine,
    seg_column,
    seg_row,
    mixer,
    projected,
    attended,
    parts,
):
    span = seg_column.shape[1]
    depth = projections.shape[1] // 3
    heads = depth // HDIM
    tile = min(span, 256)
    rows = pl.ds(micro * span, span)
    for start in range(0, span, tile):
        here = pl.ds(micro * span + start, tile)
        values = hidden[here, :].astype(F32)
        mixer[here, :] = (values * rms_scale(values) * gain).astype(BF16)
    projected[rows, :] = dot(mixer[rows, :], projections[...], NN)
    yield
    for head in range(heads):
        own = projected[rows, :]
        _, _, query_rot = head_forward(own, head, head_gains[0], cosine[...], sine[...])
        _, _, key_rot = head_forward(own, heads + head, head_gains[1], cosine[...], sine[...])
        values = own[:, (2 * heads + head) * HDIM : (2 * heads + head + 1) * HDIM]
        probs = head_probs(query_rot, key_rot, seg_column[micro], seg_row[micro])
        attended[rows, head * HDIM : (head + 1) * HDIM] = dot(
            probs.astype(BF16), values.astype(BF16), NN
        ).astype(BF16)
        yield
    parts[rows, :] = dot(attended[rows, :], output_weight[...], NN).astype(BF16)
    yield


def backward_steps(
    micro,
    branch,
    projected,
    projections,
    output_weight,
    head_gains,
    cosine,
    sine,
    seg_column,
    seg_row,
    parts,
    gain_terms,
    attended_grad,
    projected_grad,
):
    span = seg_column.shape[1]
    heads = output_weight.shape[0] // HDIM
    scale = 1.0 / math.sqrt(HDIM)
    rows = pl.ds(micro * span, span)
    attended_grad[rows, :] = dot(branch[rows, :], output_weight[...], NT).astype(BF16)
    yield
    for head in range(heads):
        own = projected[rows, :]
        query_scale, query_unit, query_rot = head_forward(
            own, head, head_gains[0], cosine[...], sine[...]
        )
        key_scale, key_unit, key_rot = head_forward(
            own, heads + head, head_gains[1], cosine[...], sine[...]
        )
        values = own[:, (2 * heads + head) * HDIM : (2 * heads + head + 1) * HDIM]
        probs = head_probs(query_rot, key_rot, seg_column[micro], seg_row[micro])
        out_grad = attended_grad[rows, head * HDIM : (head + 1) * HDIM]
        prob_grad = dot(out_grad, values.astype(BF16), NT)
        row_delta = jnp.sum(probs * prob_grad, axis=-1, keepdims=True)
        score_grad = (probs * (prob_grad - row_delta)).astype(BF16)
        projected_grad[rows, (2 * heads + head) * HDIM : (2 * heads + head + 1) * HDIM] = dot(
            probs.astype(BF16), out_grad, TN
        ).astype(BF16)
        for which, (rot_grad, unit, unit_scale) in enumerate(
            (
                (dot(score_grad, key_rot, NN) * scale, query_unit, query_scale),
                (dot(score_grad, query_rot, TN) * scale, key_unit, key_scale),
            )
        ):
            unit_grad = turn(rot_grad, cosine[...], -sine[...])
            gain_terms[which : which + 1] += jnp.sum(unit_grad * unit, axis=0, keepdims=True)
            place = (which * heads + head) * HDIM
            projected_grad[rows, place : place + HDIM] = norm_back(
                unit_grad * head_gains[which], unit, unit_scale
            ).astype(BF16)
        yield
    parts[rows, :] = dot(projected_grad[rows, :], projections[...], NT).astype(BF16)
    yield


def weight_steps(branch, mixer, attended, projected_grad, projection_terms, output_terms):
    width = branch.shape[1]
    tile = min(512, width)
    for start in range(0, width, tile):
        here = pl.ds(start, tile)
        output_terms[:, here] = dot(attended[...], branch[:, here], TN).astype(BF16)
        projection_terms[here, :] = dot(mixer[:, here], projected_grad[...], TN).astype(BF16)
        yield


class AttentionForward:
    def __init__(
        self, weights, smalls, inputs, cotangent, output_weight, tables, segments, layout
    ):
        _, deep, wide = layout
        micros, rows, width = inputs.shape
        shards = deep * wide
        tokens = micros * shards * rows
        depth = output_weight.shape[0]
        self.columns = Columns(weights, smalls, layout)
        self.operands = [
            *self.columns.operands,
            inputs,
            cotangent,
            output_weight,
            *tables,
            *segments,
        ]
        self.in_specs = [*self.columns.in_specs, ANYWHERE, ANYWHERE, *[RESIDENT] * 5]
        self.outs = [
            *self.columns.outs[1:],
            jax.ShapeDtypeStruct((shards, depth, 3 * depth), BF16),
            jax.ShapeDtypeStruct((tokens, width), BF16),
            jax.ShapeDtypeStruct((tokens, width), BF16),
            jax.ShapeDtypeStruct((tokens, 3 * depth), F32),
            jax.ShapeDtypeStruct((tokens, depth), BF16),
            jax.ShapeDtypeStruct((micros, rows, width), F32),
        ]
        self.out_specs = [ANYWHERE, RESIDENT, RESIDENT, ANYWHERE, *[RESIDENT] * 4]
        gathers = gather_scratch(micros, deep, wide)
        scatters = scatter_scratch(rows, width, deep, wide)
        self.sizes = [len(self.columns.scratch), len(gathers), len(gathers), len(scatters)]
        columns_out = self.columns.outs[0]
        self.scratch = [
            pltpu.VMEM(columns_out.shape, BF16),
            pltpu.VMEM((tokens, width), BF16),
            pltpu.VMEM((tokens, width), BF16),
            pltpu.VMEM((1, width), F32),
            *self.columns.scratch,
            *gathers,
            *gathers,
            *scatters * micros,
        ]
        self.steps = self.columns.steps | grid_steps(deep, wide)

    def run(
        self,
        place,
        query_weight,
        key_weight,
        value_weight,
        small,
        gains,
        inputs,
        cotangent,
        output_weight,
        cosine,
        sine,
        seg_column,
        seg_row,
        small_all,
        gains_all,
        projections,
        upstream,
        mixer,
        projected,
        attended,
        total,
        swapped,
        hidden,
        parts,
        gain,
        *scratch,
    ):
        micros, shards, deep = inputs.shape[0], place.shards, place.deep
        scratch = list(scratch)

        def take(count):
            return [scratch.pop(0) for _ in range(count)]

        columns = self.columns.run(
            place,
            query_weight,
            key_weight,
            value_weight,
            small,
            gains,
            swapped,
            small_all,
            gains_all,
            *take(self.sizes[0]),
        )
        inward = gather_steps(place, inputs, hidden, *take(self.sizes[1]))
        upward = gather_steps(place, cotangent, upstream, *take(self.sizes[2]))
        scatters = [
            scatter_steps(place, parts, micro, total.at[micro], *take(self.sizes[3]))
            for micro in range(micros)
        ]
        next(columns)
        next(inward)
        next(columns)
        yield from until(inward, 1)
        yield from columns
        part, depth = swapped.shape[2], output_weight.shape[0]
        head_gains = jnp.zeros((1, 2 * HDIM), F32)
        for shard in range(shards):
            for group in range(place.groups):
                projections[shard, group * part : (group + 1) * part, :] = swapped[shard, group]
            known = gains_all[shard].astype(F32)
            gain[:, shard * depth : (shard + 1) * depth] = known[0:1, :depth]
            head_gains = head_gains + known[1:2, : 2 * HDIM]
        head_gains = (head_gains[:, :HDIM], head_gains[:, HDIM:])
        weight = projections[...].reshape(-1, projections.shape[2])
        running = []
        for micro in range(micros):
            for _ in forward_steps(
                micro,
                hidden,
                weight,
                output_weight,
                gain[...],
                head_gains,
                cosine,
                sine,
                seg_column,
                seg_row,
                mixer,
                projected,
                attended,
                parts,
            ):
                for each in list(running):
                    if next(each, END) is END:
                        running.remove(each)
                if micro + 1 < micros:
                    next(inward, END)
                yield
            if micro + 1 < micros:
                yield from until(inward, micro + 2)
            running.append(scatters[micro])
            next(scatters[micro])
        running.append(upward)
        yield from inward
        yield from together(*running)


class AttentionBackward:
    def __init__(
        self,
        branch,
        mixer,
        projected,
        attended,
        projections,
        output_weight,
        head_gains,
        tables,
        segments,
        beside,
        layout,
    ):
        _, deep, wide = layout
        micros, rows, width = branch.shape
        tokens = micros * deep * wide * rows
        depth = output_weight.shape[0]
        self.beside = beside
        self.operands = [
            branch,
            mixer,
            projected,
            attended,
            projections,
            output_weight,
            head_gains,
            *tables,
            *segments,
            *[operand for part in beside for operand in part.operands],
        ]
        self.in_specs = [ANYWHERE] + [RESIDENT] * 10
        self.in_specs += [spec for part in beside for spec in part.in_specs]
        self.outs = [
            jax.ShapeDtypeStruct((width, 3 * depth), BF16),
            jax.ShapeDtypeStruct((depth, width), BF16),
            jax.ShapeDtypeStruct((8, HDIM), F32),
            jax.ShapeDtypeStruct((micros, rows, width), F32),
            *[out for part in beside for out in part.outs],
        ]
        self.out_specs = [RESIDENT] * 4 + [spec for part in beside for spec in part.out_specs]
        gathers = gather_scratch(micros, deep, wide)
        scatters = scatter_scratch(rows, width, deep, wide)
        self.sizes = [len(gathers), len(scatters)]
        self.scratch = [
            pltpu.VMEM((tokens, width), BF16),
            pltpu.VMEM((tokens, width), BF16),
            pltpu.VMEM((tokens, depth), BF16),
            pltpu.VMEM((tokens, 3 * depth), BF16),
            *gathers,
            *scatters * micros,
            *[buffer for part in beside for buffer in part.scratch],
        ]
        self.steps = grid_steps(deep, wide).union(*(part.steps for part in beside))

    def run(self, place, *refs):
        refs = list(refs)

        def take(count):
            return [refs.pop(0) for _ in range(count)]

        (
            branch,
            mixer,
            projected,
            attended,
            projections,
            output_weight,
            head_gains,
            cosine,
            sine,
            seg_column,
            seg_row,
        ) = take(11)
        beside_in = [take(len(part.operands)) for part in self.beside]
        projection_terms, output_terms, gain_terms, total = take(4)
        beside_out = [take(len(part.outs)) for part in self.beside]
        branch_all, parts, attended_grad, projected_grad = take(4)
        micros = branch.shape[0]
        inward = gather_steps(place, branch, branch_all, *take(self.sizes[0]))
        scatters = [
            scatter_steps(place, parts, micro, total.at[micro], *take(self.sizes[1]))
            for micro in range(micros)
        ]
        sides = [
            part.run(place, *own_in, *own_out, *take(len(part.scratch)))
            for part, own_in, own_out in zip(self.beside, beside_in, beside_out, strict=True)
        ]
        next(inward)
        for side in sides[:1]:
            next(side)
            for _ in range(2):
                next(inward)
                next(side)
        for side in sides[1:]:
            next(side)
        gain_terms[...] = jnp.zeros_like(gain_terms)
        gains = (head_gains[0:1], head_gains[1:2])
        yield from until(inward, 1)
        for side in sides[1:]:
            next(side)
            next(side)
        running = []
        for micro in range(micros):
            for _ in backward_steps(
                micro,
                branch_all,
                projected,
                projections,
                output_weight,
                gains,
                cosine,
                sine,
                seg_column,
                seg_row,
                parts,
                gain_terms,
                attended_grad,
                projected_grad,
            ):
                for each in list(running):
                    if next(each, END) is END:
                        running.remove(each)
                if micro + 1 < micros:
                    next(inward, END)
                yield
            if micro + 1 < micros:
                yield from until(inward, micro + 2)
            running.append(scatters[micro])
            next(scatters[micro])
        for side in sides[:1]:
            yield from side
        running.append(inward)
        running.append(
            weight_steps(
                branch_all, mixer, attended, projected_grad, projection_terms, output_terms
            )
        )
        yield from together(*running)
        for side in sides[1:]:
            yield from side


def units_kernel(
    span,
    rows_ref,
    upstream_ref,
    share_ref,
    gate_ref,
    up_ref,
    down_ref,
    hidden_ref,
    gate_pre_ref,
    up_pre_ref,
    dot_ref,
):
    half = pl.program_id(0)
    half_width = gate_ref.shape[2]
    lanes = lax.broadcasted_iota(jnp.int32, share_ref.shape, 1)
    share = jnp.sum(jnp.where(lanes == half, share_ref[...], 0.0), axis=1, keepdims=True)

    def body(step, carry):
        units = pl.ds(pl.multiple_of(step * span, span), span)
        gate_pre = dot(rows_ref[...], gate_ref[0, :, units], NN)
        up_pre = dot(rows_ref[...], up_ref[0, :, units], NN)
        units_grad = dot(upstream_ref[...], down_ref[0, units, :], NT)
        sigmoid_gate = 1.0 / (1.0 + jnp.exp(-gate_pre))
        swish_gate = gate_pre * sigmoid_gate
        activated = swish_gate * up_pre
        dots = jnp.sum(activated * units_grad, axis=1, keepdims=True)
        dot_ref[...] += jnp.where(lanes == half, dots, 0.0)
        hidden_ref[0, :, units] = (activated * share).astype(BF16)
        weighted = units_grad * share
        gate_pre_ref[0, :, units] = (
            weighted * up_pre * (sigmoid_gate * (1.0 + gate_pre * (1.0 - sigmoid_gate)))
        ).astype(BF16)
        up_pre_ref[0, :, units] = (weighted * swish_gate).astype(BF16)
        return carry

    @pl.when(half == 0)
    def _():
        dot_ref[...] = jnp.zeros_like(dot_ref)

    lax.fori_loop(0, half_width // span, body, 0)


def expert_units(rows, upstream, share, gate_all, up_all, down_all):
    tokens, width = rows.shape
    halves, _, units = gate_all.shape

    def each(*shape):
        return pl.BlockSpec((1,) + shape, lambda half: (half,) + (0,) * len(shape))

    whole = pl.BlockSpec(memory_space=pltpu.VMEM)
    return pl.pallas_call(
        functools.partial(units_kernel, 256 if tokens <= 1024 else 128),
        grid=(halves,),
        in_specs=[whole, whole, whole, each(width, units), each(width, units), each(units, width)],
        out_specs=[each(tokens, units), each(tokens, units), each(tokens, units), whole],
        out_shape=[
            jax.ShapeDtypeStruct((halves, tokens, units), BF16),
            jax.ShapeDtypeStruct((halves, tokens, units), BF16),
            jax.ShapeDtypeStruct((halves, tokens, units), BF16),
            jax.ShapeDtypeStruct(share.shape, F32),
        ],
        compiler_params=pltpu.CompilerParams(vmem_limit_bytes=VMEM_LIMIT),
        cost_estimate=pl.CostEstimate(
            flops=6 * tokens * width * units * halves,
            bytes_accessed=6 * width * units * halves,
            transcendentals=0,
        ),
    )(rows, upstream, share, gate_all, up_all, down_all)


def merge_kernel(gate_pre_ref, up_pre_ref, gate_ref, up_ref, grad_ref):
    halves = gate_pre_ref.shape[0]
    grad = dot(gate_pre_ref[0], gate_ref[0], NT) + dot(up_pre_ref[0], up_ref[0], NT)
    for half in range(1, halves):
        grad = grad + dot(gate_pre_ref[half], gate_ref[half], NT)
        grad = grad + dot(up_pre_ref[half], up_ref[half], NT)
    grad_ref[...] = grad.astype(BF16)


def expert_merge(gate_pre, up_pre, gate_all, up_all):
    halves, tokens, units = gate_pre.shape
    width = gate_all.shape[1]
    span = 256
    batch = min(tokens, 1024)
    slab = pl.BlockSpec(
        (halves, batch, units), lambda turn, step: (0, turn, 0), pipeline_mode=pl.Buffered(1)
    )
    tile = pl.BlockSpec((halves, span, units), lambda turn, step: (0, step, 0))
    return pl.pallas_call(
        merge_kernel,
        grid=(tokens // batch, width // span),
        in_specs=[slab, slab, tile, tile],
        out_specs=pl.BlockSpec((batch, span), lambda turn, step: (turn, step)),
        out_shape=jax.ShapeDtypeStruct((tokens, width), BF16),
        compiler_params=pltpu.CompilerParams(vmem_limit_bytes=VMEM_LIMIT),
        cost_estimate=pl.CostEstimate(
            flops=4 * tokens * width * units * halves,
            bytes_accessed=4 * width * units * halves,
            transcendentals=0,
        ),
    )(gate_pre, up_pre, gate_all, up_all)


def output_kernel(hidden_ref, down_ref, out_ref):
    halves = hidden_ref.shape[0]
    out = dot(hidden_ref[0], down_ref[0], NN)
    for half in range(1, halves):
        out = out + dot(hidden_ref[half], down_ref[half], NN)
    out_ref[...] = out.astype(BF16)


def expert_output(hidden, down_all):
    halves, tokens, units = hidden.shape
    width = down_all.shape[2]
    span = 256
    batch = min(tokens, 1024)
    slab = pl.BlockSpec(
        (halves, batch, units), lambda turn, step: (0, turn, 0), pipeline_mode=pl.Buffered(1)
    )
    return pl.pallas_call(
        output_kernel,
        grid=(tokens // batch, width // span),
        in_specs=[slab, pl.BlockSpec((halves, units, span), lambda turn, step: (0, 0, step))],
        out_specs=pl.BlockSpec((batch, span), lambda turn, step: (turn, step)),
        out_shape=jax.ShapeDtypeStruct((tokens, width), BF16),
        compiler_params=pltpu.CompilerParams(vmem_limit_bytes=VMEM_LIMIT),
        cost_estimate=pl.CostEstimate(
            flops=2 * tokens * width * units * halves,
            bytes_accessed=2 * width * units * halves,
            transcendentals=0,
        ),
    )(hidden, down_all)


def weights_kernel(
    span,
    rows_ref,
    upstream_ref,
    hidden_ref,
    gate_pre_ref,
    up_pre_ref,
    gate_grad_ref,
    up_grad_ref,
    down_grad_ref,
):
    def body(step, carry):
        units = pl.ds(pl.multiple_of(step * span, span), span)
        gate_grad_ref[0, :, units] = dot(rows_ref[...], gate_pre_ref[0, :, units], TN).astype(BF16)
        up_grad_ref[0, :, units] = dot(rows_ref[...], up_pre_ref[0, :, units], TN).astype(BF16)
        down_grad_ref[0, units, :] = dot(
            hidden_ref[0, :, units], upstream_ref[...], TN
        ).astype(BF16)
        return carry

    lax.fori_loop(0, gate_grad_ref.shape[2] // span, body, 0)


def expert_weights(rows, upstream, hidden, gate_pre, up_pre):
    tokens, width = rows.shape
    halves, _, units = hidden.shape

    def each(*shape):
        return pl.BlockSpec((1,) + shape, lambda half: (half,) + (0,) * len(shape))

    whole = pl.BlockSpec(memory_space=pltpu.VMEM)
    slab = each(tokens, units)
    return pl.pallas_call(
        functools.partial(weights_kernel, 256),
        grid=(halves,),
        in_specs=[whole, whole, slab, slab, slab],
        out_specs=[each(width, units), each(width, units), each(units, width)],
        out_shape=[
            jax.ShapeDtypeStruct((halves, width, units), BF16),
            jax.ShapeDtypeStruct((halves, width, units), BF16),
            jax.ShapeDtypeStruct((halves, units, width), BF16),
        ],
        compiler_params=pltpu.CompilerParams(vmem_limit_bytes=VMEM_LIMIT),
        cost_estimate=pl.CostEstimate(
            flops=6 * tokens * width * units * halves,
            bytes_accessed=6 * width * units * halves,
            transcendentals=0,
        ),
    )(rows, upstream, hidden, gate_pre, up_pre)


def experts_in_turn(
    expert_input, upstream_all, choose, router_full, gate_all, up_all, down_all, layout, micros
):
    groups, deep, wide = layout
    shards = deep * wide
    experts = router_full.shape[1]
    shard_place = lax.axis_index("shard")
    ((expert_all,),) = fuse([Gather(expert_input, layout)], layout, 2, "experts_in")
    logits = jnp.dot(expert_all, router_full, preferred_element_type=F32)
    share = softmax_rows(jnp.sum(choose * logits[:, None, :], axis=-1))
    share_wide = jnp.sum(choose * share[:, :, None], axis=1)
    served = (jnp.arange(groups, dtype=jnp.int32) * shards + shard_place) // 2
    serves = (served[:, None] == jnp.arange(experts, dtype=jnp.int32)).astype(F32)
    share_own = jnp.pad(
        jnp.dot(share_wide, serves.T, precision=PRECISE), ((0, 0), (0, 128 - groups))
    )
    activated, gate_pre, up_pre, dots = expert_units(
        expert_all, upstream_all, share_own, gate_all, up_all, down_all
    )
    expert_grad_parts = expert_merge(gate_pre, up_pre, gate_all, up_all)
    gate_pre, expert_grad_parts = lax.optimization_barrier((gate_pre, expert_grad_parts))
    gate_terms, up_terms, down_terms = expert_weights(
        expert_all, upstream_all, activated, gate_pre, up_pre
    )
    out_parts = expert_output(activated, down_all)

    halves = groups * shards
    lanes = halves + -halves % 128
    columns = jnp.arange(groups, dtype=jnp.int32) * shards + shard_place
    columns = (columns[:, None] == jnp.arange(lanes, dtype=jnp.int32)).astype(F32)
    placed = jnp.dot(dots[:, :groups], columns, precision=PRECISE)
    placed_high = placed.astype(BF16)
    placed_low = (placed - placed_high.astype(F32)).astype(BF16)
    placed = jnp.concatenate([placed_high, placed_low], axis=1)
    (dot_total,), (expert_grad,) = fuse(
        [Scatter(placed, micros, layout), Scatter(expert_grad_parts, micros, layout)],
        layout,
        3,
        "experts_out",
    )
    return gate_terms, up_terms, down_terms, out_parts, share, expert_grad, dot_total, lanes


def per_device(
    groups,
    shards,
    wide,
    inputs,
    segment_ids,
    routes,
    cotangent,
    query_weight,
    key_weight,
    value_weight,
    output_weight,
    router_weight,
    attention_gain,
    expert_gain,
    query_gain,
    key_gain,
    gate_weight,
    up_weight,
    down_weight,
):
    micros, rows, width = inputs.shape
    deep = shards // wide
    span = shards * rows
    tokens = micros * span
    experts = router_weight.shape[1]
    column_width = width // shards
    shard_place = lax.axis_index("shard")
    layout = (groups, deep, shards // deep)

    gate_all = lax.all_gather(gate_weight, "expert", axis=0, tiled=True)
    up_all = lax.all_gather(up_weight, "expert", axis=0, tiled=True)
    down_all = lax.all_gather(down_weight, "expert", axis=0, tiled=True)

    cuts = [column_width * experts, routes.size]
    small_own = jnp.concatenate(
        [router_weight.reshape(-1), routes.reshape(-1).astype(BF16)]
    )
    small_own = jnp.pad(small_own, (0, -sum(cuts) % 2048)).reshape(-1, 128)

    def placed_row(gain):
        row = jnp.zeros((gain.shape[0] * shards,), BF16)
        return lax.dynamic_update_slice_in_dim(row, gain, shard_place * gain.shape[0], 0)

    gains_own = jnp.zeros((16, max(2 * column_width, 2 * HDIM)), BF16)
    gains_own = gains_own.at[0, : 2 * column_width].set(
        jnp.concatenate([attention_gain, expert_gain])
    )
    gains_own = gains_own.at[1, : 2 * HDIM].set(
        jnp.concatenate([placed_row(query_gain), placed_row(key_gain)])
    )

    tables = rotary(span)
    segments = (segment_ids[:, :, None], segment_ids[:, None, :])
    (
        (
            small,
            gains_all,
            projections,
            upstream_all,
            mixer_all,
            projected,
            attended,
            middle_total,
        ),
    ) = fuse(
        [
            AttentionForward(
                (query_weight, key_weight, value_weight),
                (small_own, gains_own),
                inputs,
                cotangent,
                output_weight,
                tables,
                segments,
                layout,
            )
        ],
        layout,
        0,
        "attention_forward",
    )
    projections = projections.reshape(width, 3 * column_width)
    small = small.reshape(shards, -1)
    router_full = small[:, : cuts[0]].reshape(width, experts)
    routes_all = small[:, cuts[0] : sum(cuts)].reshape(shards, micros, rows, -1)
    routes_all = routes_all.transpose(1, 0, 2, 3).reshape(tokens, -1).astype(jnp.int32)
    attn_gain = gains_all[:, 0, :column_width].reshape(-1).astype(F32)
    expert_gain_full = gains_all[:, 0, column_width : 2 * column_width].reshape(-1).astype(F32)
    head_gains = jnp.sum(gains_all[:, 1, : 2 * HDIM].astype(F32), axis=0).reshape(2, HDIM)
    head_gains = jnp.pad(head_gains, ((0, 6), (0, 0)))
    hidden = inputs.astype(F32)
    middle = hidden + middle_total

    scale_second = rms_scale(middle)
    normed_second = middle * scale_second
    expert_input = (normed_second * expert_gain_full).astype(BF16)
    early = tokens <= 1024 and 4 * groups * shards <= 256
    choose = (routes_all[:, :, None] == jnp.arange(experts, dtype=jnp.int32)).astype(F32)
    if early:
        mask = jnp.pad(jnp.sum(choose, axis=1), ((0, 0), (0, 128 - experts)))
        router_wide = jnp.pad(router_full, ((0, 0), (0, 128 - experts)))
        (
            (
                gate_terms,
                up_terms,
                down_terms,
                out_parts,
                share_wide,
                expert_grad,
                dot_total,
            ),
        ) = fuse(
            [
                Experts(
                    expert_input,
                    upstream_all,
                    mask,
                    router_wide,
                    gate_all,
                    up_all,
                    down_all,
                    layout,
                )
            ],
            layout,
            2,
            "experts",
        )
        share = jnp.sum(choose * share_wide[:, None, :experts], axis=-1)
        half_lanes = 64
    else:
        (
            gate_terms,
            up_terms,
            down_terms,
            out_parts,
            share,
            expert_grad,
            dot_total,
            half_lanes,
        ) = experts_in_turn(
            expert_input,
            upstream_all,
            choose,
            router_full,
            gate_all,
            up_all,
            down_all,
            layout,
            micros,
        )

    def own_rows(values):
        return lax.dynamic_slice_in_dim(
            values.reshape((micros, span) + values.shape[1:]), shard_place * rows, rows, 1
        )

    own_choose, own_share = own_rows(choose), own_rows(share)
    halves = groups * shards
    share_grad_wide = (
        dot_total[..., :halves] + dot_total[..., half_lanes : half_lanes + halves]
    )
    share_grad_wide = share_grad_wide.reshape(micros, rows, experts, 2).sum(axis=-1)
    share_grad = jnp.sum(own_choose * share_grad_wide[:, :, None, :], axis=-1)
    chosen_grad = own_share * (
        share_grad - jnp.sum(own_share * share_grad, axis=-1, keepdims=True)
    )
    own_logits_grad = jnp.sum(own_choose * chosen_grad[..., None], axis=2)
    logits_high = lax.reduce_precision(own_logits_grad, 8, 7)
    logits_pair = jnp.concatenate([logits_high, own_logits_grad - logits_high], axis=-1)
    logits_pair = logits_pair.astype(BF16)
    expert_grad = expert_grad + jnp.einsum(
        "mte,de->mtd",
        logits_pair,
        jnp.concatenate([router_full, router_full], axis=1),
        preferred_element_type=F32,
    )
    expert_gain_term = jnp.sum(expert_grad * normed_second, axis=(0, 1))
    middle_grad = cotangent.astype(F32) + norm_back(
        expert_grad * expert_gain_full, normed_second, scale_second
    )
    router_term = jnp.einsum(
        "mtd,mte->de", expert_input, logits_pair, preferred_element_type=F32
    )
    router_term = router_term[:, :experts] + router_term[:, experts:]

    beside = []
    if early:
        beside = [ExpertScatter(gate_terms, layout), ExpertScatter(up_terms, layout)]
    ((projection_terms, output_term, head_gain_terms, mixer_grad, *side_grads),) = fuse(
        [
            AttentionBackward(
                middle_grad.astype(BF16),
                mixer_all,
                projected,
                attended,
                projections,
                output_weight,
                head_gains,
                tables,
                segments,
                beside,
                layout,
            )
        ],
        layout,
        4,
        "attention_backward",
    )
    scale_first = rms_scale(hidden)
    normed_first = hidden * scale_first
    attn_gain_term = jnp.sum(mixer_grad * normed_first, axis=(0, 1))
    hidden_grad = middle_grad + norm_back(mixer_grad * attn_gain, normed_first, scale_first)

    part = column_width // groups
    tail = jnp.concatenate(
        [
            term.reshape(shards, -1)
            for term in (
                router_term,
                attn_gain_term,
                expert_gain_term,
                head_gain_terms[0],
                head_gain_terms[1],
            )
        ],
        axis=1,
    )
    tail = jnp.pad(tail, ((0, 0), (0, -tail.shape[1] % 1024))).reshape(shards, -1, 128)
    (output_grad, tail, query_grad, key_grad, value_grad), (outs,), *last_grads = fuse(
        [
            Rows(
                projection_terms.reshape(shards, groups, part, 3 * column_width),
                output_term.reshape(groups, part, width),
                tail,
                layout,
            ),
            Scatter(out_parts, micros, layout),
            *([ExpertScatter(down_terms, layout)] if early else []),
        ],
        layout,
        5,
        "exit",
    )
    if early:
        gate_grad, up_grad = side_grads
        ((down_grad,),) = last_grads
    else:
        gate_grad, up_grad, down_grad = (
            fuse([ExpertScatter(terms, layout)], layout, 6 + index, "weights")[0][0]
            for index, terms in enumerate((gate_terms, up_terms, down_terms))
        )
    result = middle + outs
    tail = tail.reshape(-1)
    lengths = [column_width * experts] + [column_width] * 2 + [HDIM // shards] * 2
    starts = [sum(lengths[:place]) for place in range(len(lengths))]
    tails = [
        tail[start : start + length] for start, length in zip(starts, lengths, strict=True)
    ]
    return (
        result.astype(BF16),
        hidden_grad.astype(BF16),
        query_grad.astype(F32).reshape(column_width, width),
        key_grad.astype(F32).reshape(column_width, width),
        value_grad.astype(F32).reshape(column_width, width),
        output_grad.astype(F32).reshape(column_width, width),
        tails[0].reshape(column_width, experts),
        tails[1],
        tails[2],
        tails[3],
        tails[4],
        gate_grad.astype(F32)[None],
        up_grad.astype(F32)[None],
        down_grad.astype(F32)[None],
    )


def solution(mesh):
    groups, shards = mesh.shape["expert"], mesh.shape["shard"]
    wide = shards // 4 if shards % 4 == 0 else 1
    in_specs = (
        P(None, ("expert", "shard"), None),
        P(None, "expert"),
        P(None, ("expert", "shard"), None),
        P(None, ("expert", "shard"), None),
        P("shard", None),
        P("shard", None),
        P("shard", None),
        P("shard", None),
        P("shard", None),
        P("shard"),
        P("shard"),
        P("shard"),
        P("shard"),
        P(("expert", "shard"), None, None),
        P(("expert", "shard"), None, None),
        P(("expert", "shard"), None, None),
    )
    out_specs = (
        P(None, ("expert", "shard"), None),
        P(None, ("expert", "shard"), None),
        P("shard", None),
        P("shard", None),
        P("shard", None),
        P("shard", None),
        P("shard", None),
        P("shard"),
        P("shard"),
        P("shard"),
        P("shard"),
        P(("expert", "shard"), None, None),
        P(("expert", "shard"), None, None),
        P(("expert", "shard"), None, None),
    )
    return jax.shard_map(
        functools.partial(per_device, groups, shards, wide),
        mesh=mesh,
        in_specs=in_specs,
        out_specs=out_specs,
        check_vma=False,
    )
```
